128 devices in a mesh: dp: 8 (over z, core), fsdp: 16 (over x, y).
Axes of the slice: x: 4, y: 4, z: 4, core: 2. Of those that a mesh axis runs over, the one named last changes fastest.
Arguments:
- tokens: bfloat16 [65536, 768], P(('dp', 'fsdp')), may hold values from -24 to 24
- lengths: int32 [8, 2], P('dp'), may hold values from 1024 to 7168, as said below
- routed: int32 [8, 1024], P('dp'), may hold values from 0 to 8191, as said below
- cotangent: bfloat16 [65536, 768], P(('dp', 'fsdp')), may hold values from -6 to 6
- gain_attn: float32 [768], P(('dp', 'fsdp')), may hold values from 0.5 to 1.5
- gain_ffn: float32 [768], P(('dp', 'fsdp')), may hold values from 0.5 to 1.5
- router_attn: float32 [768], P(('dp', 'fsdp')), may hold values from -0.15625 to 0.15625
- router_ffn: float32 [768], P(('dp', 'fsdp')), may hold values from -0.15625 to 0.15625
- light_q: float32 [768, 768], P(('dp', 'fsdp')), may hold values from -0.21875 to 0.21875
- light_k: float32 [768, 768], P(('dp', 'fsdp')), may hold values from -0.21875 to 0.21875
- light_v: float32 [768, 768], P(('dp', 'fsdp')), may hold values from -0.21875 to 0.21875
- light_o: float32 [768, 768], P(('dp', 'fsdp')), may hold values from -1.75 to 1.75
- light_gate: float32 [768, 1024], P(('dp', 'fsdp')), may hold values from -0.21875 to 0.21875
- light_up: float32 [768, 1024], P(('dp', 'fsdp')), may hold values from -0.21875 to 0.21875
- light_down: float32 [1024, 768], P(('dp', 'fsdp')), may hold values from -0.1875 to 0.1875
- heavy_q: float32 [768, 768], P(('dp', 'fsdp')), may hold values from -0.21875 to 0.21875
- heavy_k: float32 [768, 768], P(('dp', 'fsdp')), may hold values from -0.21875 to 0.21875
- heavy_v: float32 [768, 768], P(('dp', 'fsdp')), may hold values from -0.21875 to 0.21875
- heavy_o: float32 [768, 768], P(('dp', 'fsdp')), may hold values from -2.5 to 2.5
- heavy_gate: float32 [768, 4096], P(('dp', 'fsdp')), may hold values from -0.21875 to 0.21875
- heavy_up: float32 [768, 4096], P(('dp', 'fsdp')), may hold values from -0.21875 to 0.21875
- heavy_down: float32 [4096, 768], P(('dp', 'fsdp')), may hold values from -0.1875 to 0.1875
Outputs:
- output: bfloat16 [65536, 768], P(('dp', 'fsdp'))
- grad_tokens: bfloat16 [65536, 768], P(('dp', 'fsdp'))
- grad_gain_attn: float32 [768], P(('dp', 'fsdp'))
- grad_gain_ffn: float32 [768], P(('dp', 'fsdp'))
- grad_router_attn: float32 [768], P(('dp', 'fsdp'))
- grad_router_ffn: float32 [768], P(('dp', 'fsdp'))
- grad_light_q: float32 [768, 768], P(('dp', 'fsdp'))
- grad_light_k: float32 [768, 768], P(('dp', 'fsdp'))
- grad_light_v: float32 [768, 768], P(('dp', 'fsdp'))
- grad_light_o: float32 [768, 768], P(('dp', 'fsdp'))
- grad_light_gate: float32 [768, 1024], P(('dp', 'fsdp'))
- grad_light_up: float32 [768, 1024], P(('dp', 'fsdp'))
- grad_light_down: float32 [1024, 768], P(('dp', 'fsdp'))
- grad_heavy_q: float32 [768, 768], P(('dp', 'fsdp'))
- grad_heavy_k: float32 [768, 768], P(('dp', 'fsdp'))
- grad_heavy_v: float32 [768, 768], P(('dp', 'fsdp'))
- grad_heavy_o: float32 [768, 768], P(('dp', 'fsdp'))
- grad_heavy_gate: float32 [768, 4096], P(('dp', 'fsdp'))
- grad_heavy_up: float32 [768, 4096], P(('dp', 'fsdp'))
- grad_heavy_down: float32 [4096, 768], P(('dp', 'fsdp'))
The draws below stay inside these ranges and needn't reach their ends.
Inputs may be any that keep to these rules, and one draw needn't show every extreme that they name: Each row holds 2 lengths, each a multiple of 8, that add up to 8192. `routed`: each row lists, in increasing order, positions within its pack: from every sequence exactly its length / 8 distinct positions, among them the sequence's first and last position.
All inputs are finite; a program needn't handle non-finite values.
Results may differ from the reference program's by a relative error of at most 0.013.
The reference program's roundings to bfloat16 on the way count: a program that leaves them out, or rounds other values in their place, can miss the bound.
Values may be sent and summed in bfloat16 or wider, within the bound.
No kernel may reach another device: no remote copies, remote signals or barrier semaphores. Data moves between devices by JAX's collectives and lax.ppermute only.
A program may use at most 256 MiB of HBM per device.

```python
import jax
import jax.numpy as jnp
from jax import lax

D = 768
HL = 8
HH = 12
FL = 1024
FH = 4096
WIN = 128
NSEQ = 2
LMIN = 1024
TOK_DEV = 512
PACK = 8192
TOKENS = 65536
RP = 1024
CAP = 6
N_DP = 8
N_FSDP = 16


def one_pack(pack_key, pack_number):
    pack_len = TOK_DEV * N_FSDP
    spare = (pack_len - NSEQ * LMIN) // 8
    pick_key, region_key, score_key, extra_key = jax.random.split(pack_key, 4)
    long_pick = jax.random.randint(pick_key, (), 0, NSEQ)
    seq_order = jnp.arange(NSEQ, dtype=jnp.int32)
    is_long = seq_order == long_pick
    extras = jax.random.randint(extra_key, (NSEQ,), 0, spare // (2 * NSEQ) + 1).astype(jnp.int32)
    extras = jnp.where(is_long | (pack_number == 0), 0, extras)
    short_lengths = LMIN + 8 * extras
    long_length = pack_len - jnp.sum(jnp.where(is_long, 0, short_lengths))
    seq_lengths = jnp.where(is_long, long_length, short_lengths).astype(jnp.int32)
    seq_ends = jnp.cumsum(seq_lengths)
    seq_starts = seq_ends - seq_lengths
    places = jnp.arange(pack_len, dtype=jnp.int32)
    seg_ids = jnp.sum((places[:, None] >= seq_ends[None, :]).astype(jnp.int32), axis=1)
    offsets = places - seq_starts[seg_ids]
    seg_len = seq_lengths[seg_ids]
    region_start = jax.random.randint(region_key, (NSEQ,), 0, 1 << 20) % seq_lengths
    in_region = (offsets - region_start[seg_ids]) % seg_len < seg_len // 4
    scores = jax.random.randint(score_key, (pack_len,), 0, 2048) + 512 * in_region.astype(jnp.int32)
    at_ends = (offsets == 0) | (offsets == seg_len - 1)
    scores = jnp.where(at_ends, 4096, scores)
    combined = scores * pack_len + places
    sort_key = seg_ids * (1 << 29) + (1 << 28) - combined
    ordering = jnp.argsort(sort_key, stable=True)
    sorted_seg = seg_ids[ordering]
    rank_in = places - seq_starts[sorted_seg]
    picked = (rank_in < seq_lengths[sorted_seg] // 8).astype(jnp.int32)
    chosen = jnp.zeros((pack_len,), jnp.int32).at[ordering].set(picked)
    routed_list = jnp.nonzero(chosen, size=pack_len // 8)[0].astype(jnp.int32)
    return (seq_lengths, routed_list)


def route_plan(key):
    pack_keys = jax.random.split(key, N_DP)
    pack_numbers = jnp.arange(N_DP, dtype=jnp.int32)
    return jax.vmap(one_pack)(pack_keys, pack_numbers)


def draw_lengths(key, part):
    seq_lengths, routed_list = route_plan(key)
    return seq_lengths


def draw_routed(key, part):
    seq_lengths, routed_list = route_plan(key)
    return routed_list


def with_spikes(entries, own_key, source, target, blocks, factor):
    def block_of(dim):
        return (jnp.arange(entries.shape[dim]) // (entries.shape[dim] // blocks)).reshape((-1,) + (1,) * (entries.ndim - 1 - dim))

    one_side = jax.random.permutation(own_key, blocks)[block_of(target)]
    other_side = (block_of(target) + blocks // 2) % blocks
    return jnp.where((block_of(source) == one_side) | (block_of(source) == other_side), factor * entries, entries)


def block_scale(key, extent, shards, least, high):
    level = 1.0
    for dim, parts in shards:
        steps = jax.random.uniform(jax.random.fold_in(jax.random.fold_in(key, 6), dim), (parts,), jnp.float32, least / len(shards), high / len(shards))
        level = level * jnp.repeat(jnp.exp(steps), extent[dim] // parts).reshape((-1,) + (1,) * (len(extent) - 1 - dim))
    return level


def scatter_about(rng, dims, deviation, most, shards=(), held_as=jnp.bfloat16):
    values = deviation * jax.random.normal(rng, dims, jnp.float32)
    if shards:
        values = values * block_scale(rng, dims, shards, -0.22, 0.18)
    return jnp.clip(values, -most, most).astype(held_as)


def bell_draw_with(own_key, dims, scale, limit, cuts, heavy, held_as=jnp.bfloat16):
    entries = scale * jax.random.normal(own_key, dims, jnp.float32)
    if cuts:
        entries = entries * block_scale(own_key, dims, cuts, -0.22, 0.18)
    return jnp.clip(with_spikes(entries, jax.random.fold_in(own_key, 3), *heavy), -limit, limit).astype(held_as)


def setup_inputs(seed: int = 0) -> dict:
    arg_keys = jax.random.split(jax.random.key(seed), 23)
    return {
        "tokens": bell_draw_with(arg_keys[0], (TOKENS, D), 1.0, 24.0, ((0, 128),), (0, 1, 128, 5.5)),
        "lengths": draw_lengths(jax.random.fold_in(arg_keys[22], 71), 0),
        "routed": draw_routed(jax.random.fold_in(arg_keys[22], 71), 0),
        "cotangent": scatter_about(arg_keys[3], (TOKENS, D), 1.0, 6.0, ((0, 128),)),
        "gain_attn": jnp.clip(1.0 + 0.1 * jax.random.normal(arg_keys[4], (D,), jnp.float32), 0.5, 1.5),
        "gain_ffn": jnp.clip(1.0 + 0.1 * jax.random.normal(arg_keys[5], (D,), jnp.float32), 0.5, 1.5),
        "router_attn": scatter_about(arg_keys[6], (D,), (2 * D) ** -0.5, 0.15625, ((0, 128),), jnp.float32),
        "router_ffn": scatter_about(arg_keys[7], (D,), (2 * D) ** -0.5, 0.15625, ((0, 128),), jnp.float32),
        "light_q": scatter_about(arg_keys[8], (D, D), D ** -0.5, 0.21875, ((0, 128),), jnp.float32),
        "light_k": scatter_about(arg_keys[9], (D, D), D ** -0.5, 0.21875, ((0, 128),), jnp.float32),
        "light_v": scatter_about(arg_keys[10], (D, D), D ** -0.5, 0.21875, ((0, 128),), jnp.float32),
        "light_o": scatter_about(arg_keys[11], (D, D), (D // 64) ** -0.5, 1.75, ((0, 128),), jnp.float32),
        "light_gate": scatter_about(arg_keys[12], (D, FL), D ** -0.5, 0.21875, ((0, 128),), jnp.float32),
        "light_up": scatter_about(arg_keys[13], (D, FL), D ** -0.5, 0.21875, ((0, 128),), jnp.float32),
        "light_down": scatter_about(arg_keys[14], (FL, D), FL ** -0.5, 0.1875, ((0, 128),), jnp.float32),
        "heavy_q": scatter_about(arg_keys[15], (D, D), D ** -0.5, 0.21875, ((0, 128),), jnp.float32),
        "heavy_k": scatter_about(arg_keys[16], (D, D), D ** -0.5, 0.21875, ((0, 128),), jnp.float32),
        "heavy_v": scatter_about(arg_keys[17], (D, D), D ** -0.5, 0.21875, ((0, 128),), jnp.float32),
        "heavy_o": scatter_about(arg_keys[18], (D, D), (D // 128) ** -0.5, 2.5, ((0, 128),), jnp.float32),
        "heavy_gate": scatter_about(arg_keys[19], (D, FH), D ** -0.5, 0.21875, ((0, 128),), jnp.float32),
        "heavy_up": scatter_about(arg_keys[20], (D, FH), D ** -0.5, 0.21875, ((0, 128),), jnp.float32),
        "heavy_down": scatter_about(arg_keys[21], (FH, D), (FH // 4) ** -0.5, 0.1875, ((0, 128),), jnp.float32),
    }


@jax.custom_vjp
def low(v):
    return lax.optimization_barrier(v.astype(jnp.bfloat16)).astype(jnp.float32)

@jax.custom_vjp
def low_back(v):
    return v

def low_keep(v):
    return (low(v), None)

def low_pass(kept, grad):
    return (grad,)

def back_keep(v):
    return (v, None)

def back_low(kept, grad):
    return (low(grad),)
low.defvjp(low_keep, low_pass)
low_back.defvjp(back_keep, back_low)
epsilon = 1e-06
negative = -1e+30
highest = lax.Precision.HIGHEST

def product(left_op, right_op):
    return jnp.dot(left_op, right_op, precision=highest, preferred_element_type=jnp.float32)

def rounded(value):
    return low_back(low(value))

def normalize(row_data, gain):
    scaling = lax.rsqrt(lax.optimization_barrier(jnp.mean(row_data * row_data, axis=-1, keepdims=True)) + epsilon)
    return row_data * scaling * gain

def gelu_mix(gate_pre, up_part):
    return jax.nn.gelu(gate_pre, approximate=True) * up_part

def softmax_attend(q_part, k_part, v_part, allowed, head_count):
    row_count = q_part.shape[0]
    head_size = q_part.shape[1] // head_count
    q_heads = q_part.reshape(row_count, head_count, head_size)
    k_heads = k_part.reshape(k_part.shape[0], head_count, head_size)
    v_heads = v_part.reshape(v_part.shape[0], head_count, head_size)
    scores = jnp.einsum('qhd,khd->hqk', q_heads, k_heads, precision=highest) * head_size ** (-0.5)
    scores = low_back(scores)
    scores = jnp.where(allowed[None], scores, negative)
    probs_b = rounded(jax.nn.softmax(scores, axis=-1))
    mixed = jnp.einsum('hqk,khd->qhd', probs_b, v_heads, precision=highest)
    return mixed.reshape(row_count, head_count * head_size)

def light_attention(a_in, seg_pack, q_w, k_w, v_w, o_w):
    queries = rounded(product(a_in, q_w))
    keys_all = rounded(product(a_in, k_w))
    values = rounded(product(a_in, v_w))
    half_win = WIN // 2
    slab_len = 512 + 2 * half_win
    pad_keys = jnp.pad(keys_all, ((half_win, half_win), (0, 0)))
    pad_values = jnp.pad(values, ((half_win, half_win), (0, 0)))
    pad_seg = jnp.pad(seg_pack, (half_win, half_win), constant_values=-1)
    offsets = jnp.arange(512, dtype=jnp.int32)[:, None] - jnp.arange(slab_len, dtype=jnp.int32)[None, :] + half_win
    in_window = jnp.abs(offsets) <= half_win

    def one_block(block_start):
        q_part = lax.dynamic_slice_in_dim(queries, block_start, 512, 0)
        k_part = lax.dynamic_slice_in_dim(pad_keys, block_start, slab_len, 0)
        v_part = lax.dynamic_slice_in_dim(pad_values, block_start, slab_len, 0)
        seg_q = lax.dynamic_slice_in_dim(seg_pack, block_start, 512, 0)
        seg_k = lax.dynamic_slice_in_dim(pad_seg, block_start, slab_len, 0)
        allowed = in_window & (seg_q[:, None] == seg_k[None, :])
        return softmax_attend(q_part, k_part, v_part, allowed, HL)
    starts = (jnp.arange(PACK // 512) * 512).astype(jnp.int32)
    attended = lax.map(jax.checkpoint(one_block), starts).reshape(PACK, D)
    return product(rounded(attended), o_w)

def light_ffn(f_in, gate_w, up_w, down_w):
    gate_pre = low_back(product(f_in, gate_w))
    up_part = low_back(product(f_in, up_w))
    hidden = low(gelu_mix(gate_pre, up_part))
    return product(hidden, down_w)

def heavy_branch(x_rows, kept, seg_rows, gain_a, gain_f, router_a, router_f, q_w, k_w, v_w, o_w, gate_w, up_w, down_w):
    a_r = low(normalize(x_rows, gain_a))
    f_r = low(normalize(x_rows, gain_f))
    score_a = jax.nn.sigmoid(jnp.dot(a_r, router_a, precision=highest, preferred_element_type=jnp.float32))
    score_f = jax.nn.sigmoid(jnp.dot(f_r, router_f, precision=highest, preferred_element_type=jnp.float32))
    queries = rounded(product(a_r, q_w))
    keys_all = rounded(product(a_r, k_w))
    values = rounded(product(a_r, v_w))
    block_rows = min(512, RP)
    key_ok = kept > 0.5

    def one_block(block_start):
        q_part = lax.dynamic_slice_in_dim(queries, block_start, block_rows, 0)
        seg_part = lax.dynamic_slice_in_dim(seg_rows, block_start, block_rows, 0)
        allowed = (seg_part[:, None] == seg_rows[None, :]) & key_ok[None, :]
        return softmax_attend(q_part, keys_all, values, allowed, HH)
    starts = (jnp.arange(RP // block_rows) * block_rows).astype(jnp.int32)
    attended = lax.map(jax.checkpoint(one_block), starts).reshape(RP, D)
    heavy_attn = low_back(product(rounded(attended), o_w))
    gate_pre = low_back(product(f_r, gate_w))
    up_part = low_back(product(f_r, up_w))
    hidden = low(gelu_mix(gate_pre, up_part))
    heavy_out = low_back(product(hidden, down_w))
    mixed_rows = (score_a[:, None] * heavy_attn + score_f[:, None] * heavy_out) * kept[:, None]
    return low(mixed_rows)

def pack_forward(x_pack, seg_pack, routed_pack, kept_pack, weights):
    gain_a, gain_f, router_a, router_f, light_qw, light_kw, light_vw, light_ow, light_gw, light_uw, light_dw, heavy_qw, heavy_kw, heavy_vw, heavy_ow, heavy_gw, heavy_uw, heavy_dw = weights
    a_in = low(normalize(x_pack, gain_a))
    f_in = low(normalize(x_pack, gain_f))
    light_part = light_attention(a_in, seg_pack, light_qw, light_kw, light_vw, light_ow)
    light_part = light_part + light_ffn(f_in, light_gw, light_uw, light_dw)
    x_rows = low_back(x_pack[routed_pack] * kept_pack[:, None])
    seg_rows = seg_pack[routed_pack]
    heavy_rows = heavy_branch(x_rows, kept_pack, seg_rows, gain_a, gain_f, router_a, router_f, heavy_qw, heavy_kw, heavy_vw, heavy_ow, heavy_gw, heavy_uw, heavy_dw)
    spread = jnp.zeros_like(x_pack).at[routed_pack].add(heavy_rows)
    return x_pack + light_part + spread

def segments(seq_lengths):
    seq_ends = jnp.cumsum(seq_lengths)
    places = jnp.arange(PACK, dtype=jnp.int32)
    return lax.optimization_barrier(jnp.sum((places[:, None] >= seq_ends[None, :]).astype(jnp.int32), axis=1))

def routing_kept(routed_pack):
    entry_order = jnp.arange(RP, dtype=jnp.int32)
    source = routed_pack // TOK_DEV
    owners = jnp.arange(N_FSDP, dtype=jnp.int32)
    bounds = lax.optimization_barrier(jnp.sum((routed_pack[None, :] < (owners * TOK_DEV)[:, None]).astype(jnp.int32), axis=1))
    before = bounds[source]
    target = entry_order % N_FSDP
    slot_id = (entry_order - before - (target - before) % N_FSDP) // N_FSDP
    return (slot_id < CAP).astype(jnp.float32)

def reference(tokens, lengths, routed, cotangent, gain_attn, gain_ffn, router_attn, router_ffn, light_q, light_k, light_v, light_o, light_gate, light_up, light_down, heavy_q, heavy_k, heavy_v, heavy_o, heavy_gate, heavy_up, heavy_down):
    masters = (gain_attn, gain_ffn, router_attn, router_ffn, light_q, light_k, light_v, light_o, light_gate, light_up, light_down, heavy_q, heavy_k, heavy_v, heavy_o, heavy_gate, heavy_up, heavy_down)
    seg_all = jax.vmap(segments)(lengths)
    kept_all = jax.vmap(routing_kept)(routed)
    x_all = tokens.astype(jnp.float32).reshape(N_DP, PACK, D)

    def forward(x_whole, params):
        weights = tuple((low(master) for master in params))

        def step(carried, packed):
            x_pack, seg_pack, routed_pack, kept_pack = packed
            return (carried, pack_forward(x_pack, seg_pack, routed_pack, kept_pack, weights))
        start_carry = jnp.zeros((), jnp.float32)
        _, results = lax.scan(jax.checkpoint(step), start_carry, (x_whole, seg_all, routed, kept_all))
        return results
    result, pullback = jax.vjp(forward, x_all, masters)
    d_x, d_params = pullback(cotangent.astype(jnp.float32).reshape(N_DP, PACK, D))
    output = result.reshape(TOKENS, D).astype(jnp.bfloat16)
    grad_tokens = d_x.reshape(TOKENS, D).astype(jnp.bfloat16)
    return (output, grad_tokens, d_params[0], d_params[1], d_params[2], d_params[3], d_params[4], d_params[5], d_params[6], d_params[7], d_params[8], d_params[9], d_params[10], d_params[11], d_params[12], d_params[13], d_params[14], d_params[15], d_params[16], d_params[17])
```

```python
import jax
import jax.numpy as jnp
from jax import lax
from jax.experimental import pallas as pl
from jax.experimental.pallas import tpu as pltpu
from jax.sharding import PartitionSpec as P

BF = jnp.bfloat16
F32 = jnp.float32
EPS = 1e-6
NEG = -1e30
ALL = ("dp", "fsdp")
CAP = 96
LIGHT_SCALE = 96**-0.5
HEAVY_SCALE = 64**-0.5
PARAMS = pltpu.CompilerParams(vmem_limit_bytes=60 * 1024 * 1024)
SMEM = pl.BlockSpec(memory_space=pltpu.SMEM)
VMEM = pl.BlockSpec(memory_space=pltpu.VMEM)
HBM = pl.BlockSpec(memory_space=pl.ANY)

C_VEC, C_O, C_DOWN, C_HO, C_ALL = 5120, 5376, 6144, 6912, 7680


def dot(a, b):
    return jnp.dot(a, b, preferred_element_type=F32)


def dot_nt(a, b):
    return lax.dot_general(a, b, (((1,), (1,)), ((), ())), preferred_element_type=F32)


def dot_tn(a, b):
    return lax.dot_general(a, b, (((0,), (0,)), ((), ())), preferred_element_type=F32)


def pick6(rows, cols, shift=0):
    r = lax.broadcasted_iota(jnp.int32, (rows, cols), 0) + shift
    c = lax.broadcasted_iota(jnp.int32, (rows, cols), 1)
    low = c & 7
    return ((6 * (c >> 3) + low == r) & (low < 6)).astype(F32).astype(BF)


def unpad_rows(ref, out_ref, pick):
    for b in range(8):
        block = dot(pick, ref[128 * b : 128 * b + 128, :])
        out_ref[96 * b : 96 * b + 96, :] = block.astype(BF)


def vector_rows(vec_ref, pick):
    blocks = [dot(pick, vec_ref[128 * b : 128 * b + 128, :]) for b in range(8)]
    return jnp.concatenate(blocks, axis=0).T


def fetch(wall, sems, pieces):
    copies = []
    for n, (at, ref) in enumerate(pieces):
        copy = pltpu.make_async_copy(wall.at[:, at : at + ref.shape[1]], ref, sems.at[n])
        copy.start()
        copies.append(copy)
    return copies


def unit(rows):
    scale = lax.rsqrt(jnp.mean(rows * rows, axis=-1, keepdims=True) + EPS)
    return rows * scale, scale


def gelu_parts(gate):
    c0, c1 = 0.7978845608, 0.044715
    sq = gate * gate
    t = jnp.tanh(gate * (c0 + (c0 * c1) * sq))
    half = 0.5 * (1.0 + t)
    slope = half + (0.5 * gate) * (1.0 - t * t) * (c0 + (3.0 * c0 * c1) * sq)
    return gate * half, slope


def prep_kernel(
    q, k, v, o, gate, up, down, hq, hk, hv, ho, hgate, hup, hdown, vec, pack, hsend, hd, scr
):
    scr[...] = jnp.zeros_like(scr)
    zero128 = jnp.zeros((8, 128), BF)

    def padded(ref):
        cols = ref.shape[1]
        scr[0:6, 0:cols] = ref[...]
        return scr[:, 0:cols].astype(BF)

    gp, upp = padded(gate), padded(up)
    for c in range(4):
        pack[:, 512 * c : 512 * c + 256] = gp[:, 256 * c : 256 * c + 256]
        pack[:, 512 * c + 256 : 512 * c + 512] = upp[:, 256 * c : 256 * c + 256]
    spread = pick6(384, 512)
    for n, ref in enumerate((q, k, v)):
        w = padded(ref)
        for half in range(2):
            wide = dot(w[:, 384 * half : 384 * half + 384], spread)
            at = 2048 + 1024 * n + 512 * half
            pack[:, at : at + 512] = wide.astype(BF)
    pack[:, C_VEC : C_VEC + 128] = vec[...].astype(BF)
    pack[:, C_VEC + 128 : C_O] = zero128
    pack[:, C_O : C_O + 768] = padded(o)
    pack[:, C_DOWN : C_DOWN + 768] = down[...].astype(BF)
    pack[:, C_HO : C_HO + 768] = padded(ho)
    wq, wk, wv = padded(hq), padded(hk), padded(hv)
    wg, wu = padded(hgate), padded(hup)
    for j in range(16):
        hsend[j, :, 0:256] = wg[:, 256 * j : 256 * j + 256]
        hsend[j, :, 256:512] = wu[:, 256 * j : 256 * j + 256]
        for n, w in enumerate((wq, wk, wv)):
            p = j // 2
            part = w[:, 128 * p : 128 * p + 128] if j < 12 else zero128
            hsend[j, :, 512 + 128 * n : 640 + 128 * n] = part
    hd[...] = hdown[...].astype(BF)


def light_ffn_kernel(x, g, wall, ffn, cf, grad, gvec, gu, fin, gu_pad, down, vec, sems):
    copies = fetch(wall, sems, [(C_VEC, vec), (0, gu_pad), (C_DOWN, down)])
    pick = pick6(96, 128)
    for copy in copies:
        copy.wait()
    unpad_rows(gu_pad, gu, pick)
    gain_f = vector_rows(vec, pick)[1:2, :]
    u, _ = unit(x[...].astype(F32))
    fin[...] = (u * gain_f).astype(BF)
    for c in range(4):
        w = gu[:, 512 * c : 512 * c + 512]
        wd = down[256 * c : 256 * c + 256, :]
        both = dot(fin[...], w)
        act, slope = gelu_parts(both[:, 0:256])
        up = both[:, 256:512]
        hidden = (act * up).astype(BF)
        dh = dot_nt(g[...], wd)
        dgu = jnp.concatenate([(dh * up * slope).astype(BF), (dh * act).astype(BF)], axis=1)
        term = dot(hidden, wd)
        dterm = dot_nt(dgu, w)
        if c == 0:
            ffn[...] = term
            cf[...] = dterm
        else:
            ffn[...] += term
            cf[...] += dterm
        grad[:, 512 * c : 512 * c + 512] = dot_tn(fin[...], dgu).astype(BF)
        gd = dot_tn(hidden, g[...]).astype(BF)
        for n in range(2):
            b, r0 = 2 * c + n, 128 * n
            grad[96 * b : 96 * b + 96, 2048:2816] = gd[r0 : r0 + 96, :]
            for t in range(3):
                grad[96 * b + 32 * t : 96 * b + 32 * t + 32, 2816:3072] = gd[
                    r0 + 96 : r0 + 128, 256 * t : 256 * t + 256
                ]
    u, _ = unit(x[...].astype(F32))
    d_f = cf[...]
    gvec[...] = jnp.zeros_like(gvec)
    gvec[1:2, :] = jnp.sum(d_f * u, axis=0, keepdims=True)
    cf[...] = d_f * gain_f


def light_attn_kernel(
    meta, xl, x, xr, g, wall, ffn, cf, gin,
    lo, dxg, halo, grad, gvec,
    w, xs, a, q, k, v, o, do, dq, dk, dv, mask, qp, kp, vp, wo, vec, sems,
):
    copies = fetch(
        wall, sems, [(C_VEC, vec), (2048, qp), (3072, kp), (4096, vp), (C_O, wo)]
    )
    pick = pick6(96, 128)
    for copy in copies:
        copy.wait()
    for n, ref in enumerate((qp, kp, vp)):
        unpad_rows(ref, w.at[:, 1024 * n : 1024 * n + 1024], pick)
    gain_a = vector_rows(vec, pick)[0:1, :]
    xs[0:64, :] = xl[...]
    xs[64:576, :] = x[...]
    xs[576:640, :] = xr[...]
    u, _ = unit(xs[...].astype(F32))
    a[...] = (u * gain_a).astype(BF)
    q[...] = dot(a[64:576, :], w[:, 0:1024]).astype(BF)
    k[...] = dot(a[...], w[:, 1024:2048]).astype(BF)
    v[...] = dot(a[...], w[:, 2048:3072]).astype(BF)
    do[...] = dot_nt(g[...], wo[...]).astype(BF)
    first, base, pack_len = meta[0], meta[1], meta[2]
    key = lax.broadcasted_iota(jnp.int32, (256, 128), 0)
    qry = lax.broadcasted_iota(jnp.int32, (256, 128), 1)
    gap = key - qry
    for b in range(4):
        qpos = base + 128 * b + qry
        kpos = base + 128 * b - 64 + key
        ok = (gap >= 0) & (gap <= 128) & ((qpos < first) == (kpos < first))
        ok = ok & (kpos >= 0) & (kpos < pack_len)
        mask[b] = jnp.where(ok, 0.0, NEG)
    dk[...] = jnp.zeros_like(dk)
    dv[...] = jnp.zeros_like(dv)

    @pl.loop(0, 8)
    def _(h):
        cols = pl.ds(pl.multiple_of(h * 128, 128), 128)
        for b in range(4):
            rq, rk = pl.ds(128 * b, 128), pl.ds(128 * b, 256)
            qb, kb, vb, dob = q[rq, cols], k[rk, cols], v[rk, cols], do[rq, cols]
            s = dot_nt(kb, qb) * LIGHT_SCALE + mask[b]
            e = jnp.exp(s - jnp.max(s, axis=0, keepdims=True))
            p = e * (1.0 / jnp.sum(e, axis=0, keepdims=True))
            pb = p.astype(BF)
            o[rq, cols] = dot_tn(pb, vb).astype(BF)
            dp = dot_nt(vb, dob).astype(BF).astype(F32)
            ds = (p * (dp - jnp.sum(p * dp, axis=0, keepdims=True))).astype(BF)
            dq[rq, cols] = (dot_tn(ds, kb) * LIGHT_SCALE).astype(BF)
            dk[rk, cols] += dot(ds, qb) * LIGHT_SCALE
            dv[rk, cols] += dot(pb, dob)

    k[...] = dk[...].astype(BF)
    v[...] = dv[...].astype(BF)
    lo[...] = x[...].astype(F32) + ffn[...] + dot(o[...], wo[...])
    d_a = dot_nt(k[...], w[:, 1024:2048]) + dot_nt(v[...], w[:, 2048:3072])
    d_own = d_a[64:576, :] + dot_nt(dq[...], w[:, 0:1024])
    u, scale = unit(xs[...].astype(F32))
    gvec[...] = gin[...]
    gvec[0:1, :] = (
        jnp.sum(d_own * u[64:576, :], axis=0, keepdims=True)
        + jnp.sum(d_a[0:64, :] * u[0:64, :], axis=0, keepdims=True)
        + jnp.sum(d_a[576:640, :] * u[576:640, :], axis=0, keepdims=True)
    )

    def norm_back(c, rows):
        ur = u[rows]
        return scale[rows] * (c - ur * jnp.mean(ur * c, axis=-1, keepdims=True))

    own = slice(64, 576)
    dxg[...] = norm_back(d_own * gain_a + cf[...], own) + g[...].astype(F32)
    halo[0:64, :] = norm_back(d_a[0:64, :] * gain_a, slice(0, 64)).astype(BF)
    halo[64:128, :] = norm_back(d_a[576:640, :] * gain_a, slice(576, 640)).astype(BF)

    narrow = pick6(384, 512)
    for half in range(2):
        wide = slice(512 * half, 512 * half + 512)
        at = 384 * half
        grad[:, at : at + 384] = dot_tn(a[64:576, :], dot_nt(dq[:, wide], narrow).astype(BF)).astype(BF)
        grad[:, 768 + at : 768 + at + 384] = dot_tn(
            a[...], dot_nt(k[:, wide], narrow).astype(BF)
        ).astype(BF)
        grad[:, 1536 + at : 1536 + at + 384] = dot_tn(
            a[...], dot_nt(v[:, wide], narrow).astype(BF)
        ).astype(BF)
        grad[at : at + 384, 2304:3072] = dot_tn(
            dot_nt(o[:, wide], narrow).astype(BF), g[...]
        ).astype(BF)


def heavy_kernel(
    meta, xs, gs, hw, wall, gin,
    parts, grad,
    x, gy, w, wd, wo, ar, fr, q, k, v, o, do, dq, dk, dv, kmask, da, dgu, hid, y, sa, sf, la,
    wo_pad, vec, sems,
):
    copies = fetch(wall, sems, [(C_VEC, vec), (C_HO, wo_pad)])
    pick = pick6(96, 128)
    for copy in copies:
        copy.wait()
    for b in range(8):
        w[96 * b : 96 * b + 96, :] = dot(pick, hw[b, 0:128, :]).astype(BF)
        wd[32 * b : 32 * b + 32, :] = hw[b, 128:160, 0:768]
    vrows = vector_rows(vec, pick)
    gain_a, gain_f, r_a, r_f = (vrows[n : n + 1, :] for n in range(4))
    head_row = lax.broadcasted_iota(jnp.int32, (128, 1024), 0) >> 6
    low = meta[18]
    mine = pick6(128, 1024, low)
    wo_all = dot(jnp.where((head_row == meta[19]), mine.astype(F32), 0.0).astype(BF), wo_pad[...])
    wo[...] = wo_all.astype(BF)

    x[...] = jnp.zeros_like(x)
    gy[...] = jnp.zeros_like(gy)
    near = lax.broadcasted_iota(jnp.int32, (CAP + 8, 768), 0)
    for d in range(16):
        shift = meta[d] & 7
        rows = pl.ds(pl.multiple_of(meta[d] - shift, 8), CAP + 8)
        for ref, block in ((x, xs), (gy, gs)):
            wide = jnp.concatenate([block[d].astype(F32), jnp.zeros((8, 768), F32)], axis=0)
            ref[rows, :] = jnp.where(near >= shift, pltpu.roll(wide, shift, 0), ref[rows, :])
    kidx = lax.broadcasted_iota(jnp.int32, (1024, 128), 0)
    km = jnp.zeros((1024, 128), F32)
    for d in range(16):
        km = jnp.where((kidx >= meta[d] + CAP) & (kidx < meta[d + 1]), NEG, km)
    kmask[...] = km

    lane_head = lax.broadcasted_iota(jnp.int32, (256, 128), 1) >> 6
    on = lane_head == meta[19]
    for b in range(4):
        rows = slice(256 * b, 256 * b + 256)
        u, _ = unit(x[rows, :])
        arb, frb = (u * gain_a).astype(BF), (u * gain_f).astype(BF)
        ar[rows, :], fr[rows, :] = arb, frb
        sab = jax.nn.sigmoid(jnp.sum(arb.astype(F32) * r_a, axis=-1, keepdims=True))
        sfb = jax.nn.sigmoid(jnp.sum(frb.astype(F32) * r_f, axis=-1, keepdims=True))
        sa[rows, :], sf[rows, :] = sab, sfb
        qkv = dot(arb, w[:, 512:896])
        q[rows, :] = jnp.where(on, qkv[:, 0:128], 0.0).astype(BF)
        k[rows, :] = qkv[:, 128:256].astype(BF)
        v[rows, :] = jnp.where(on, qkv[:, 256:384], 0.0).astype(BF)
        dab = (sab * gy[rows, :]).astype(BF)
        da[rows, :] = dab
        do[rows, :] = dot_nt(dab, wo[...]).astype(BF)
    n0 = meta[17]
    dk[...] = jnp.zeros_like(dk)
    dv[...] = jnp.zeros_like(dv)
    for b in range(8):
        rows = slice(128 * b, 128 * b + 128)
        qidx = lax.broadcasted_iota(jnp.int32, (1024, 128), 1) + 128 * b
        same = (kidx < n0) == (qidx < n0)
        qb, dob = q[rows, :], do[rows, :]
        s = jnp.where(same, dot_nt(k[...], qb) * HEAVY_SCALE + kmask[...], NEG)
        e = jnp.exp(s - jnp.max(s, axis=0, keepdims=True))
        p = e * (1.0 / jnp.sum(e, axis=0, keepdims=True))
        pb = p.astype(BF)
        ob = dot_tn(pb, v[...]).astype(BF)
        o[rows, :] = ob
        la[rows, :] = (1.0 - sa[rows, :]) * jnp.sum(
            ob.astype(F32) * dob.astype(F32), axis=-1, keepdims=True
        )
        dp = dot_nt(v[...], dob).astype(BF).astype(F32)
        ds = (p * (dp - jnp.sum(p * dp, axis=0, keepdims=True))).astype(BF)
        dq[rows, :] = jnp.where(on[0:128], dot_tn(ds, k[...]) * HEAVY_SCALE, 0.0).astype(BF)
        dk[...] += dot(ds, qb) * HEAVY_SCALE
        dv[...] += dot(pb, dob)
    k[...] = dk[...].astype(BF)
    v[...] = dv[...].astype(BF)

    gw_o = dot_tn(o[...], da[...]).astype(BF)
    gqkv = jnp.concatenate([dq[...], k[...], v[...]], axis=1)
    grad[:, 512:896] = dot_tn(ar[...], gqkv).astype(BF)
    grad[:, 896:1664] = jnp.zeros((768, 768), BF)
    for p6 in range(6):

        @pl.when(low == 128 * p6)
        def _():
            grad[128 * p6 : 128 * p6 + 128, 896:1664] = gw_o

    y[1024:1128, :] = jnp.zeros((104, 768), F32)
    g_a = jnp.zeros((1, 768), F32)
    g_f, g_ra, g_rf = g_a, g_a, g_a
    for b in range(4):
        rows = slice(256 * b, 256 * b + 256)
        frb = fr[rows, :]
        sfb = sf[rows, :]
        dfb = (sfb * gy[rows, :]).astype(BF)
        both = dot(frb, w[:, 0:512])
        act, slope = gelu_parts(both[:, 0:256])
        up = both[:, 256:512]
        hidden = (act * up).astype(BF)
        hid[rows, :] = hidden
        dh = dot_nt(dfb, wd[...])
        lfb = (1.0 - sfb) * jnp.sum(hidden.astype(F32) * dh, axis=-1, keepdims=True)
        dgub = jnp.concatenate([(dh * up * slope).astype(BF), (dh * act).astype(BF)], axis=1)
        dgu[rows, :] = dgub
        y[rows, :] = sa[rows, :] * dot(o[rows, :], wo[...]) + sfb * dot(hidden, wd[...])
        lab = la[rows, :]
        d_f = dot_nt(dgub, w[:, 0:512]) + lfb * r_f
        d_a = (
            dot_nt(dq[rows, :], w[:, 512:640])
            + dot_nt(k[rows, :], w[:, 640:768])
            + dot_nt(v[rows, :], w[:, 768:896])
            + lab * r_a
        )
        u, _ = unit(x[rows, :])
        g_a = g_a + jnp.sum(d_a * u, axis=0, keepdims=True)
        g_f = g_f + jnp.sum(d_f * u, axis=0, keepdims=True)
        g_ra = g_ra + jnp.sum(lab * ar[rows, :].astype(F32), axis=0, keepdims=True)
        g_rf = g_rf + jnp.sum(lfb * frb.astype(F32), axis=0, keepdims=True)
        da[rows, :] = dfb
        gy[rows, :] = d_a * gain_a + d_f * gain_f
    gy[1024:1128, :] = jnp.zeros((104, 768), F32)
    grad[:, 0:512] = dot_tn(fr[...], dgu[...]).astype(BF)
    gd = dot_tn(hid[...], da[...]).astype(BF)
    for r in range(8):
        for t in range(3):
            grad[96 * r + 32 * t : 96 * r + 32 * t + 32, 1792:2048] = gd[
                32 * r : 32 * r + 32, 256 * t : 256 * t + 256
            ]
    vecs = jnp.concatenate(
        [
            g_a + gin[0:1, :],
            g_f + gin[1:2, :],
            g_ra,
            g_rf,
            jnp.zeros((124, 768), F32),
        ],
        axis=0,
    )
    grad[:, 1664:1792] = vecs.T.astype(BF)
    for d in range(16):
        shift = meta[d] & 7
        rows = pl.ds(pl.multiple_of(meta[d] - shift, 8), CAP + 8)
        back = lax.rem(CAP + 8 - shift, CAP + 8)
        parts[d, :, 0:768] = pltpu.roll(y[rows, :], back, 0)[0:CAP].astype(BF)
        parts[d, :, 768:1536] = pltpu.roll(gy[rows, :], back, 0)[0:CAP].astype(BF)


def tokens_kernel(parts, xs, smap, lo, dxg, hl, hr, out, grad):
    total = parts[0].astype(F32)
    for d in range(1, 16):
        total = total + parts[d].astype(F32)
    u, scale = unit(xs[...].astype(F32))
    c = total[:, 768:1536]
    dxr = (scale * (c - u * jnp.mean(u * c, axis=-1, keepdims=True))).astype(BF)
    yb = total[:, 0:768].astype(BF)
    out[...] = (lo[...] + dot_tn(smap[...], yb)).astype(BF)
    dx = dxg[...] + dot_tn(smap[...], dxr)
    grad[0:64, :] = (dx[0:64, :] + hl[...].astype(F32)).astype(BF)
    grad[64:448, :] = dx[64:448, :].astype(BF)
    grad[448:512, :] = (dx[448:512, :] + hr[...].astype(F32)).astype(BF)


def tail_rows(block, low):
    last = jnp.concatenate([block[32 * t : 32 * t + 32, low + 768 : low + 1024] for t in range(3)], axis=1)
    return jnp.concatenate([block[:, low : low + 768], last], axis=0)


def spread_ffn_kernel(r, send):
    pick = pick6(96, 128)
    send[:, 0:2048] = dot_tn(pick, r[:, 0:2048]).astype(BF)
    send[:, 2048:2816] = tail_rows(r[...], 2048)


def spread_rest_kernel(r, send, hd):
    pick = pick6(96, 128)
    send[...] = dot_tn(pick, r[:, 0:4864]).astype(BF)
    hd[...] = jnp.concatenate(
        [r[32 * t : 32 * t + 32, 4864:5120] for t in range(3)], axis=1
    )


def sum_ffn_kernel(got, gate, up, down):
    total = got[0].astype(F32)
    for d in range(1, 16):
        total = total + got[d].astype(F32)
    for c in range(4):
        gate[:, 256 * c : 256 * c + 256] = total[0:6, 512 * c : 512 * c + 256]
        up[:, 256 * c : 256 * c + 256] = total[0:6, 512 * c + 256 : 512 * c + 512]
    down[...] = total[:, 2048:2816]


def sum_rest_kernel(got, q, k, v, o, hq, hk, hv, ho, hgate, hup, vec):
    def total(a, b):
        t = got[0, :, a:b].astype(F32)
        for d in range(1, 16):
            t = t + got[d, :, a:b].astype(F32)
        return t

    light = total(0, 3072)
    for n, ref in enumerate((q, k, v, o)):
        ref[...] = light[0:6, 768 * n : 768 * n + 768]
    for j in range(16):
        hgate[:, 256 * j : 256 * j + 256] = got[j, :, 3072:3328].astype(F32)[0:6]
        hup[:, 256 * j : 256 * j + 256] = got[j, :, 3328:3584].astype(F32)[0:6]
    for p in range(6):
        pair = got[2 * p, :, 3584:3968].astype(F32) + got[2 * p + 1, :, 3584:3968].astype(F32)
        for n, ref in enumerate((hq, hk, hv)):
            ref[:, 128 * p : 128 * p + 128] = pair[0:6, 128 * n : 128 * n + 128]
    rest = total(3968, 4864)
    ho[...] = rest[0:6, 0:768]
    vec[...] = rest[:, 768:896]


def call(kernel, outs, args, scratch=(), in_specs=None, name=None, sems=0):
    return pl.pallas_call(
        kernel,
        out_shape=[jax.ShapeDtypeStruct(s, t) for s, t in outs],
        in_specs=in_specs or [VMEM] * len(args),
        out_specs=[VMEM] * len(outs),
        scratch_shapes=[pltpu.VMEM(s, t) for s, t in scratch]
        + ([pltpu.SemaphoreType.DMA((sems,))] if sems else []),
        compiler_params=PARAMS,
        name=name,
    )(*args)


def body(
    tokens, lengths, routed, cotangent, gain_attn, gain_ffn, router_attn, router_ffn,
    light_q, light_k, light_v, light_o, light_gate, light_up, light_down,
    heavy_q, heavy_k, heavy_v, heavy_o, heavy_gate, heavy_up, heavy_down,
):
    me = lax.axis_index("fsdp")
    vec = jnp.stack([gain_attn, gain_ffn, router_attn, router_ffn], axis=1)
    vec = jnp.pad(vec, ((0, 2), (0, 124)))
    pack, hsend, hd = call(
        prep_kernel,
        [((8, C_ALL), BF), ((16, 8, 896), BF), ((32, 768), BF)],
        (
            light_q, light_k, light_v, light_o, light_gate, light_up, light_down,
            heavy_q, heavy_k, heavy_v, heavy_o, heavy_gate, heavy_up, heavy_down, vec,
        ),
        [((8, 4096), F32)],
        name="prep",
    )
    wall = lax.all_gather(pack, ALL, axis=0, tiled=True)

    hcols = lax.all_to_all(hsend, "fsdp", split_axis=0, concat_axis=0, tiled=True)
    hd = lax.ppermute(hd, ALL, [(d, (d % 8) * 16 + d // 8) for d in range(128)])
    hblock = jnp.concatenate([hcols.reshape(128, 896), jnp.pad(hd, ((0, 0), (0, 128)))], axis=0)
    hw = lax.all_gather(hblock, "dp", axis=0, tiled=False)

    flat = routed[0]
    edges = jnp.arange(17, dtype=jnp.int32) * 512
    bounds = jnp.sum((flat[None, :] < edges[:, None]).astype(jnp.int32), axis=1)
    start = lax.dynamic_index_in_dim(bounds, me, keepdims=False)
    stop = lax.dynamic_index_in_dim(bounds, me + 1, keepdims=False)
    mine = lax.dynamic_slice_in_dim(jnp.pad(flat, (0, CAP)), start, CAP) - me * 512
    valid = start + jnp.arange(CAP, dtype=jnp.int32) < stop
    smap = ((mine[:, None] == jnp.arange(512, dtype=jnp.int32)[None, :]) & valid[:, None]).astype(BF)
    xslots = dot(smap, tokens).astype(BF)
    gslots = dot(smap, cotangent).astype(BF)

    def to_pack(rows):
        many = jnp.broadcast_to(rows[None], (16, CAP, 768))
        return lax.all_to_all(many, "fsdp", split_axis=0, concat_axis=0, tiled=True)

    xs, gs = to_pack(xslots), to_pack(gslots)
    right = [(i, i + 1) for i in range(15)]
    left = [(i + 1, i) for i in range(15)]
    xl = lax.ppermute(tokens[448:512], "fsdp", right)
    xr = lax.ppermute(tokens[0:64], "fsdp", left)

    ffn, cf, grad_ffn, gvec = call(
        light_ffn_kernel,
        [((512, 768), F32), ((512, 768), F32), ((768, 3072), BF), ((8, 768), F32)],
        (tokens, cotangent, wall),
        [
            ((768, 2048), BF), ((512, 768), BF),
            ((1024, 2048), BF), ((1024, 768), BF), ((1024, 128), BF),
        ],
        [VMEM, VMEM, HBM],
        sems=3,
        name="light_ffn",
    )
    rs_ffn = lax.psum_scatter(grad_ffn, "dp", scatter_dimension=0, tiled=True)

    meta = jnp.stack([lengths[0, 0], me * 512, jnp.int32(8192)])
    lo, dxg, halo, grad_attn, gvec = call(
        light_attn_kernel,
        [
            ((512, 768), F32), ((512, 768), F32), ((128, 768), BF),
            ((768, 3072), BF), ((8, 768), F32),
        ],
        (meta, xl, tokens, xr, cotangent, wall, ffn, cf, gvec),
        [
            ((768, 3072), BF), ((640, 768), BF), ((640, 768), BF),
            ((512, 1024), BF), ((640, 1024), BF), ((640, 1024), BF),
            ((512, 1024), BF), ((512, 1024), BF), ((512, 1024), BF),
            ((640, 1024), F32), ((640, 1024), F32), ((4, 256, 128), F32),
            ((1024, 1024), BF), ((1024, 1024), BF), ((1024, 1024), BF),
            ((1024, 768), BF), ((1024, 128), BF),
        ],
        [SMEM] + [VMEM] * 4 + [HBM] + [VMEM] * 3,
        sems=5,
        name="light_attn",
    )
    hr = lax.ppermute(halo[0:64], "fsdp", left)
    hl = lax.ppermute(halo[64:128], "fsdp", right)

    pair = jnp.where(me < 12, me // 2, 5)
    hmeta = jnp.concatenate(
        [
            bounds,
            jnp.stack([lengths[0, 0] // 8, 128 * pair, jnp.where(me < 12, me % 2, 2)]),
        ]
    )
    parts, grad_heavy = call(
        heavy_kernel,
        [((16, CAP, 1536), BF), ((768, 2048), BF)],
        (hmeta, xs, gs, hw, wall, gvec),
        [
            ((1128, 768), F32), ((1128, 768), F32), ((768, 896), BF), ((256, 768), BF), ((128, 768), BF),
            ((1024, 768), BF), ((1024, 768), BF),
            ((1024, 128), BF), ((1024, 128), BF), ((1024, 128), BF),
            ((1024, 128), BF), ((1024, 128), BF), ((1024, 128), BF),
            ((1024, 128), F32), ((1024, 128), F32), ((1024, 128), F32),
            ((1024, 768), BF), ((1024, 512), BF), ((1024, 256), BF), ((1128, 768), F32),
            ((1024, 1), F32), ((1024, 1), F32), ((1024, 1), F32),
            ((1024, 768), BF), ((1024, 128), BF),
        ],
        [SMEM, VMEM, VMEM, VMEM, HBM, VMEM],
        sems=2,
        name="heavy",
    )
    home = lax.all_to_all(parts, "fsdp", split_axis=0, concat_axis=0, tiled=True)
    rest = jnp.concatenate([grad_attn, grad_heavy], axis=1)
    rs_rest = lax.psum_scatter(rest, "dp", scatter_dimension=0, tiled=True)

    output, grad_tokens = call(
        tokens_kernel,
        [((512, 768), BF), ((512, 768), BF)],
        (home, xslots, smap, lo, dxg, hl, hr),
        name="tokens",
    )

    (send_ffn,) = call(spread_ffn_kernel, [((128, 2816), BF)], (rs_ffn,), name="spread_ffn")
    got_ffn = lax.all_to_all(
        send_ffn.reshape(16, 8, 2816), "fsdp", split_axis=0, concat_axis=0, tiled=True
    )
    g_gate, g_up, g_down = call(
        sum_ffn_kernel,
        [((6, 1024), F32), ((6, 1024), F32), ((8, 768), F32)],
        (got_ffn,),
        name="sum_ffn",
    )
    send_rest, g_hd = call(
        spread_rest_kernel, [((128, 4864), BF), ((32, 768), BF)], (rs_rest,), name="spread_rest"
    )
    g_hd = lax.ppermute(g_hd, ALL, [((d % 8) * 16 + d // 8, d) for d in range(128)])
    got = lax.all_to_all(
        send_rest.reshape(16, 8, 4864), "fsdp", split_axis=0, concat_axis=0, tiled=True
    )
    six = ((6, 768), F32)
    g_q, g_k, g_v, g_o, g_hq, g_hk, g_hv, g_ho, g_hgate, g_hup, g_vec = call(
        sum_rest_kernel,
        [six] * 8 + [((6, 4096), F32), ((6, 4096), F32), ((8, 128), F32)],
        (got,),
        name="sum_rest",
    )
    return (
        output, grad_tokens,
        g_vec[0:6, 0], g_vec[0:6, 1], g_vec[0:6, 2], g_vec[0:6, 3],
        g_q, g_k, g_v, g_o, g_gate, g_up, g_down,
        g_hq, g_hk, g_hv, g_ho, g_hgate, g_hup, g_hd.astype(F32),
    )


def solution(mesh):
    rows = P(ALL, None)
    flat = P(ALL)
    in_specs = (rows, P("dp", None), P("dp", None), rows) + (flat,) * 4 + (rows,) * 14
    out_specs = (rows, rows) + (flat,) * 4 + (rows,) * 14
    return jax.shard_map(body, mesh=mesh, in_specs=in_specs, out_specs=out_specs, check_vma=False)
```

```python
import jax
import jax.numpy as jnp
from jax import lax
from jax.experimental import pallas as pl
from jax.experimental.pallas import tpu as pltpu
from jax.sharding import PartitionSpec as P

BF = jnp.bfloat16
F32 = jnp.float32
EPS = 1e-6
NEG = -1e30
ALL = ("dp", "fsdp")
CAP = 96
LIGHT_SCALE = 96**-0.5
HEAVY_SCALE = 64**-0.5
PARAMS = pltpu.CompilerParams(vmem_limit_bytes=60 * 1024 * 1024)
SMEM = pl.BlockSpec(memory_space=pltpu.SMEM)
VMEM = pl.BlockSpec(memory_space=pltpu.VMEM)
HBM = pl.BlockSpec(memory_space=pl.ANY)

C_QKVO, C_VEC, C_DOWN, C_HO, C_ALL = 2048, 5120, 5248, 6016, 6784
L_GU, L_DOWN, L_ALL = 3072, 5120, 6144
S_HEAVY, S_BACK, S_ALL = 5888, 7680, 9216
H_HO, H_VEC, H_DOWN, H_ALL = 896, 1664, 1792, 2048


def dot(a, b):
    return jnp.dot(a, b, preferred_element_type=F32)


def dot_nt(a, b):
    return lax.dot_general(a, b, (((1,), (1,)), ((), ())), preferred_element_type=F32)


def dot_tn(a, b):
    return lax.dot_general(a, b, (((0,), (0,)), ((), ())), preferred_element_type=F32)


def pick6(rows, cols, shift=0):
    r = lax.broadcasted_iota(jnp.int32, (rows, cols), 0) + shift
    c = lax.broadcasted_iota(jnp.int32, (rows, cols), 1)
    low = c & 7
    return ((6 * (c >> 3) + low == r) & (low < 6)).astype(F32).astype(BF)


def unpad_rows(ref, out_ref, pick, at=0, width=None):
    width = width or ref.shape[1]
    for b in range(8):
        block = dot(pick, ref[128 * b : 128 * b + 128, at : at + width])
        out_ref[96 * b : 96 * b + 96, at : at + width] = block.astype(BF)


def vector_rows(vec_ref, pick):
    blocks = [dot(pick, vec_ref[128 * b : 128 * b + 128, :]) for b in range(8)]
    return jnp.concatenate(blocks, axis=0).T


class Copies:
    def __init__(self, sems):
        self.sems, self.used, self.open = sems, 0, []

    def start(self, src, dst):
        copy = pltpu.make_async_copy(src, dst, self.sems.at[self.used])
        self.used += 1
        copy.start()
        return copy

    def send(self, src, dst):
        self.open.append(self.start(src, dst))

    def finish(self):
        for copy in self.open:
            copy.wait()


def unit(rows):
    scale = lax.rsqrt(jnp.mean(rows * rows, axis=-1, keepdims=True) + EPS)
    return rows * scale, scale


def gelu_parts(gate):
    c0, c1 = 0.7978845608, 0.044715
    sq = gate * gate
    t = jnp.tanh(gate * (c0 + (c0 * c1) * sq))
    half = 0.5 * (1.0 + t)
    slope = half + (0.5 * gate) * (1.0 - t * t) * (c0 + (3.0 * c0 * c1) * sq)
    return gate * half, slope


def prep_kernel(
    q, k, v, o, gate, up, down, hq, hk, hv, ho, hgate, hup, hdown, vec, pack, hsend, hd, scr
):
    scr[...] = jnp.zeros_like(scr)
    zero128 = jnp.zeros((8, 128), BF)

    def padded(ref):
        cols = ref.shape[1]
        scr[0:6, 0:cols] = ref[...]
        return scr[:, 0:cols].astype(BF)

    gp, upp = padded(gate), padded(up)
    for c in range(4):
        pack[:, 512 * c : 512 * c + 256] = gp[:, 256 * c : 256 * c + 256]
        pack[:, 512 * c + 256 : 512 * c + 512] = upp[:, 256 * c : 256 * c + 256]
    for n, ref in enumerate((q, k, v, o)):
        pack[:, C_QKVO + 768 * n : C_QKVO + 768 * n + 768] = padded(ref)
    pack[:, C_VEC : C_VEC + 128] = vec[...].astype(BF)
    pack[:, C_DOWN : C_DOWN + 768] = down[...].astype(BF)
    pack[:, C_HO : C_HO + 768] = padded(ho)
    wq, wk, wv = padded(hq), padded(hk), padded(hv)
    wg, wu = padded(hgate), padded(hup)
    for j in range(16):
        hsend[j, :, 0:256] = wg[:, 256 * j : 256 * j + 256]
        hsend[j, :, 256:512] = wu[:, 256 * j : 256 * j + 256]
        for n, w in enumerate((wq, wk, wv)):
            p = j // 2
            part = w[:, 128 * p : 128 * p + 128] if j < 12 else zero128
            hsend[j, :, 512 + 128 * n : 640 + 128 * n] = part
    hd[...] = hdown[...].astype(BF)


def light_ffn_kernel(
    x, g, wall, ffn, cf, light, gvec, gu, fin, fin_t, gbuf, gu_pad, down, vec, in_sems, out_sems
):
    loads, stores = Copies(in_sems), Copies(out_sems)
    got_vec = loads.start(wall.at[:, C_VEC : C_VEC + 128], vec)
    got = []
    for c in range(4):
        wide, rows = pl.ds(512 * c, 512), pl.ds(256 * c, 256)
        got.append(
            (
                loads.start(wall.at[:, wide], gu_pad.at[:, wide]),
                loads.start(wall.at[rows, C_DOWN : C_DOWN + 768], down.at[rows, :]),
            )
        )
    pick = pick6(96, 128)
    u, _ = unit(x[...].astype(F32))
    got_vec.wait()
    gain_f = vector_rows(vec, pick)[1:2, :]
    f = (u * gain_f).astype(BF)
    fin[...] = f
    fin_t[...] = f.T
    for c in range(4):
        for copy in got[c]:
            copy.wait()
        unpad_rows(gu_pad, gu, pick, 512 * c, 512)
        w = gu[:, 512 * c : 512 * c + 512]
        wd = down[256 * c : 256 * c + 256, :]
        both = dot(fin[...], w)
        act, slope = gelu_parts(both[:, 0:256])
        up = both[:, 256:512]
        hidden = (act * up).astype(BF)
        dh = dot_nt(g[...], wd)
        dgu = jnp.concatenate([(dh * up * slope).astype(BF), (dh * act).astype(BF)], axis=1)
        term = dot(hidden, wd)
        dterm = dot_nt(dgu, w)
        if c == 0:
            ffn[...] = term
            cf[...] = dterm
        else:
            ffn[...] += term
            cf[...] += dterm
        gbuf[:, 512 * c : 512 * c + 512] = dot(fin_t[...], dgu).astype(BF)
        gd = dot_tn(hidden, g[...]).astype(BF)
        for n in range(2):
            b, r0 = 2 * c + n, 128 * n
            gbuf[96 * b : 96 * b + 96, 2048:2816] = gd[r0 : r0 + 96, :]
            for t in range(3):
                gbuf[96 * b + 32 * t : 96 * b + 32 * t + 32, 2816:3072] = gd[
                    r0 + 96 : r0 + 128, 256 * t : 256 * t + 256
                ]
        wide, rows = pl.ds(512 * c, 512), pl.ds(192 * c, 192)
        stores.send(gbuf.at[:, wide], light.at[:, pl.ds(L_GU + 512 * c, 512)])
        stores.send(gbuf.at[rows, 2048:3072], light.at[rows, L_DOWN:L_ALL])
    u, _ = unit(x[...].astype(F32))
    d_f = cf[...]
    gvec[...] = jnp.zeros_like(gvec)
    gvec[1:2, :] = jnp.sum(d_f * u, axis=0, keepdims=True)
    cf[...] = d_f * gain_f
    stores.finish()


def light_attn_kernel(
    meta, xl, x, xr, g, wall, ffn_in, cf_in, gin, light_in,
    lo, dxg, halo, light, gvec,
    w, xs, a, q, k, v, o, do, dqkv, dk, dv, mask, w_pad, vec, ffn, cf, lo_buf, gbuf, in_sems, out_sems,
):
    loads, stores = Copies(in_sems), Copies(out_sems)
    got_vec = loads.start(wall.at[:, C_VEC : C_VEC + 128], vec)
    got = []
    for n in range(4):
        wide = pl.ds(768 * n, 768)
        got.append(loads.start(wall.at[:, C_QKVO + 768 * n : C_QKVO + 768 * n + 768], w_pad.at[:, wide]))
    got_ffn = loads.start(ffn_in, ffn)
    got_cf = loads.start(cf_in, cf)
    pick = pick6(96, 128)
    xs[0:64, :] = xl[...]
    xs[64:576, :] = x[...]
    xs[576:640, :] = xr[...]
    first, base, pack_len = meta[0], meta[1], meta[2]
    key = lax.broadcasted_iota(jnp.int32, (256, 256), 0)
    qry = lax.broadcasted_iota(jnp.int32, (256, 256), 1) & 127
    gap = key - qry
    for b in range(4):
        qpos = base + 128 * b + qry
        kpos = base + 128 * b - 64 + key
        ok = (gap >= 0) & (gap <= 128) & ((qpos < first) == (kpos < first))
        ok = ok & (kpos >= 0) & (kpos < pack_len)
        mask[b] = jnp.where(ok, 0.0, NEG)
    dk[...] = jnp.zeros_like(dk)
    dv[...] = jnp.zeros_like(dv)
    dqkv[0:64, 0:768] = jnp.zeros((64, 768), BF)
    dqkv[576:640, 0:768] = jnp.zeros((64, 768), BF)
    u, _ = unit(xs[...].astype(F32))
    got_vec.wait()
    gain_a = vector_rows(vec, pick)[0:1, :]
    a[...] = (u * gain_a).astype(BF)
    outs = ((64, 576, q), (0, 640, k), (0, 640, v))
    for n, (r0, r1, ref) in enumerate(outs):
        got[n].wait()
        unpad_rows(w_pad, w, pick, 768 * n, 768)
        ref[...] = dot(a[r0:r1, :], w[:, 768 * n : 768 * n + 768]).astype(BF)
    got[3].wait()
    unpad_rows(w_pad, w, pick, 2304, 768)
    do[...] = dot_nt(g[...], w[:, 2304:3072]).astype(BF)

    lane = lax.broadcasted_iota(jnp.int32, (128, 256), 1)

    def pair(b, group, second):
        low = 64 * second
        even = (lane >= low) & (lane < low + 96)
        odd = (lane >= low + 96) & (lane < low + 192)

        def split(t):
            zero = jnp.zeros_like(t)
            return jnp.concatenate([jnp.where(even, t, zero), jnp.where(odd, t, zero)], axis=0)

        def join(t):
            return jnp.where(even, t[0:128], 0.0) + jnp.where(odd, t[128:256], 0.0)

        win = slice(384 * group + 128 * second, 384 * group + 128 * second + 256)
        rq = pl.ds(pl.multiple_of(128 * b, 128), 128)
        rk = pl.ds(pl.multiple_of(128 * b, 128), 256)
        kw, vw = k[rk, win], v[rk, win]
        q2, do2 = split(q[rq, win]), split(do[rq, win])
        s = dot_nt(kw, q2) * LIGHT_SCALE + mask[b]
        dp = dot_nt(vw, do2).astype(BF).astype(F32)
        e = jnp.exp(s - jnp.max(s, axis=0, keepdims=True))
        p = e * (1.0 / jnp.sum(e, axis=0, keepdims=True))
        pb = p.astype(BF)
        ds = (p * (dp - jnp.sum(p * dp, axis=0, keepdims=True))).astype(BF)
        dk[rk, win] += dot(ds, q2) * LIGHT_SCALE
        dv[rk, win] += dot(pb, do2)
        return join(dot_tn(pb, vw)), join(dot_tn(ds, kw)) * LIGHT_SCALE

    @pl.loop(0, 4)
    def _(b):
        rq = pl.ds(pl.multiple_of(128 * b, 128), 128)
        rd = pl.ds(pl.multiple_of(128 * b + 64, 64), 128)
        for group in range(2):
            o0, dq0 = pair(b, group, 0)
            o1, dq1 = pair(b, group, 1)
            c0 = 384 * group
            for ref, rows, t0, t1 in ((o, rq, o0, o1), (dqkv, rd, dq0, dq1)):
                ref[rows, c0 : c0 + 128] = t0[:, 0:128].astype(BF)
                ref[rows, c0 + 128 : c0 + 256] = (t0[:, 128:256] + t1[:, 0:128]).astype(BF)
                ref[rows, c0 + 256 : c0 + 384] = t1[:, 128:256].astype(BF)

    got_ffn.wait()
    lo_buf[...] = x[...].astype(F32) + ffn[...] + dot(o[...], w[:, 2304:3072])
    stores.send(lo_buf, lo)
    gbuf[:, 2304:3072] = dot_tn(o[...], g[...]).astype(BF)
    stores.send(gbuf.at[:, 2304:3072], light.at[:, 2304:3072])
    dqkv[:, 768:1536] = dk[...].astype(BF)
    dqkv[:, 1536:2304] = dv[...].astype(BF)
    a_t = a[...].T
    for n in range(3):
        wide = pl.ds(768 * n, 768)
        gbuf[:, wide] = dot(a_t, dqkv[:, wide]).astype(BF)
        stores.send(gbuf.at[:, wide], light.at[:, wide])
    d_a = dot_nt(dqkv[...], w[:, 0:2304])
    u, scale = unit(xs[...].astype(F32))
    gvec[...] = gin[...]
    gvec[0:1, :] = jnp.sum(d_a * u, axis=0, keepdims=True)

    def norm_back(c, rows):
        ur = u[rows]
        return scale[rows] * (c - ur * jnp.mean(ur * c, axis=-1, keepdims=True))

    got_cf.wait()
    own = slice(64, 576)
    dxg[...] = norm_back(d_a[own] * gain_a + cf[...], own) + g[...].astype(F32)
    halo[0:64, :] = norm_back(d_a[0:64, :] * gain_a, slice(0, 64)).astype(BF)
    halo[64:128, :] = norm_back(d_a[576:640, :] * gain_a, slice(576, 640)).astype(BF)
    stores.finish()


def slots_kernel(meta, routed, x, g, slots, st):
    me = meta[20]
    start = meta[me]
    token = lax.broadcasted_iota(jnp.int32, (512, 1024), 0) + 512 * me
    r = jnp.broadcast_to(routed[...], (512, 1024))
    rank = jnp.sum((r < token).astype(F32), axis=1, keepdims=True).astype(jnp.int32) - start
    hit = jnp.sum((r == token).astype(F32), axis=1, keepdims=True)
    row = ((start + rank) & 15) * 8 + (rank >> 4)
    row = jnp.where((hit > 0.5) & (rank < CAP), row, -1)
    lane = lax.broadcasted_iota(jnp.int32, (512, 128), 1)
    onehot = (lane == row).astype(F32).astype(BF)
    st[...] = onehot
    slots[:, 0:768] = dot_tn(onehot, x[...]).astype(BF)
    slots[:, 768:1536] = dot_tn(onehot, g[...]).astype(BF)


def entry_slots(meta):
    p = 16 * lax.broadcasted_iota(jnp.int32, (64, 128), 0) + meta[20]
    source, before = jnp.zeros_like(p), jnp.zeros_like(p)
    for d in range(1, 16):
        source = source + (p >= meta[d]).astype(jnp.int32)
        before = jnp.where(p >= meta[d], meta[d], before)
    rank = p - before
    lane = lax.broadcasted_iota(jnp.int32, (64, 128), 1)
    return ((lane == source * 8 + (rank >> 4)) & (rank < CAP)).astype(F32).astype(BF)


def entries_kernel(meta, got, own, many):
    rows = dot(entry_slots(meta), got[...]).astype(BF)
    own[...] = rows
    for t in range(16):
        many[t] = rows


def home_kernel(meta, parts, own, send_in, send, back, sems):
    total = parts[0].astype(F32)
    for t in range(1, 16):
        total = total + parts[t].astype(F32)
    u, scale = unit(own[:, 0:768].astype(F32))
    c = total[:, 768:1536]
    dxr = scale * (c - u * jnp.mean(u * c, axis=-1, keepdims=True))
    onehot = entry_slots(meta)
    back[:, 0:768] = dot_tn(onehot, total[:, 0:768].astype(BF)).astype(BF)
    back[:, 768:1536] = dot_tn(onehot, dxr.astype(BF)).astype(BF)
    Copies(sems).start(back, send.at[:, S_BACK:S_ALL]).wait()


def entry_of(row):
    return ((row & 63) << 4) + (row >> 6)


def heavy_kernel(
    meta, xg_in, hw_in, wall, gin,
    parts, keep, give,
    xg, w, wd, wo, ar, fr, q, k, v, o, do, dqkv, dk, dv, kmask, da, dgu, hid, sa, sf, la,
    hw, wo_pad, vec, pbuf, gbuf, gvec, in_sems, out_sems,
):
    loads, stores = Copies(in_sems), Copies(out_sems)
    got_vec = loads.start(wall.at[:, C_VEC : C_VEC + 128], vec)
    got_hw = loads.start(hw_in, hw)
    got_wo = loads.start(wall.at[:, C_HO : C_HO + 768], wo_pad)
    got_xg = loads.start(xg_in, xg)
    pick = pick6(96, 128)
    kid = entry_of(lax.broadcasted_iota(jnp.int32, (1024, 128), 0))
    km = jnp.zeros((1024, 128), F32)
    for d in range(16):
        km = jnp.where((kid >= meta[d] + CAP) & (kid < meta[d + 1]), NEG, km)
    kmask[...] = km
    got_vec.wait()
    vrows = vector_rows(vec, pick)
    gain_a, gain_f, r_a, r_f = (vrows[n : n + 1, :] for n in range(4))
    got_hw.wait()
    for b in range(8):
        w[96 * b : 96 * b + 96, :] = dot(pick, hw[b, 0:128, :]).astype(BF)
        wd[32 * b : 32 * b + 32, :] = hw[b, 128:160, 0:768]
    got_wo.wait()
    low, head = meta[18], meta[19]
    head_row = lax.broadcasted_iota(jnp.int32, (128, 1024), 0) >> 6
    mine = jnp.where(head_row == head, pick6(128, 1024, low).astype(F32), 0.0).astype(BF)
    wo[...] = dot(mine, wo_pad[...]).astype(BF)
    on = (lax.broadcasted_iota(jnp.int32, (256, 128), 1) >> 6) == head
    got_xg.wait()

    @pl.loop(0, 4)
    def _(b):
        rows = pl.ds(pl.multiple_of(256 * b, 256), 256)
        u, _ = unit(xg[rows, 0:768].astype(F32))
        arb, frb = (u * gain_a).astype(BF), (u * gain_f).astype(BF)
        ar[rows, :], fr[rows, :] = arb, frb
        sab = jax.nn.sigmoid(jnp.sum(arb.astype(F32) * r_a, axis=-1, keepdims=True))
        sfb = jax.nn.sigmoid(jnp.sum(frb.astype(F32) * r_f, axis=-1, keepdims=True))
        sa[rows, :], sf[rows, :] = sab, sfb
        qkv = dot(arb, w[:, 512:896])
        q[rows, :] = jnp.where(on, qkv[:, 0:128], 0.0).astype(BF)
        k[rows, :] = qkv[:, 128:256].astype(BF)
        v[rows, :] = jnp.where(on, qkv[:, 256:384], 0.0).astype(BF)
        dab = (sab * xg[rows, 768:1536].astype(F32)).astype(BF)
        da[rows, :] = dab
        do[rows, :] = dot_nt(dab, wo[...]).astype(BF)

    n0 = meta[17]
    dk[...] = jnp.zeros_like(dk)
    dv[...] = jnp.zeros_like(dv)

    @pl.loop(0, 4)
    def _(b):
        rows = pl.ds(pl.multiple_of(256 * b, 256), 256)
        kid = entry_of(lax.broadcasted_iota(jnp.int32, (1024, 256), 0))
        qid = entry_of(lax.broadcasted_iota(jnp.int32, (1024, 256), 1) + 256 * b)
        km = kmask[...]
        bias = jnp.where((kid < n0) == (qid < n0), jnp.concatenate([km, km], axis=1), NEG)
        qb, dob = q[rows, :], do[rows, :]
        s = dot_nt(k[...], qb) * HEAVY_SCALE + bias
        e = jnp.exp(s - jnp.max(s, axis=0, keepdims=True))
        p = e * (1.0 / jnp.sum(e, axis=0, keepdims=True))
        pb = p.astype(BF)
        ob = dot_tn(pb, v[...]).astype(BF)
        o[rows, :] = ob
        la[rows, :] = (1.0 - sa[rows, :]) * jnp.sum(
            ob.astype(F32) * dob.astype(F32), axis=-1, keepdims=True
        )
        dp = dot_nt(v[...], dob).astype(BF).astype(F32)
        ds = (p * (dp - jnp.sum(p * dp, axis=0, keepdims=True))).astype(BF)
        dqkv[rows, 0:128] = jnp.where(on, dot_tn(ds, k[...]) * HEAVY_SCALE, 0.0).astype(BF)
        dk[...] += dot(ds, qb) * HEAVY_SCALE
        dv[...] += dot(pb, dob)

    dqkv[:, 128:256] = dk[...].astype(BF)
    dqkv[:, 256:384] = dv[...].astype(BF)
    gbuf[:, 512:896] = dot_tn(ar[...], dqkv[...]).astype(BF)
    gbuf[:, H_HO:H_VEC] = jnp.zeros((768, 768), BF)
    gbuf[pl.ds(pl.multiple_of(low, 128), 128), H_HO:H_VEC] = dot_tn(o[...], da[...]).astype(BF)
    gvec[...] = gin[...]

    @pl.loop(0, 4)
    def _(b):
        rows = pl.ds(pl.multiple_of(256 * b, 256), 256)
        frb = fr[rows, :]
        sfb = sf[rows, :]
        dfb = (sfb * xg[rows, 768:1536].astype(F32)).astype(BF)
        both = dot(frb, w[:, 0:512])
        act, slope = gelu_parts(both[:, 0:256])
        up = both[:, 256:512]
        hidden = (act * up).astype(BF)
        hid[rows, :] = hidden
        dh = dot_nt(dfb, wd[...])
        lfb = (1.0 - sfb) * jnp.sum(hidden.astype(F32) * dh, axis=-1, keepdims=True)
        dgub = jnp.concatenate([(dh * up * slope).astype(BF), (dh * act).astype(BF)], axis=1)
        dgu[rows, :] = dgub
        y = sa[rows, :] * dot(o[rows, :], wo[...]) + sfb * dot(hidden, wd[...])
        lab = la[rows, :]
        d_f = dot_nt(dgub, w[:, 0:512]) + lfb * r_f
        d_a = dot_nt(dqkv[rows, :], w[:, 512:896]) + lab * r_a
        u, _ = unit(xg[rows, 0:768].astype(F32))
        gvec[0:1, :] += jnp.sum(d_a * u, axis=0, keepdims=True)
        gvec[1:2, :] += jnp.sum(d_f * u, axis=0, keepdims=True)
        gvec[2:3, :] += jnp.sum(lab * ar[rows, :].astype(F32), axis=0, keepdims=True)
        gvec[3:4, :] += jnp.sum(lfb * frb.astype(F32), axis=0, keepdims=True)
        da[rows, :] = dfb
        pbuf[rows, 0:768] = y.astype(BF)
        pbuf[rows, 768:1536] = (d_a * gain_a + d_f * gain_f).astype(BF)

    stores.send(pbuf, parts)
    gbuf[:, 0:512] = dot_tn(fr[...], dgu[...]).astype(BF)
    vecs = jnp.concatenate([gvec[...], jnp.zeros((120, 768), F32)], axis=0)
    gbuf[:, H_VEC:H_DOWN] = vecs.T.astype(BF)
    gd = dot_tn(hid[...], da[...]).astype(BF)
    for r in range(8):
        for t in range(3):
            gbuf[96 * r + 32 * t : 96 * r + 32 * t + 32, H_DOWN:H_ALL] = gd[
                32 * r : 32 * r + 32, 256 * t : 256 * t + 256
            ]
    for z in range(4):
        for ref, core in ((keep, meta[22]), (give, 1 - meta[22])):
            rows = pl.ds(pl.multiple_of(96 * (2 * z + core), 96), 96)
            stores.send(gbuf.at[rows, :], ref.at[z])
    stores.finish()


def core_sum_kernel(meta, keep, got, own, to1, to2, to3):
    for n, ref in enumerate((own, to1, to2, to3)):
        z = (meta[21] + n) & 3
        ref[...] = (keep[z].astype(F32) + got[z].astype(F32)).astype(BF)


def tokens_kernel(got, st, lo, dxg, hl, hr, out, grad):
    back = dot(st[...], got[:, :, S_BACK:S_ALL].reshape(128, 1536))
    out[...] = (lo[...] + back[:, 0:768]).astype(BF)
    dx = dxg[...] + back[:, 768:1536]
    grad[0:64, :] = (dx[0:64, :] + hl[...].astype(F32)).astype(BF)
    grad[64:448, :] = dx[64:448, :].astype(BF)
    grad[448:512, :] = (dx[448:512, :] + hr[...].astype(F32)).astype(BF)


def tail_rows(block, low):
    last = jnp.concatenate([block[32 * t : 32 * t + 32, low + 768 : low + 1024] for t in range(3)], axis=1)
    return jnp.concatenate([block[:, low : low + 768], last], axis=0)


def spread_heavy_kernel(own, a, b, c, send, hd, rows, sems):
    total = own[...].astype(F32) + a[...].astype(F32) + b[...].astype(F32) + c[...].astype(F32)
    low = total.astype(BF)
    rows[...] = dot_tn(pick6(96, 128), low[:, 0:H_DOWN]).astype(BF)
    copy = Copies(sems).start(rows, send.at[:, S_HEAVY:S_BACK])
    hd[...] = jnp.concatenate([low[32 * t : 32 * t + 32, H_DOWN:H_ALL] for t in range(3)], axis=1)
    copy.wait()


def spread_light_kernel(r, send_in, send, rows, sems):
    pick = pick6(96, 128)
    rows[:, 0:L_DOWN] = dot_tn(pick, r[:, 0:L_DOWN]).astype(BF)
    rows[:, L_DOWN:S_HEAVY] = tail_rows(r[...], L_DOWN)
    Copies(sems).start(rows, send.at[:, 0:S_HEAVY]).wait()


def sum_parts(got, a, b):
    t = got[0, :, a:b].astype(F32)
    for d in range(1, 16):
        t = t + got[d, :, a:b].astype(F32)
    return t


def sum_light_kernel(got, q, k, v, o, gate, up, down):
    for n, ref in enumerate((q, k, v, o)):
        ref[...] = sum_parts(got, 768 * n, 768 * n + 768)[0:6]
    for c in range(4):
        both = sum_parts(got, L_GU + 512 * c, L_GU + 512 * c + 512)
        gate[:, 256 * c : 256 * c + 256] = both[0:6, 0:256]
        up[:, 256 * c : 256 * c + 256] = both[0:6, 256:512]
    down[...] = sum_parts(got, L_DOWN, L_DOWN + 768)


def sum_heavy_kernel(got, hq, hk, hv, ho, hgate, hup, vec):
    at = S_HEAVY
    for j in range(16):
        hgate[:, 256 * j : 256 * j + 256] = got[j, :, at : at + 256].astype(F32)[0:6]
        hup[:, 256 * j : 256 * j + 256] = got[j, :, at + 256 : at + 512].astype(F32)[0:6]
    at = S_HEAVY + 512
    for p in range(6):
        pair = got[2 * p, :, at : at + 384].astype(F32) + got[2 * p + 1, :, at : at + 384].astype(F32)
        for n, ref in enumerate((hq, hk, hv)):
            ref[:, 128 * p : 128 * p + 128] = pair[0:6, 128 * n : 128 * n + 128]
    ho[...] = sum_parts(got, S_HEAVY + H_HO, S_HEAVY + H_VEC)[0:6]
    vec[...] = sum_parts(got, S_HEAVY + H_VEC, S_BACK)


def last_kernel(
    got, st, lo, dxg, hl, hr,
    out, grad, q, k, v, o, gate, up, down, hq, hk, hv, ho, hgate, hup, vec,
):
    tokens_kernel(got, st, lo, dxg, hl, hr, out, grad)
    sum_light_kernel(got, q, k, v, o, gate, up, down)
    sum_heavy_kernel(got, hq, hk, hv, ho, hgate, hup, vec)


def call(kernel, outs, args, scratch=(), in_specs=None, out_specs=None, sems=(), name=None, us=0.05, aliases={}):
    return pl.pallas_call(
        kernel,
        out_shape=[jax.ShapeDtypeStruct(s, t) for s, t in outs],
        in_specs=in_specs or [VMEM] * len(args),
        out_specs=out_specs or [VMEM] * len(outs),
        scratch_shapes=[pltpu.VMEM(s, t) for s, t in scratch]
        + [pltpu.SemaphoreType.DMA((n,)) for n in sems],
        compiler_params=PARAMS,
        cost_estimate=pl.CostEstimate(
            flops=int(us * 1.0e9), bytes_accessed=int(us * 3.0e6), transcendentals=0
        ),
        input_output_aliases=aliases,
        name=name,
    )(*args)


def run_light_ffn(tokens, cotangent, wall):
    return call(
        light_ffn_kernel,
        [((512, 768), F32), ((512, 768), F32), ((768, L_ALL), BF), ((8, 768), F32)],
        (tokens, cotangent, wall),
        [
            ((768, 2048), BF), ((512, 768), BF), ((768, 512), BF), ((768, 3072), BF),
            ((1024, 2048), BF), ((1024, 768), BF), ((1024, 128), BF),
        ],
        [VMEM, VMEM, HBM],
        [VMEM, VMEM, HBM, VMEM],
        sems=(9, 8),
        name="light_ffn",
        us=200,
    )


def run_light_attn(meta, xl, tokens, xr, cotangent, wall, ffn, cf, gvec, light):
    return call(
        light_attn_kernel,
        [
            ((512, 768), F32), ((512, 768), F32), ((128, 768), BF), ((768, L_ALL), BF), ((8, 768), F32),
        ],
        (meta, xl, tokens, xr, cotangent, wall, ffn, cf, gvec, light),
        [
            ((768, 3072), BF), ((640, 768), BF), ((640, 768), BF),
            ((512, 768), BF), ((640, 768), BF), ((640, 768), BF),
            ((512, 768), BF), ((512, 768), BF), ((640, 2304), BF),
            ((640, 768), F32), ((640, 768), F32), ((4, 256, 256), F32),
            ((1024, 3072), BF), ((1024, 128), BF), ((512, 768), F32), ((512, 768), F32),
            ((512, 768), F32), ((768, 3072), BF),
        ],
        [SMEM] + [VMEM] * 4 + [HBM] * 3 + [VMEM, HBM],
        [HBM, VMEM, VMEM, HBM, VMEM],
        sems=(7, 5),
        name="light_attn",
        us=2,
        aliases={9: 3},
    )


def run_heavy(meta, xg, hw, wall, gvec):
    col = ((1024, 1), F32)
    rows, narrow = ((1024, 768), BF), ((1024, 128), BF)
    return call(
        heavy_kernel,
        [((1024, 1536), BF), ((4, 96, H_ALL), BF), ((4, 96, H_ALL), BF)],
        (meta, xg, hw, wall, gvec),
        [
            ((1024, 1536), BF), ((768, 896), BF), ((256, 768), BF), ((128, 768), BF), rows, rows,
            narrow, narrow, narrow, narrow, narrow, ((1024, 384), BF),
            ((1024, 128), F32), ((1024, 128), F32), ((1024, 128), F32),
            rows, ((1024, 512), BF), ((1024, 256), BF), col, col, col,
            ((8, 160, 896), BF), rows, narrow, ((1024, 1536), BF), ((768, H_ALL), BF), ((8, 768), F32),
        ],
        [SMEM, HBM, HBM, HBM, VMEM],
        [HBM, HBM, HBM],
        sems=(4, 9),
        name="heavy",
        us=200,
    )


def body(
    tokens, lengths, routed, cotangent, gain_attn, gain_ffn, router_attn, router_ffn,
    light_q, light_k, light_v, light_o, light_gate, light_up, light_down,
    heavy_q, heavy_k, heavy_v, heavy_o, heavy_gate, heavy_up, heavy_down,
):
    me = lax.axis_index("fsdp")
    vec = jnp.stack([gain_attn, gain_ffn, router_attn, router_ffn], axis=1)
    vec = jnp.pad(vec, ((0, 2), (0, 124)))
    pack, hsend, hd = call(
        prep_kernel,
        [((8, C_ALL), BF), ((16, 8, 896), BF), ((32, 768), BF)],
        (
            light_q, light_k, light_v, light_o, light_gate, light_up, light_down,
            heavy_q, heavy_k, heavy_v, heavy_o, heavy_gate, heavy_up, heavy_down, vec,
        ),
        [((8, 4096), F32)],
        name="prep",
    )
    wall = lax.all_gather(pack, ALL, axis=0, tiled=True)

    hcols = lax.all_to_all(hsend, "fsdp", split_axis=0, concat_axis=0, tiled=True)
    hd = lax.ppermute(hd, ALL, [(d, (d % 8) * 16 + d // 8) for d in range(128)])
    hblock = jnp.concatenate([hcols.reshape(128, 896), jnp.pad(hd, ((0, 0), (0, 128)))], axis=0)

    edges = jnp.arange(17, dtype=jnp.int32) * 512
    bounds = jnp.sum((routed[0][None, :] < edges[:, None]).astype(jnp.int32), axis=1)
    dp = lax.axis_index("dp")
    pair = jnp.where(me < 12, me // 2, 5)
    meta = jnp.concatenate(
        [
            bounds,
            jnp.stack(
                [
                    lengths[0, 0] // 8, 128 * pair, jnp.where(me < 12, me % 2, 2),
                    me, dp // 2, dp % 2, lengths[0, 0],
                ]
            ),
        ]
    )

    def swap(rows):
        return lax.all_to_all(rows, "fsdp", split_axis=0, concat_axis=0, tiled=True)

    slots, st = call(
        slots_kernel,
        [((128, 1536), BF), ((512, 128), BF)],
        (meta, routed, tokens, cotangent),
        in_specs=[SMEM, VMEM, VMEM, VMEM],
        name="slots",
    )
    own, many = call(
        entries_kernel,
        [((64, 1536), BF), ((16, 64, 1536), BF)],
        (meta, swap(slots.reshape(16, 8, 1536)).reshape(128, 1536)),
        in_specs=[SMEM, VMEM],
        name="entries",
    )
    right = [(i, i + 1) for i in range(15)]
    left = [(i + 1, i) for i in range(15)]
    xl = lax.ppermute(tokens[448:512], "fsdp", right)
    xr = lax.ppermute(tokens[0:64], "fsdp", left)

    wall, many, xl, xr, hblock = lax.optimization_barrier((wall, many, xl, xr, hblock))
    hw = lax.all_gather(hblock, "dp", axis=0, tiled=False)
    xg = swap(many).reshape(1024, 1536)
    ffn, cf, light, gvec = run_light_ffn(tokens, cotangent, wall)
    lmeta = jnp.stack([lengths[0, 0], me * 512, jnp.int32(8192)])
    lo, dxg, halo, light, gvec = run_light_attn(
        lmeta, xl, tokens, xr, cotangent, wall, ffn, cf, gvec, light
    )
    rs_light = lax.psum_scatter(light, "dp", scatter_dimension=0, tiled=True)
    parts, keep, give = run_heavy(meta, xg, hw, wall, gvec)
    hr = lax.ppermute(halo[0:64], "fsdp", left)
    hl = lax.ppermute(halo[64:128], "fsdp", right)

    from_core = lax.ppermute(give, "dp", [(i, i ^ 1) for i in range(8)])
    h0, *hz = call(
        core_sum_kernel,
        [((96, H_ALL), BF)] * 4,
        (meta, keep, from_core),
        in_specs=[SMEM, VMEM, VMEM],
        name="core_sum",
    )
    hz = [
        lax.ppermute(block, "dp", [(i, (i + 2 * n) % 8) for i in range(8)])
        for n, block in enumerate(hz, 1)
    ]
    send, g_hd = call(
        spread_heavy_kernel,
        [((128, S_ALL), BF), ((32, 768), BF)],
        (h0, *hz),
        [((128, H_DOWN), BF)],
        out_specs=[HBM, VMEM],
        sems=(1,),
        name="spread_heavy",
    )
    g_hd = lax.ppermute(g_hd, ALL, [((d % 8) * 16 + d // 8, d) for d in range(128)])
    (send,) = call(
        spread_light_kernel,
        [((128, S_ALL), BF)],
        (rs_light, send),
        [((128, S_HEAVY), BF)],
        [VMEM, HBM],
        [HBM],
        sems=(1,),
        name="spread_light",
        aliases={1: 0},
    )
    parts = swap(parts.reshape(16, 64, 1536))
    parts, send, hr, hl, g_hd = lax.optimization_barrier((parts, send, hr, hl, g_hd))
    (send,) = call(
        home_kernel,
        [((128, S_ALL), BF)],
        (meta, parts, own, send),
        [((128, 1536), BF)],
        [SMEM, VMEM, VMEM, HBM],
        [HBM],
        sems=(1,),
        name="home",
        aliases={3: 0},
    )
    got = swap(send.reshape(16, 8, S_ALL))
    six, four, big = ((6, 768), F32), ((6, 1024), F32), ((6, 4096), F32)
    (
        output, grad_tokens, g_q, g_k, g_v, g_o, g_gate, g_up, g_down,
        g_hq, g_hk, g_hv, g_ho, g_hgate, g_hup, g_vec,
    ) = call(
        last_kernel,
        [((512, 768), BF), ((512, 768), BF)] + [six] * 4 + [four, four, ((8, 768), F32)]
        + [six] * 4 + [big, big, ((8, 128), F32)],
        (got, st, lo, dxg, hl, hr),
        name="last",
    )
    return (
        output, grad_tokens,
        g_vec[0:6, 0], g_vec[0:6, 1], g_vec[0:6, 2], g_vec[0:6, 3],
        g_q, g_k, g_v, g_o, g_gate, g_up, g_down,
        g_hq, g_hk, g_hv, g_ho, g_hgate, g_hup, g_hd.astype(F32),
    )


def solution(mesh):
    rows = P(ALL, None)
    flat = P(ALL)
    in_specs = (rows, P("dp", None), P("dp", None), rows) + (flat,) * 4 + (rows,) * 14
    out_specs = (rows, rows) + (flat,) * 4 + (rows,) * 14
    return jax.shard_map(body, mesh=mesh, in_specs=in_specs, out_specs=out_specs, check_vma=False)
```

```python
import jax
import jax.numpy as jnp
from jax import lax
from jax.experimental import pallas as pl
from jax.experimental.pallas import tpu as pltpu
from jax.sharding import PartitionSpec as P

BF = jnp.bfloat16
F32 = jnp.float32
EPS = 1e-6
NEG = -1e30
ALL = ("dp", "fsdp")
CAP = 96
LIGHT_SCALE = 96**-0.5
HEAVY_SCALE = 64**-0.5
PARAMS = pltpu.CompilerParams(vmem_limit_bytes=60 * 1024 * 1024)
SMEM = pl.BlockSpec(memory_space=pltpu.SMEM)
VMEM = pl.BlockSpec(memory_space=pltpu.VMEM)
HBM = pl.BlockSpec(memory_space=pl.ANY)

C_QKVO, C_VEC, C_DOWN, C_HO, C_ALL = 2048, 5120, 5248, 6016, 6784
F_DOWN, F_ALL = 2048, 3072
R_HEAVY, R_HO, R_VEC, R_DOWN, R_ALL = 3072, 3968, 4736, 4864, 5120
S_DOWN, S_REST, S_BACK, S_ALL = 1536, 2304, 6144, 7680

def dot(a, b):
    return jnp.dot(a, b, preferred_element_type=F32)


def dot_nt(a, b):
    return lax.dot_general(a, b, (((1,), (1,)), ((), ())), preferred_element_type=F32)


def dot_tn(a, b):
    return lax.dot_general(a, b, (((0,), (0,)), ((), ())), preferred_element_type=F32)


def pick6(rows, cols, shift=0):
    r = lax.broadcasted_iota(jnp.int32, (rows, cols), 0) + shift
    c = lax.broadcasted_iota(jnp.int32, (rows, cols), 1)
    low = c & 7
    return ((6 * (c >> 3) + low == r) & (low < 6)).astype(F32).astype(BF)


def unpad_rows(ref, out_ref, pick, at=0, width=None):
    width = width or ref.shape[1]
    for b in range(8):
        block = dot(pick, ref[128 * b : 128 * b + 128, at : at + width])
        out_ref[96 * b : 96 * b + 96, at : at + width] = block.astype(BF)


def vector_rows(vec_ref, pick):
    blocks = [dot(pick, vec_ref[128 * b : 128 * b + 128, :]) for b in range(8)]
    return jnp.concatenate(blocks, axis=0).T


class Copies:
    def __init__(self, sems, used=0):
        self.sems, self.used, self.open = sems, used, []

    def start(self, src, dst):
        copy = pltpu.make_async_copy(src, dst, self.sems.at[self.used])
        self.used += 1
        copy.start()
        return copy

    def send(self, src, dst):
        self.open.append(self.start(src, dst))

    def finish(self):
        for copy in self.open:
            copy.wait()


def unit(rows):
    scale = lax.rsqrt(jnp.mean(rows * rows, axis=-1, keepdims=True) + EPS)
    return rows * scale, scale


def gelu_parts(gate):
    c0, c1 = 0.7978845608, 0.044715
    sq = gate * gate
    t = jnp.tanh(gate * (c0 + (c0 * c1) * sq))
    half = 0.5 * (1.0 + t)
    slope = half + (0.5 * gate) * (1.0 - t * t) * (c0 + (3.0 * c0 * c1) * sq)
    return gate * half, slope


def prep_kernel(
    q, k, v, o, gate, up, down, hq, hk, hv, ho, hgate, hup, hdown, ga, gf, ra, rf, pack, hsend, hd, scr, rows
):
    scr[...] = jnp.zeros_like(scr)
    zero128 = jnp.zeros((8, 128), BF)

    def padded(ref):
        cols = ref.shape[1]
        scr[0:6, 0:cols] = ref[...]
        return scr[:, 0:cols].astype(BF)

    gp, upp = padded(gate), padded(up)
    for c in range(4):
        pack[:, 512 * c : 512 * c + 256] = gp[:, 256 * c : 256 * c + 256]
        pack[:, 512 * c + 256 : 512 * c + 512] = upp[:, 256 * c : 256 * c + 256]
    for n, ref in enumerate((q, k, v, o)):
        pack[:, C_QKVO + 768 * n : C_QKVO + 768 * n + 768] = padded(ref)
    rows[...] = jnp.zeros_like(rows)
    for n, ref in enumerate((ga, gf, ra, rf)):
        rows[n : n + 1, 0:6] = ref[...]
    pack[:, C_VEC : C_VEC + 128] = rows[...].T[0:8, :].astype(BF)
    pack[:, C_DOWN : C_DOWN + 768] = down[...].astype(BF)
    pack[:, C_HO : C_HO + 768] = padded(ho)
    wq, wk, wv = padded(hq), padded(hk), padded(hv)
    wg, wu = padded(hgate), padded(hup)
    for j in range(16):
        hsend[j, :, 0:256] = wg[:, 256 * j : 256 * j + 256]
        hsend[j, :, 256:512] = wu[:, 256 * j : 256 * j + 256]
        for n, w in enumerate((wq, wk, wv)):
            p = j // 2
            part = w[:, 128 * p : 128 * p + 128] if j < 12 else zero128
            hsend[j, :, 512 + 128 * n : 640 + 128 * n] = part
    hd[...] = hdown[...].astype(BF)


def light_ffn_kernel(
    x_in, g_in, wall, ffn, cf, light, gvec, vrows, x, g, gu, fin, fin_t, gbuf, gu_pad, down, vec, in_sems, out_sems
):
    def wide(c, at=0):
        return pl.ds(pl.multiple_of(at + 512 * c, 128), 512)

    def loads(c):
        rows = pl.ds(pl.multiple_of(256 * c, 256), 256)
        yield pltpu.make_async_copy(wall.at[:, wide(c)], gu_pad.at[:, wide(c)], in_sems.at[2 * c])
        yield pltpu.make_async_copy(
            wall.at[rows, C_DOWN : C_DOWN + 768], down.at[rows, :], in_sems.at[2 * c + 1]
        )

    def stores(c):
        rows = pl.ds(pl.multiple_of(192 * c, 64), 192)
        yield pltpu.make_async_copy(gbuf.at[:, wide(c)], light.at[:, wide(c)], out_sems.at[2 * c])
        yield pltpu.make_async_copy(
            gbuf.at[rows, 2048:3072], light.at[rows, F_DOWN:F_ALL], out_sems.at[2 * c + 1]
        )

    first = Copies(in_sems, 8)
    got_x = first.start(x_in, x)
    got_vec = first.start(wall.at[:, C_VEC : C_VEC + 128], vec)
    got_g = first.start(g_in, g)
    for c in range(4):
        for copy in loads(c):
            copy.start()
    pick = pick6(96, 128)
    got_x.wait()
    u, _ = unit(x[...].astype(F32))
    got_vec.wait()
    vrows[...] = vector_rows(vec, pick)[0:8, :]
    gain_f = vrows[1:2, :]
    f = (u * gain_f).astype(BF)
    fin[...] = f
    fin_t[...] = f.T
    ffn[...] = jnp.zeros_like(ffn)
    cf[...] = jnp.zeros_like(cf)
    got_g.wait()

    @pl.loop(0, 4)
    def _(c):
        for copy in loads(c):
            copy.wait()
        for b in range(8):
            block = dot(pick, gu_pad[128 * b : 128 * b + 128, wide(c)])
            gu[96 * b : 96 * b + 96, :] = block.astype(BF)
        w = gu[...]
        wd = down[pl.ds(pl.multiple_of(256 * c, 256), 256), :]
        both = dot(fin[...], w)
        act, slope = gelu_parts(both[:, 0:256])
        up = both[:, 256:512]
        hidden = (act * up).astype(BF)
        dh = dot_nt(g[...], wd)
        dgu = jnp.concatenate([(dh * up * slope).astype(BF), (dh * act).astype(BF)], axis=1)
        ffn[...] += dot(hidden, wd)
        cf[...] += dot_nt(dgu, w)
        gbuf[:, wide(c)] = dot(fin_t[...], dgu).astype(BF)
        gd = dot_tn(hidden, g[...]).astype(BF)
        for n in range(2):
            r0 = 128 * n
            at = pl.multiple_of(192 * c + 96 * n, 32)
            gbuf[pl.ds(at, 96), 2048:2816] = gd[r0 : r0 + 96, :]
            for t in range(3):
                gbuf[pl.ds(pl.multiple_of(at + 32 * t, 32), 32), 2816:3072] = gd[
                    r0 + 96 : r0 + 128, 256 * t : 256 * t + 256
                ]
        for copy in stores(c):
            copy.start()

    u, _ = unit(x[...].astype(F32))
    d_f = cf[...]
    gvec[...] = jnp.zeros_like(gvec)
    gvec[1:2, :] = jnp.sum(d_f * u, axis=0, keepdims=True)
    cf[...] = d_f * gain_f
    for c in range(4):
        for copy in stores(c):
            copy.wait()


def light_attn_kernel(
    meta, xl, x_in, xr, g_in, wall, ffn_in, cf_in, gin, vrows,
    lo, dxg, halo, rest, gvec,
    w, xs, a, a_t, qkv, o, do, dqkv, dk, dv, mask, w_pad, g, ffn, cf, lo_buf, d_a, gbuf, in_sems, out_sems,
):
    def wide(n, at=0):
        return pl.ds(pl.multiple_of(at + 768 * n, 128), 768)

    def load(n):
        return pltpu.make_async_copy(wall.at[:, wide(n, C_QKVO)], w_pad.at[:, wide(n)], in_sems.at[n])

    def store(n):
        return pltpu.make_async_copy(gbuf.at[:, wide(n)], rest.at[:, wide(n)], out_sems.at[n])

    loads, stores = Copies(in_sems, 4), Copies(out_sems, 4)
    x = xs.at[64:576, :]
    got_x = loads.start(x_in, x)
    for n in range(4):
        load(n).start()
    got_g = loads.start(g_in, g)
    got_ffn = loads.start(ffn_in, ffn)
    got_cf = loads.start(cf_in, cf)
    pick = pick6(96, 128)
    xs[0:64, :] = xl[...]
    xs[576:640, :] = xr[...]
    first, base, pack_len = meta[0], meta[1], meta[2]
    key = lax.broadcasted_iota(jnp.int32, (256, 256), 0)
    qry = lax.broadcasted_iota(jnp.int32, (256, 256), 1) & 127
    gap = key - qry

    @pl.loop(0, 4)
    def _(b):
        qpos = base + 128 * b + qry
        kpos = base + 128 * b - 64 + key
        ok = (gap >= 0) & (gap <= 128) & ((qpos < first) == (kpos < first))
        ok = ok & (kpos >= 0) & (kpos < pack_len)
        mask[b] = jnp.where(ok, 0.0, NEG)

    dk[...] = jnp.zeros_like(dk)
    dv[...] = jnp.zeros_like(dv)
    dqkv[0:64, 0:768] = jnp.zeros((64, 768), BF)
    dqkv[576:640, 0:768] = jnp.zeros((64, 768), BF)
    got_x.wait()
    u, _ = unit(xs[...].astype(F32))
    gain_a = vrows[0:1, :]
    a[...] = (u * gain_a).astype(BF)

    def unpad(n):
        load(n).wait()
        for b in range(8):
            w[96 * b : 96 * b + 96, wide(n)] = dot(pick, w_pad[128 * b : 128 * b + 128, wide(n)]).astype(BF)

    @pl.loop(0, 3)
    def _(n):
        unpad(n)
        qkv[:, wide(n)] = dot(a[...], w[:, wide(n)]).astype(BF)

    unpad(3)
    got_g.wait()
    do[...] = dot_nt(g[...], w[:, 2304:3072]).astype(BF)

    lane = lax.broadcasted_iota(jnp.int32, (128, 256), 1)

    def pair(b, group, second):
        low = 64 * second
        even = (lane >= low) & (lane < low + 96)
        odd = (lane >= low + 96) & (lane < low + 192)

        def split(t):
            zero = jnp.zeros_like(t)
            return jnp.concatenate([jnp.where(even, t, zero), jnp.where(odd, t, zero)], axis=0)

        def join(t):
            return jnp.where(even, t[0:128], 0.0) + jnp.where(odd, t[128:256], 0.0)

        def win(part):
            return pl.ds(pl.multiple_of(768 * part + 384 * group + 128 * second, 128), 256)

        rq = pl.ds(pl.multiple_of(128 * b, 128), 128)
        rd = pl.ds(pl.multiple_of(128 * b + 64, 64), 128)
        rk = pl.ds(pl.multiple_of(128 * b, 128), 256)
        kw, vw = qkv[rk, win(1)], qkv[rk, win(2)]
        q2, do2 = split(qkv[rd, win(0)]), split(do[rq, win(0)])
        s = dot_nt(kw, q2) * LIGHT_SCALE + mask[b]
        dp = dot_nt(vw, do2)
        e = jnp.exp(s - jnp.max(s, axis=0, keepdims=True))
        p = e * (1.0 / jnp.sum(e, axis=0, keepdims=True))
        pb = p.astype(BF)
        ds = (p * (dp - jnp.sum(p * dp, axis=0, keepdims=True))).astype(BF)
        dk[rk, win(0)] += dot(ds, q2) * LIGHT_SCALE
        dv[rk, win(0)] += dot(pb, do2)
        return join(dot_tn(pb, vw)), join(dot_tn(ds, kw)) * LIGHT_SCALE

    @pl.loop(0, 8)
    def _(i):
        b, group = i >> 1, i & 1
        rq = pl.ds(pl.multiple_of(128 * b, 128), 128)
        rd = pl.ds(pl.multiple_of(128 * b + 64, 64), 128)
        o0, dq0 = pair(b, group, 0)
        o1, dq1 = pair(b, group, 1)

        def tile(n):
            return pl.ds(pl.multiple_of(384 * group + 128 * n, 128), 128)

        for ref, rows, t0, t1 in ((o, rq, o0, o1), (dqkv, rd, dq0, dq1)):
            ref[rows, tile(0)] = t0[:, 0:128].astype(BF)
            ref[rows, tile(1)] = (t0[:, 128:256] + t1[:, 0:128]).astype(BF)
            ref[rows, tile(2)] = t1[:, 128:256].astype(BF)

    got_ffn.wait()
    lo_buf[...] = x[...].astype(F32) + ffn[...] + dot(o[...], w[:, 2304:3072])
    stores.send(lo_buf, lo)
    gbuf[:, 2304:3072] = dot_tn(o[...], g[...]).astype(BF)
    store(3).start()
    dqkv[:, 768:1536] = dk[...].astype(BF)
    dqkv[:, 1536:2304] = dv[...].astype(BF)
    a_t[...] = a[...].T
    d_a[...] = jnp.zeros_like(d_a)

    @pl.loop(0, 3)
    def _(n):
        part = dqkv[:, wide(n)]
        gbuf[:, wide(n)] = dot(a_t[...], part).astype(BF)
        store(n).start()
        d_a[...] += dot_nt(part, w[:, wide(n)])

    u, scale = unit(xs[...].astype(F32))
    c = d_a[...]
    gvec[...] = gin[...]
    gvec[0:1, :] = jnp.sum(c * u, axis=0, keepdims=True)
    c = c * gain_a
    got_cf.wait()

    def norm_back(c, rows):
        ur = u[rows]
        return scale[rows] * (c - ur * jnp.mean(ur * c, axis=-1, keepdims=True))

    own = slice(64, 576)
    dxg[...] = norm_back(c[own] + cf[...], own) + g[...].astype(F32)
    halo[0:64, :] = norm_back(c[0:64], slice(0, 64)).astype(BF)
    halo[64:128, :] = norm_back(c[576:640], slice(576, 640)).astype(BF)
    stores.finish()
    for n in range(4):
        store(n).wait()


def slots_kernel(meta, routed, x, g, slots, st):
    me = meta[20]
    start = meta[me]
    token = lax.broadcasted_iota(jnp.int32, (512, 1024), 0) + 512 * me
    r = jnp.broadcast_to(routed[...], (512, 1024))
    rank = jnp.sum((r < token).astype(F32), axis=1, keepdims=True).astype(jnp.int32) - start
    hit = jnp.sum((r == token).astype(F32), axis=1, keepdims=True)
    row = ((start + rank) & 15) * 8 + (rank >> 4)
    row = jnp.where((hit > 0.5) & (rank < CAP), row, -1)
    lane = lax.broadcasted_iota(jnp.int32, (512, 128), 1)
    onehot = (lane == row).astype(F32).astype(BF)
    st[...] = onehot
    slots[:, 0:768] = dot_tn(onehot, x[...]).astype(BF)
    slots[:, 768:1536] = dot_tn(onehot, g[...]).astype(BF)


def entry_slots(meta):
    p = 16 * lax.broadcasted_iota(jnp.int32, (64, 128), 0) + meta[20]
    source, before = jnp.zeros_like(p), jnp.zeros_like(p)
    for d in range(1, 16):
        source = source + (p >= meta[d]).astype(jnp.int32)
        before = jnp.where(p >= meta[d], meta[d], before)
    rank = p - before
    lane = lax.broadcasted_iota(jnp.int32, (64, 128), 1)
    return ((lane == source * 8 + (rank >> 4)) & (rank < CAP)).astype(F32).astype(BF)


def entries_kernel(meta, got, own, many, kmask):
    entry = entry_of(lax.broadcasted_iota(jnp.int32, (1024, 128), 0))
    bias = jnp.zeros((1024, 128), F32)
    for d in range(16):
        bias = jnp.where((entry >= meta[d] + CAP) & (entry < meta[d + 1]), NEG, bias)
    kmask[:, 0:128] = jnp.where(entry < meta[17], bias, NEG)
    kmask[:, 128:256] = jnp.where(entry < meta[17], NEG, bias)
    rows = dot(entry_slots(meta), got[...]).astype(BF)
    own[...] = rows
    for t in range(16):
        many[t] = rows


def home_kernel(meta, parts, own_in, send_in, send, back, own, sems):
    copies = Copies(sems)
    got_own = copies.start(own_in, own)
    total = parts[0].astype(F32)
    for t in range(1, 16):
        total = total + parts[t].astype(F32)
    got_own.wait()
    u, scale = unit(own[:, 0:768].astype(F32))
    c = total[:, 768:1536]
    dxr = scale * (c - u * jnp.mean(u * c, axis=-1, keepdims=True))
    onehot = entry_slots(meta)
    back[:, 0:768] = dot_tn(onehot, total[:, 0:768].astype(BF)).astype(BF)
    back[:, 768:1536] = dot_tn(onehot, dxr.astype(BF)).astype(BF)
    copies.start(back, send.at[:, S_BACK:S_ALL]).wait()


def entry_of(row):
    return ((row & 63) << 4) + (row >> 6)


def heavy_kernel(
    meta, xg_in, hw_in, wall, kmask_in, gin, vrows, rest_in,
    parts, rest,
    xg, w, wd, wo, ar, fr, q, k, v, o, do, dqkv, dk, dv, kmask, da, dgu, hid, sa, sf, la,
    hw, wo_pad, pbuf, gbuf, gvec, in_sems, out_sems,
):
    loads, stores = Copies(in_sems), Copies(out_sems)
    got_hw = loads.start(hw_in, hw)
    got_wo = loads.start(wall.at[:, C_HO : C_HO + 768], wo_pad)
    got_xg = loads.start(xg_in, xg)
    got_kmask = loads.start(kmask_in, kmask)
    pick = pick6(96, 128)
    gain_a, gain_f, r_a, r_f = (vrows[n : n + 1, :] for n in range(4))
    got_hw.wait()
    for b in range(8):
        w[96 * b : 96 * b + 96, :] = dot(pick, hw[b, 0:128, :]).astype(BF)
        wd[32 * b : 32 * b + 32, :] = hw[b, 128:160, 0:768]
    got_wo.wait()
    low, head = meta[18], meta[19]
    head_row = lax.broadcasted_iota(jnp.int32, (128, 1024), 0) >> 6
    mine = jnp.where(head_row == head, pick6(128, 1024, low).astype(F32), 0.0).astype(BF)
    wo[...] = dot(mine, wo_pad[...]).astype(BF)
    on = (lax.broadcasted_iota(jnp.int32, (256, 128), 1) >> 6) == head
    got_xg.wait()

    @pl.loop(0, 4)
    def _(b):
        rows = pl.ds(pl.multiple_of(256 * b, 256), 256)
        u, _ = unit(xg[rows, 0:768].astype(F32))
        arb, frb = (u * gain_a).astype(BF), (u * gain_f).astype(BF)
        ar[rows, :], fr[rows, :] = arb, frb
        sab = jax.nn.sigmoid(jnp.sum(arb.astype(F32) * r_a, axis=-1, keepdims=True))
        sfb = jax.nn.sigmoid(jnp.sum(frb.astype(F32) * r_f, axis=-1, keepdims=True))
        sa[rows, :], sf[rows, :] = sab, sfb
        qkv = dot(arb, w[:, 512:896])
        q[rows, :] = jnp.where(on, qkv[:, 0:128], 0.0).astype(BF)
        k[rows, :] = qkv[:, 128:256].astype(BF)
        v[rows, :] = jnp.where(on, qkv[:, 256:384], 0.0).astype(BF)
        dab = (sab * xg[rows, 768:1536].astype(F32)).astype(BF)
        da[rows, :] = dab
        do[rows, :] = dot_nt(dab, wo[...]).astype(BF)

    got_kmask.wait()
    n0 = meta[17]
    dk[...] = jnp.zeros_like(dk)
    dv[...] = jnp.zeros_like(dv)

    @pl.loop(0, 4, unroll=2)
    def _(b):
        rows = pl.ds(pl.multiple_of(256 * b, 256), 256)
        first = entry_of(lax.broadcasted_iota(jnp.int32, (1, 128), 1) + 256 * b) < n0
        second = entry_of(lax.broadcasted_iota(jnp.int32, (1, 128), 1) + 256 * b + 128) < n0
        bias = jnp.concatenate(
            [jnp.where(first, kmask[:, 0:128], kmask[:, 128:256]),
             jnp.where(second, kmask[:, 0:128], kmask[:, 128:256])],
            axis=1,
        )
        qb, dob = q[rows, :], do[rows, :]
        s = dot_nt(k[...], qb) * HEAVY_SCALE + bias
        e = jnp.exp(s - jnp.max(s, axis=0, keepdims=True))
        p = e * (1.0 / jnp.sum(e, axis=0, keepdims=True))
        pb = p.astype(BF)
        ob = dot_tn(pb, v[...]).astype(BF)
        o[rows, :] = ob
        la[rows, :] = (1.0 - sa[rows, :]) * jnp.sum(
            ob.astype(F32) * dob.astype(F32), axis=-1, keepdims=True
        )
        dp = dot_nt(v[...], dob)
        ds = (p * (dp - jnp.sum(p * dp, axis=0, keepdims=True))).astype(BF)
        dqkv[rows, 0:128] = jnp.where(on, dot_tn(ds, k[...]) * HEAVY_SCALE, 0.0).astype(BF)
        dk[...] += dot(ds, qb) * HEAVY_SCALE
        dv[...] += dot(pb, dob)

    dqkv[:, 128:256] = dk[...].astype(BF)
    dqkv[:, 256:384] = dv[...].astype(BF)
    gbuf[:, 512:896] = dot_tn(ar[...], dqkv[...]).astype(BF)
    gbuf[:, R_HO - R_HEAVY : R_VEC - R_HEAVY] = jnp.zeros((768, 768), BF)
    gbuf[pl.ds(pl.multiple_of(low, 128), 128), R_HO - R_HEAVY : R_VEC - R_HEAVY] = dot_tn(o[...], da[...]).astype(BF)
    at = R_HEAVY
    stores.send(gbuf.at[:, 512 : R_VEC - at], rest.at[:, at + 512 : R_VEC])
    gvec[...] = gin[...]

    def send_parts(b):
        rows = pl.ds(pl.multiple_of(256 * b, 256), 256)
        return pltpu.make_async_copy(pbuf.at[rows, :], parts.at[rows, :], out_sems.at[3 + b])

    @pl.loop(0, 4, unroll=2)
    def _(b):
        rows = pl.ds(pl.multiple_of(256 * b, 256), 256)
        frb = fr[rows, :]
        sfb = sf[rows, :]
        dfb = (sfb * xg[rows, 768:1536].astype(F32)).astype(BF)
        both = dot(frb, w[:, 0:512])
        act, slope = gelu_parts(both[:, 0:256])
        up = both[:, 256:512]
        hidden = (act * up).astype(BF)
        hid[rows, :] = hidden
        dh = dot_nt(dfb, wd[...])
        lfb = (1.0 - sfb) * jnp.sum(hidden.astype(F32) * dh, axis=-1, keepdims=True)
        dgub = jnp.concatenate([(dh * up * slope).astype(BF), (dh * act).astype(BF)], axis=1)
        dgu[rows, :] = dgub
        y = sa[rows, :] * dot(o[rows, :], wo[...]) + sfb * dot(hidden, wd[...])
        lab = la[rows, :]
        d_f = dot_nt(dgub, w[:, 0:512]) + lfb * r_f
        d_a = dot_nt(dqkv[rows, :], w[:, 512:896]) + lab * r_a
        u, _ = unit(xg[rows, 0:768].astype(F32))
        gvec[0:1, :] += jnp.sum(d_a * u, axis=0, keepdims=True)
        gvec[1:2, :] += jnp.sum(d_f * u, axis=0, keepdims=True)
        gvec[2:3, :] += jnp.sum(lab * ar[rows, :].astype(F32), axis=0, keepdims=True)
        gvec[3:4, :] += jnp.sum(lfb * frb.astype(F32), axis=0, keepdims=True)
        da[rows, :] = dfb
        pbuf[rows, 0:768] = y.astype(BF)
        pbuf[rows, 768:1536] = (d_a * gain_a + d_f * gain_f).astype(BF)
        send_parts(b).start()

    gbuf[:, 0:512] = dot_tn(fr[...], dgu[...]).astype(BF)
    stores.send(gbuf.at[:, 0:512], rest.at[:, at : at + 512])
    vecs = jnp.concatenate([gvec[...], jnp.zeros((120, 768), F32)], axis=0)
    gbuf[:, R_VEC - R_HEAVY : R_DOWN - R_HEAVY] = vecs.T.astype(BF)
    gd = dot_tn(hid[...], da[...]).astype(BF)
    for r in range(8):
        for t in range(3):
            gbuf[96 * r + 32 * t : 96 * r + 32 * t + 32, R_DOWN - R_HEAVY : R_ALL - R_HEAVY] = gd[
                32 * r : 32 * r + 32, 256 * t : 256 * t + 256
            ]
    stores.send(gbuf.at[:, R_VEC - at : R_ALL - at], rest.at[:, R_VEC:R_ALL])
    stores.finish()
    for b in range(4):
        send_parts(b).wait()


def tokens_kernel(got, st, lo, dxg, hl, hr, out, grad):
    back = dot(st[...], got[:, :, S_BACK:S_ALL].reshape(128, 1536))
    out[...] = (lo[...] + back[:, 0:768]).astype(BF)
    dx = dxg[...] + back[:, 768:1536]
    grad[0:64, :] = (dx[0:64, :] + hl[...].astype(F32)).astype(BF)
    grad[64:448, :] = dx[64:448, :].astype(BF)
    grad[448:512, :] = (dx[448:512, :] + hr[...].astype(F32)).astype(BF)


def tail_rows(block, low):
    last = jnp.concatenate([block[32 * t : 32 * t + 32, low + 768 : low + 1024] for t in range(3)], axis=1)
    return jnp.concatenate([block[:, low : low + 768], last], axis=0)


def owner_rows(r, cols):
    quarter = cols // 4
    row = lax.broadcasted_iota(jnp.int32, (128, 96), 0)
    col = lax.broadcasted_iota(jnp.int32, (128, 96), 1)
    device, low = 6 * (row >> 3), row & 7
    main = ((low < 6) & (col == device + low)).astype(F32).astype(BF)
    tail = r[:, 3 * quarter : cols]
    pieces = []
    for t in range(3):
        extra = ((low >= 6) & (col == device + 3 * (low - 6) + t)).astype(F32).astype(BF)
        pieces.append((dot(main, r[:, quarter * t : quarter * t + quarter]) + dot(extra, tail)).astype(BF))
    return jnp.concatenate(pieces, axis=1)


def tail_of(block):
    cols = block.shape[1] // 3
    return jnp.concatenate(
        [block[6 + n : 7 + n, cols * t : cols * t + cols] for n in range(2) for t in range(3)], axis=0
    )


def spread_ffn_kernel(r, send, rows, sems):
    rows[:, 0:S_DOWN] = owner_rows(r, F_DOWN)
    rows[:, S_DOWN:S_REST] = tail_rows(r[...], F_DOWN)
    Copies(sems).start(rows, send.at[:, 0:S_REST]).wait()


def spread_rest_kernel(r, send_in, send, hd, rows, sems):
    rows[...] = owner_rows(r, R_ALL)
    copy = Copies(sems).start(rows, send.at[:, S_REST:S_BACK])
    hd[...] = jnp.concatenate([r[32 * t : 32 * t + 32, R_DOWN:R_ALL] for t in range(3)], axis=1)
    copy.wait()


def sum_parts(got, a, b):
    t = got[0, :, a:b].astype(F32)
    for d in range(1, 16):
        t = t + got[d, :, a:b].astype(F32)
    return t


def sum_ffn_kernel(got, gate, up, down):
    both = sum_parts(got, 0, S_DOWN)
    for c in range(3):
        gate[:, 256 * c : 256 * c + 256] = both[0:6, 512 * c : 512 * c + 256]
        up[:, 256 * c : 256 * c + 256] = both[0:6, 512 * c + 256 : 512 * c + 512]
    both = tail_of(both)
    gate[:, 768:1024] = both[:, 0:256]
    up[:, 768:1024] = both[:, 256:512]
    down[...] = sum_parts(got, S_DOWN, S_REST)


def sum_rest_kernel(got, q, k, v, o, hq, hk, hv, ho, hgate, hup, vecs):
    total = sum_parts(got, S_REST, S_BACK)
    for n, ref in enumerate((q, k, v, o)):
        ref[...] = total[0:6, 768 * n : 768 * n + 768]
    rest = tail_of(total)
    ho[...] = rest[:, 128:896]
    rows = jnp.concatenate([rest[:, 896:1024], jnp.zeros((122, 128), F32)], axis=0).T
    for n, ref in enumerate(vecs):
        ref[...] = rows[n : n + 1, 0:6]
    at = S_REST + R_HEAVY
    for j in range(16):
        hgate[:, 256 * j : 256 * j + 256] = got[j, :, at : at + 256].astype(F32)[0:6]
        hup[:, 256 * j : 256 * j + 256] = got[j, :, at + 256 : at + 512].astype(F32)[0:6]
    at = at + 512
    for p in range(6):
        two = [got[2 * p + n, :, S_REST:S_BACK].astype(F32) for n in range(2)]
        pair = two[0][:, R_HEAVY + 512 : R_HEAVY + 768] + two[1][:, R_HEAVY + 512 : R_HEAVY + 768]
        hq[:, 128 * p : 128 * p + 128] = pair[0:6, 0:128]
        hk[:, 128 * p : 128 * p + 128] = pair[0:6, 128:256]
        hv[:, 128 * p : 128 * p + 128] = tail_of(two[0] + two[1])[:, 0:128]


def last_kernel(
    got, st, lo, dxg, hl, hr,
    out, grad, q, k, v, o, gate, up, down, hq, hk, hv, ho, hgate, hup, *vecs,
):
    tokens_kernel(got, st, lo, dxg, hl, hr, out, grad)
    sum_ffn_kernel(got, gate, up, down)
    sum_rest_kernel(got, q, k, v, o, hq, hk, hv, ho, hgate, hup, vecs)


def call(kernel, outs, args, scratch=(), in_specs=None, out_specs=None, sems=(), name=None, us=0.05, aliases={}):
    return pl.pallas_call(
        kernel,
        out_shape=[jax.ShapeDtypeStruct(s, t) for s, t in outs],
        in_specs=in_specs or [VMEM] * len(args),
        out_specs=out_specs or [VMEM] * len(outs),
        scratch_shapes=[pltpu.VMEM(s, t) for s, t in scratch]
        + [pltpu.SemaphoreType.DMA((n,)) for n in sems],
        compiler_params=PARAMS,
        cost_estimate=pl.CostEstimate(
            flops=int(us * 1.0e9), bytes_accessed=int(us * 3.0e6), transcendentals=0
        ),
        input_output_aliases=aliases,
        name=name,
    )(*args)


def run_light_ffn(tokens, cotangent, wall):
    return call(
        light_ffn_kernel,
        [((512, 768), F32), ((512, 768), F32), ((768, F_ALL), BF), ((8, 768), F32), ((8, 768), F32)],
        (tokens, cotangent, wall),
        [
            ((512, 768), BF), ((512, 768), BF),
            ((768, 512), BF), ((512, 768), BF), ((768, 512), BF), ((768, 3072), BF),
            ((1024, 2048), BF), ((1024, 768), BF), ((1024, 128), BF),
        ],
        [HBM, HBM, HBM],
        [VMEM, VMEM, HBM, VMEM, VMEM],
        sems=(11, 8),
        name="light_ffn",
        us=200,
    )


def run_light_attn(meta, xl, tokens, xr, cotangent, wall, ffn, cf, gvec, vrows):
    return call(
        light_attn_kernel,
        [
            ((512, 768), F32), ((512, 768), F32), ((128, 768), BF), ((768, R_ALL), BF), ((8, 768), F32),
        ],
        (meta, xl, tokens, xr, cotangent, wall, ffn, cf, gvec, vrows),
        [
            ((768, 3072), BF), ((640, 768), BF), ((640, 768), BF), ((768, 640), BF), ((640, 2304), BF),
            ((512, 768), BF), ((512, 768), BF), ((640, 2304), BF),
            ((640, 768), F32), ((640, 768), F32), ((4, 256, 256), F32),
            ((1024, 3072), BF), ((512, 768), BF), ((512, 768), F32), ((512, 768), F32),
            ((512, 768), F32), ((640, 768), F32), ((768, 3072), BF),
        ],
        [SMEM, VMEM, HBM, VMEM, HBM] + [HBM] * 3 + [VMEM, VMEM],
        [HBM, VMEM, VMEM, HBM, VMEM],
        sems=(8, 5),
        name="light_attn",
        us=2,
    )


def run_heavy(meta, xg, hw, wall, kmask, gvec, vrows, rest):
    col = ((1024, 1), F32)
    rows, narrow = ((1024, 768), BF), ((1024, 128), BF)
    return call(
        heavy_kernel,
        [((1024, 1536), BF), ((768, R_ALL), BF)],
        (meta, xg, hw, wall, kmask, gvec, vrows, rest),
        [
            ((1024, 1536), BF), ((768, 896), BF), ((256, 768), BF), ((128, 768), BF), rows, rows,
            narrow, narrow, narrow, narrow, narrow, ((1024, 384), BF),
            ((1024, 128), F32), ((1024, 128), F32), ((1024, 256), F32),
            rows, ((1024, 512), BF), ((1024, 256), BF), col, col, col,
            ((8, 160, 896), BF), rows, ((1024, 1536), BF), ((768, R_ALL - R_HEAVY), BF), ((8, 768), F32),
        ],
        [SMEM, HBM, HBM, HBM, HBM, VMEM, VMEM, HBM],
        [HBM, HBM],
        sems=(4, 7),
        aliases={7: 1},
        name="heavy",
        us=200,
    )


def body(
    tokens, lengths, routed, cotangent, gain_attn, gain_ffn, router_attn, router_ffn,
    light_q, light_k, light_v, light_o, light_gate, light_up, light_down,
    heavy_q, heavy_k, heavy_v, heavy_o, heavy_gate, heavy_up, heavy_down,
):
    me = lax.axis_index("fsdp")
    vectors = [v.reshape(1, 6) for v in (gain_attn, gain_ffn, router_attn, router_ffn)]
    pack, hsend, hd = call(
        prep_kernel,
        [((8, C_ALL), BF), ((16, 8, 896), BF), ((32, 768), BF)],
        (
            light_q, light_k, light_v, light_o, light_gate, light_up, light_down,
            heavy_q, heavy_k, heavy_v, heavy_o, heavy_gate, heavy_up, heavy_down, *vectors,
        ),
        [((8, 4096), F32), ((128, 128), F32)],
        name="prep",
    )
    wall = lax.all_gather(pack, ALL, axis=0, tiled=True)

    hcols = lax.all_to_all(hsend, "fsdp", split_axis=0, concat_axis=0, tiled=True)
    hd = lax.ppermute(hd, ALL, [(d, (d % 8) * 16 + d // 8) for d in range(128)])
    hblock = jnp.concatenate([hcols.reshape(128, 896), jnp.pad(hd, ((0, 0), (0, 128)))], axis=0)

    edges = jnp.arange(17, dtype=jnp.int32) * 512
    bounds = jnp.sum((routed[0][None, :] < edges[:, None]).astype(jnp.int32), axis=1)
    dp = lax.axis_index("dp")
    pair = jnp.where(me < 12, me // 2, 5)
    meta = jnp.concatenate(
        [
            bounds,
            jnp.stack(
                [
                    lengths[0, 0] // 8, 128 * pair, jnp.where(me < 12, me % 2, 2),
                    me, dp // 2, dp % 2, lengths[0, 0],
                ]
            ),
        ]
    )

    def swap(rows):
        return lax.all_to_all(rows, "fsdp", split_axis=0, concat_axis=0, tiled=True)

    slots, st = call(
        slots_kernel,
        [((128, 1536), BF), ((512, 128), BF)],
        (meta, routed, tokens, cotangent),
        in_specs=[SMEM, VMEM, VMEM, VMEM],
        name="slots",
    )
    own, many, kmask = call(
        entries_kernel,
        [((64, 1536), BF), ((16, 64, 1536), BF), ((1024, 256), F32)],
        (meta, swap(slots.reshape(16, 8, 1536)).reshape(128, 1536)),
        in_specs=[SMEM, VMEM],
        name="entries",
    )
    right = [(i, i + 1) for i in range(15)]
    left = [(i + 1, i) for i in range(15)]
    xl = lax.ppermute(tokens[448:512], "fsdp", right)
    xr = lax.ppermute(tokens[0:64], "fsdp", left)

    wall, many, xl, xr, hblock = lax.optimization_barrier((wall, many, xl, xr, hblock))
    hw = lax.all_gather(hblock, "dp", axis=0, tiled=False)
    xg = swap(many).reshape(1024, 1536)
    ffn, cf, grad_ffn, gvec, vrows = run_light_ffn(tokens, cotangent, wall)
    rs_ffn = lax.psum_scatter(grad_ffn, "dp", scatter_dimension=0, tiled=True)
    lmeta = jnp.stack([lengths[0, 0], me * 512, jnp.int32(8192)])
    lo, dxg, halo, rest, gvec = run_light_attn(
        lmeta, xl, tokens, xr, cotangent, wall, ffn, cf, gvec, vrows
    )
    parts, rest = run_heavy(meta, xg, hw, wall, kmask, gvec, vrows, rest)
    rs_rest = lax.psum_scatter(rest, "dp", scatter_dimension=0, tiled=True)
    hr = lax.ppermute(halo[0:64], "fsdp", left)
    hl = lax.ppermute(halo[64:128], "fsdp", right)
    (send,) = call(
        spread_ffn_kernel,
        [((128, S_ALL), BF)],
        (rs_ffn,),
        [((128, S_REST), BF)],
        out_specs=[HBM],
        sems=(1,),
        name="spread_ffn",
    )
    parts = swap(parts.reshape(16, 64, 1536))
    parts, send, hr, hl = lax.optimization_barrier((parts, send, hr, hl))
    (send,) = call(
        home_kernel,
        [((128, S_ALL), BF)],
        (meta, parts, own, send),
        [((128, 1536), BF), ((64, 1536), BF)],
        [SMEM, VMEM, HBM, HBM],
        [HBM],
        sems=(2,),
        name="home",
        aliases={3: 0},
    )
    send, g_hd = call(
        spread_rest_kernel,
        [((128, S_ALL), BF), ((32, 768), BF)],
        (rs_rest, send),
        [((128, S_BACK - S_REST), BF)],
        [VMEM, HBM],
        [HBM, VMEM],
        sems=(1,),
        name="spread_rest",
        aliases={1: 0},
    )
    g_hd = lax.ppermute(g_hd, ALL, [((d % 8) * 16 + d // 8, d) for d in range(128)])
    got = swap(send.reshape(16, 8, S_ALL))
    six, four, big = ((6, 768), F32), ((6, 1024), F32), ((6, 4096), F32)
    (
        output, grad_tokens, g_q, g_k, g_v, g_o, g_gate, g_up, g_down,
        g_hq, g_hk, g_hv, g_ho, g_hgate, g_hup, *g_vecs,
    ) = call(
        last_kernel,
        [((512, 768), BF), ((512, 768), BF)] + [six] * 4 + [four, four, ((8, 768), F32)]
        + [six] * 4 + [big, big] + [((1, 6), F32)] * 4,
        (got, st, lo, dxg, hl, hr),
        name="last",
    )
    return (
        output, grad_tokens,
        *[v.reshape(6) for v in g_vecs],
        g_q, g_k, g_v, g_o, g_gate, g_up, g_down,
        g_hq, g_hk, g_hv, g_ho, g_hgate, g_hup, g_hd.astype(F32),
    )


def solution(mesh):
    rows = P(ALL, None)
    flat = P(ALL)
    in_specs = (rows, P("dp", None), P("dp", None), rows) + (flat,) * 4 + (rows,) * 14
    out_specs = (rows, rows) + (flat,) * 4 + (rows,) * 14
    return jax.shard_map(body, mesh=mesh, in_specs=in_specs, out_specs=out_specs, check_vma=False)
```

```python
import jax
import jax.numpy as jnp
from jax import lax
from jax.experimental import pallas as pl
from jax.experimental.pallas import tpu as pltpu
from jax.sharding import PartitionSpec as P

BF = jnp.bfloat16
F32 = jnp.float32
EPS = 1e-6
NEG = -1e30
ALL = ("dp", "fsdp")
CAP = 96
LIGHT_SCALE = 96**-0.5
HEAVY_SCALE = 64**-0.5
PARAMS = pltpu.CompilerParams(vmem_limit_bytes=60 * 1024 * 1024)
SMEM = pl.BlockSpec(memory_space=pltpu.SMEM)
VMEM = pl.BlockSpec(memory_space=pltpu.VMEM)
HBM = pl.BlockSpec(memory_space=pl.ANY)

C_QKVO, C_VEC, C_DOWN, C_ALL = 2048, 5120, 5248, 5504
F_DOWN, F_ALL = 2048, 3072
R_HEAVY, R_HO, R_VEC, R_DOWN, R_ALL = 3072, 3968, 4736, 4864, 5120
S_DOWN, S_REST, S_BACK, S_ALL = 1536, 2304, 6144, 7680

def dot(a, b):
    return jnp.dot(a, b, preferred_element_type=F32)


def dot_nt(a, b):
    return lax.dot_general(a, b, (((1,), (1,)), ((), ())), preferred_element_type=F32)


def dot_tn(a, b):
    return lax.dot_general(a, b, (((0,), (0,)), ((), ())), preferred_element_type=F32)


def pick6(rows, cols, shift=0):
    r = lax.broadcasted_iota(jnp.int32, (rows, cols), 0) + shift
    c = lax.broadcasted_iota(jnp.int32, (rows, cols), 1)
    low = c & 7
    return ((6 * (c >> 3) + low == r) & (low < 6)).astype(F32).astype(BF)


def unpad_rows(ref, out_ref, pick, at=0, width=None):
    width = width or ref.shape[1]
    for b in range(8):
        block = dot(pick, ref[128 * b : 128 * b + 128, at : at + width])
        out_ref[96 * b : 96 * b + 96, at : at + width] = block.astype(BF)


def vector_rows(vec_ref, pick):
    blocks = [dot(pick, vec_ref[128 * b : 128 * b + 128, :]) for b in range(8)]
    return jnp.concatenate(blocks, axis=0).T


class Copies:
    def __init__(self, sems, used=0):
        self.sems, self.used, self.open = sems, used, []

    def start(self, src, dst):
        copy = pltpu.make_async_copy(src, dst, self.sems.at[self.used])
        self.used += 1
        copy.start()
        return copy

    def send(self, src, dst):
        self.open.append(self.start(src, dst))

    def finish(self):
        for copy in self.open:
            copy.wait()


def unit(rows):
    scale = lax.rsqrt(jnp.mean(rows * rows, axis=-1, keepdims=True) + EPS)
    return rows * scale, scale


def gelu_parts(gate):
    c0, c1 = 0.7978845608, 0.044715
    sq = gate * gate
    t = jnp.tanh(gate * (c0 + (c0 * c1) * sq))
    half = 0.5 * (1.0 + t)
    slope = half + (0.5 * gate) * (1.0 - t * t) * (c0 + (3.0 * c0 * c1) * sq)
    return gate * half, slope


def prep_kernel(
    q, k, v, o, gate, up, down, hq, hk, hv, ho, hgate, hup, hdown, ga, gf, ra, rf, pack, hsend, hd, scr, rows, wide
):
    scr[...] = jnp.zeros_like(scr)
    zero128 = jnp.zeros((8, 128), BF)
    for c in range(4):
        cols = slice(256 * c, 256 * c + 256)
        scr[0:6, 512 * c : 512 * c + 256] = gate[:, cols]
        scr[0:6, 512 * c + 256 : 512 * c + 512] = up[:, cols]
    for n, ref in enumerate((q, k, v, o)):
        scr[0:6, C_QKVO + 768 * n : C_QKVO + 768 * n + 768] = ref[...]
    for a in range(2):
        for b in range(4):
            scr[6 + a : 7 + a, 512 * b : 512 * b + 512] = down[4 * a + b : 4 * a + b + 1, 0:512]
        for b in range(3):
            at = C_QKVO + 768 * b
            scr[6 + a : 7 + a, at : at + 768] = ho[3 * a + b : 3 * a + b + 1, :]
    scr[:, C_DOWN:C_ALL] = down[:, 512:768]
    rows[...] = jnp.zeros_like(rows)
    for n, ref in enumerate((ga, gf, ra, rf)):
        rows[n : n + 1, 0:6] = ref[...]
    scr[:, C_VEC : C_VEC + 128] = rows[...].T[0:8, :]
    pack[...] = scr[...].astype(BF)
    wide[...] = jnp.zeros_like(wide)

    def padded(ref):
        cols = ref.shape[1]
        wide[0:6, 0:cols] = ref[...]
        return wide[:, 0:cols].astype(BF)

    wq, wk, wv = padded(hq), padded(hk), padded(hv)
    wg, wu = padded(hgate), padded(hup)
    for j in range(16):
        hsend[j, :, 0:256] = wg[:, 256 * j : 256 * j + 256]
        hsend[j, :, 256:512] = wu[:, 256 * j : 256 * j + 256]
        for n, w in enumerate((wq, wk, wv)):
            p = j // 2
            part = w[:, 128 * p : 128 * p + 128] if j < 12 else zero128
            hsend[j, :, 512 + 128 * n : 640 + 128 * n] = part
    hd[...] = hdown[...].astype(BF)


def light_ffn_kernel(
    x_in, g_in, wall, ffn, cf, light, gvec, vrows, x, g, gu, fin, fin_t, gbuf, gu_pad, down, vec, wd, in_sems, out_sems
):
    def wide(c, at=0):
        return pl.ds(pl.multiple_of(at + 512 * c, 128), 512)

    def loads(c):
        rows = pl.ds(pl.multiple_of(256 * c, 256), 256)
        yield pltpu.make_async_copy(wall.at[:, wide(c)], gu_pad.at[:, wide(c)], in_sems.at[2 * c])
        yield pltpu.make_async_copy(
            wall.at[rows, C_DOWN:C_ALL], down.at[rows, :], in_sems.at[2 * c + 1]
        )

    def stores(c):
        rows = pl.ds(pl.multiple_of(192 * c, 64), 192)
        yield pltpu.make_async_copy(gbuf.at[:, wide(c)], light.at[:, wide(c)], out_sems.at[2 * c])
        yield pltpu.make_async_copy(
            gbuf.at[rows, 2048:3072], light.at[rows, F_DOWN:F_ALL], out_sems.at[2 * c + 1]
        )

    first = Copies(in_sems, 8)
    got_x = first.start(x_in, x)
    got_vec = first.start(wall.at[:, C_VEC : C_VEC + 128], vec)
    got_g = first.start(g_in, g)
    for c in range(4):
        for copy in loads(c):
            copy.start()
    pick = pick6(96, 128)
    got_x.wait()
    u, _ = unit(x[...].astype(F32))
    got_vec.wait()
    vrows[...] = vector_rows(vec, pick)[0:8, :]
    gain_f = vrows[1:2, :]
    f = (u * gain_f).astype(BF)
    fin[...] = f
    fin_t[...] = f.T
    ffn[...] = jnp.zeros_like(ffn)
    cf[...] = jnp.zeros_like(cf)
    got_g.wait()

    for c in range(4):
        for copy in loads(c):
            copy.wait()
    out_row = lax.broadcasted_iota(jnp.int32, (256, 256), 0)
    in_row = lax.broadcasted_iota(jnp.int32, (256, 256), 1)
    spare = (out_row & ~7) + 6 + ((out_row >> 2) & 1) == in_row
    spread = [(spare & ((out_row & 3) == b)).astype(F32).astype(BF) for b in range(4)]

    @pl.loop(0, 4)
    def _(c):
        for b in range(8):
            block = dot(pick, gu_pad[128 * b : 128 * b + 128, wide(c)])
            gu[96 * b : 96 * b + 96, :] = block.astype(BF)
        w = gu[...]
        rows = pl.ds(pl.multiple_of(256 * c, 256), 256)
        left = dot(spread[0], gu_pad[rows, 0:512])
        for b in range(1, 4):
            left = left + dot(spread[b], gu_pad[rows, 512 * b : 512 * b + 512])
        wd[:, 0:512] = left.astype(BF)
        wd[:, 512:768] = down[rows, :]
        both = dot(fin[...], w)
        act, slope = gelu_parts(both[:, 0:256])
        up = both[:, 256:512]
        hidden = (act * up).astype(BF)
        dh = dot_nt(g[...], wd[...])
        dgu = jnp.concatenate([(dh * up * slope).astype(BF), (dh * act).astype(BF)], axis=1)
        ffn[...] += dot(hidden, wd[...])
        cf[...] += dot_nt(dgu, w)
        gbuf[:, wide(c)] = dot(fin_t[...], dgu).astype(BF)
        gd = dot_tn(hidden, g[...]).astype(BF)
        for n in range(2):
            r0 = 128 * n
            at = pl.multiple_of(192 * c + 96 * n, 32)
            gbuf[pl.ds(at, 96), 2048:2816] = gd[r0 : r0 + 96, :]
            for t in range(3):
                gbuf[pl.ds(pl.multiple_of(at + 32 * t, 32), 32), 2816:3072] = gd[
                    r0 + 96 : r0 + 128, 256 * t : 256 * t + 256
                ]
        for copy in stores(c):
            copy.start()

    u, _ = unit(x[...].astype(F32))
    d_f = cf[...]
    gvec[...] = jnp.zeros_like(gvec)
    gvec[1:2, :] = jnp.sum(d_f * u, axis=0, keepdims=True)
    cf[...] = d_f * gain_f
    for c in range(4):
        for copy in stores(c):
            copy.wait()


def light_attn_kernel(
    meta, xl, x_in, xr, g_in, wall, ffn_in, cf_in, gin, vrows,
    lo, dxg, halo, rest, gvec, heavy_wo,
    w, xs, a, a_t, qkv, o, do, dqkv, dk, dv, mask, w_pad, g, ffn, cf, lo_buf, d_a, gbuf, in_sems, out_sems,
):
    def wide(n, at=0):
        return pl.ds(pl.multiple_of(at + 768 * n, 128), 768)

    def load(n):
        return pltpu.make_async_copy(wall.at[:, wide(n, C_QKVO)], w_pad.at[:, wide(n)], in_sems.at[n])

    def store(n):
        return pltpu.make_async_copy(gbuf.at[:, wide(n)], rest.at[:, wide(n)], out_sems.at[n])

    loads, stores = Copies(in_sems, 4), Copies(out_sems, 4)
    x = xs.at[64:576, :]
    got_x = loads.start(x_in, x)
    for n in range(4):
        load(n).start()
    got_g = loads.start(g_in, g)
    got_ffn = loads.start(ffn_in, ffn)
    got_cf = loads.start(cf_in, cf)
    pick = pick6(96, 128)
    xs[0:64, :] = xl[...]
    xs[576:640, :] = xr[...]
    first, base, pack_len = meta[0], meta[1], meta[2]
    key = lax.broadcasted_iota(jnp.int32, (256, 256), 0)
    qry = lax.broadcasted_iota(jnp.int32, (256, 256), 1) & 127
    gap = key - qry

    @pl.loop(0, 4)
    def _(b):
        qpos = base + 128 * b + qry
        kpos = base + 128 * b - 64 + key
        ok = (gap >= 0) & (gap <= 128) & ((qpos < first) == (kpos < first))
        ok = ok & (kpos >= 0) & (kpos < pack_len)
        mask[b] = jnp.where(ok, 0.0, NEG)

    dk[...] = jnp.zeros_like(dk)
    dv[...] = jnp.zeros_like(dv)
    dqkv[0:64, 0:768] = jnp.zeros((64, 768), BF)
    dqkv[576:640, 0:768] = jnp.zeros((64, 768), BF)
    got_x.wait()
    u, _ = unit(xs[...].astype(F32))
    gain_a = vrows[0:1, :]
    a[...] = (u * gain_a).astype(BF)

    def unpad(n):
        load(n).wait()
        for b in range(8):
            w[96 * b : 96 * b + 96, wide(n)] = dot(pick, w_pad[128 * b : 128 * b + 128, wide(n)]).astype(BF)

    @pl.loop(0, 3)
    def _(n):
        unpad(n)
        qkv[:, wide(n)] = dot(a[...], w[:, wide(n)]).astype(BF)

    unpad(3)
    got_g.wait()
    do[...] = dot_nt(g[...], w[:, 2304:3072]).astype(BF)

    row = lax.broadcasted_iota(jnp.int32, (128, 1024), 0)
    col = lax.broadcasted_iota(jnp.int32, (128, 1024), 1)
    entry = 6 * (col >> 3) + 3 * ((col & 7) - 6)
    keep = ((col & 7) >= 6) & ((row >> 6) == meta[4])
    wo = jnp.zeros((128, 768), F32)
    for b in range(3):
        take = (keep & (entry + b == row + meta[3])).astype(F32).astype(BF)
        wo = wo + dot(take, w_pad[:, 768 * b : 768 * b + 768])
    heavy_wo[...] = wo.astype(BF)

    lane = lax.broadcasted_iota(jnp.int32, (128, 256), 1)

    def pair(b, group, second):
        low = 64 * second
        even = (lane >= low) & (lane < low + 96)
        odd = (lane >= low + 96) & (lane < low + 192)

        def split(t):
            zero = jnp.zeros_like(t)
            return jnp.concatenate([jnp.where(even, t, zero), jnp.where(odd, t, zero)], axis=0)

        def join(t):
            return jnp.where(even, t[0:128], 0.0) + jnp.where(odd, t[128:256], 0.0)

        def win(part):
            return pl.ds(pl.multiple_of(768 * part + 384 * group + 128 * second, 128), 256)

        rq = pl.ds(pl.multiple_of(128 * b, 128), 128)
        rd = pl.ds(pl.multiple_of(128 * b + 64, 64), 128)
        rk = pl.ds(pl.multiple_of(128 * b, 128), 256)
        kw, vw = qkv[rk, win(1)], qkv[rk, win(2)]
        q2, do2 = split(qkv[rd, win(0)]), split(do[rq, win(0)])
        s = dot_nt(kw, q2) * LIGHT_SCALE + mask[b]
        dp = dot_nt(vw, do2)
        e = jnp.exp(s - jnp.max(s, axis=0, keepdims=True))
        p = e * (1.0 / jnp.sum(e, axis=0, keepdims=True))
        pb = p.astype(BF)
        ds = (p * (dp - jnp.sum(p * dp, axis=0, keepdims=True))).astype(BF)
        dk[rk, win(0)] += dot(ds, q2) * LIGHT_SCALE
        dv[rk, win(0)] += dot(pb, do2)
        return join(dot_tn(pb, vw)), join(dot_tn(ds, kw)) * LIGHT_SCALE

    @pl.loop(0, 8)
    def _(i):
        b, group = i >> 1, i & 1
        rq = pl.ds(pl.multiple_of(128 * b, 128), 128)
        rd = pl.ds(pl.multiple_of(128 * b + 64, 64), 128)
        o0, dq0 = pair(b, group, 0)
        o1, dq1 = pair(b, group, 1)

        def tile(n):
            return pl.ds(pl.multiple_of(384 * group + 128 * n, 128), 128)

        for ref, rows, t0, t1 in ((o, rq, o0, o1), (dqkv, rd, dq0, dq1)):
            ref[rows, tile(0)] = t0[:, 0:128].astype(BF)
            ref[rows, tile(1)] = (t0[:, 128:256] + t1[:, 0:128]).astype(BF)
            ref[rows, tile(2)] = t1[:, 128:256].astype(BF)

    got_ffn.wait()
    lo_buf[...] = x[...].astype(F32) + ffn[...] + dot(o[...], w[:, 2304:3072])
    stores.send(lo_buf, lo)
    gbuf[:, 2304:3072] = dot_tn(o[...], g[...]).astype(BF)
    store(3).start()
    dqkv[:, 768:1536] = dk[...].astype(BF)
    dqkv[:, 1536:2304] = dv[...].astype(BF)
    a_t[...] = a[...].T
    d_a[...] = jnp.zeros_like(d_a)

    @pl.loop(0, 3)
    def _(n):
        part = dqkv[:, wide(n)]
        gbuf[:, wide(n)] = dot(a_t[...], part).astype(BF)
        store(n).start()
        d_a[...] += dot_nt(part, w[:, wide(n)])

    u, scale = unit(xs[...].astype(F32))
    c = d_a[...]
    gvec[...] = gin[...]
    gvec[0:1, :] = jnp.sum(c * u, axis=0, keepdims=True)
    c = c * gain_a
    got_cf.wait()

    def norm_back(c, rows):
        ur = u[rows]
        return scale[rows] * (c - ur * jnp.mean(ur * c, axis=-1, keepdims=True))

    own = slice(64, 576)
    dxg[...] = norm_back(c[own] + cf[...], own) + g[...].astype(F32)
    halo[0:64, :] = norm_back(c[0:64], slice(0, 64)).astype(BF)
    halo[64:128, :] = norm_back(c[576:640], slice(576, 640)).astype(BF)
    stores.finish()
    for n in range(4):
        store(n).wait()


def slots_kernel(meta, routed, x, g, slots, st):
    me = meta[20]
    start = meta[me]
    token = lax.broadcasted_iota(jnp.int32, (512, 1024), 0) + 512 * me
    r = jnp.broadcast_to(routed[...], (512, 1024))
    rank = jnp.sum((r < token).astype(F32), axis=1, keepdims=True).astype(jnp.int32) - start
    hit = jnp.sum((r == token).astype(F32), axis=1, keepdims=True)
    row = ((start + rank) & 15) * 8 + (rank >> 4)
    row = jnp.where((hit > 0.5) & (rank < CAP), row, -1)
    lane = lax.broadcasted_iota(jnp.int32, (512, 128), 1)
    onehot = (lane == row).astype(F32).astype(BF)
    st[...] = onehot
    slots[:, 0:768] = dot_tn(onehot, x[...]).astype(BF)
    slots[:, 768:1536] = dot_tn(onehot, g[...]).astype(BF)


def entry_slots(meta):
    p = 16 * lax.broadcasted_iota(jnp.int32, (64, 128), 0) + meta[20]
    source, before = jnp.zeros_like(p), jnp.zeros_like(p)
    for d in range(1, 16):
        source = source + (p >= meta[d]).astype(jnp.int32)
        before = jnp.where(p >= meta[d], meta[d], before)
    rank = p - before
    lane = lax.broadcasted_iota(jnp.int32, (64, 128), 1)
    return ((lane == source * 8 + (rank >> 4)) & (rank < CAP)).astype(F32).astype(BF)


def entries_kernel(meta, got, own, many, kmask):
    entry = entry_of(lax.broadcasted_iota(jnp.int32, (1024, 128), 0))
    bias = jnp.zeros((1024, 128), F32)
    for d in range(16):
        bias = jnp.where((entry >= meta[d] + CAP) & (entry < meta[d + 1]), NEG, bias)
    kmask[:, 0:128] = jnp.where(entry < meta[17], bias, NEG)
    kmask[:, 128:256] = jnp.where(entry < meta[17], NEG, bias)
    rows = dot(entry_slots(meta), got[...]).astype(BF)
    own[...] = rows
    for t in range(16):
        many[t] = rows


def home_kernel(meta, parts_in, own_in, send_in, send, back, own, parts, sems):
    copies = Copies(sems)
    got = [copies.start(parts_in.at[4 * n : 4 * n + 4], parts.at[4 * n : 4 * n + 4]) for n in range(4)]
    got_own = copies.start(own_in, own)
    onehot = entry_slots(meta)
    total = jnp.zeros((64, 1536), F32)
    for n in range(4):
        got[n].wait()
        for t in range(4 * n, 4 * n + 4):
            total = total + parts[t].astype(F32)
    got_own.wait()
    u, scale = unit(own[:, 0:768].astype(F32))
    c = total[:, 768:1536]
    dxr = scale * (c - u * jnp.mean(u * c, axis=-1, keepdims=True))
    back[:, 0:768] = dot_tn(onehot, total[:, 0:768].astype(BF)).astype(BF)
    back[:, 768:1536] = dot_tn(onehot, dxr.astype(BF)).astype(BF)
    copies.start(back, send.at[:, S_BACK:S_ALL]).wait()


def entry_of(row):
    return ((row & 63) << 4) + (row >> 6)


def heavy_kernel(
    meta, xg_in, hw_in, wo, kmask_in, gin, vrows, rest_in,
    parts, rest,
    xg, w, wd, ar, fr, q, k, v, o, do, dqkv, dk, dv, kmask, da, dgu, hid, sa, sf, la,
    hw, pbuf, gbuf, gvec, in_sems, out_sems,
):
    loads, stores = Copies(in_sems), Copies(out_sems)
    got_hw = loads.start(hw_in, hw)
    got_xg = loads.start(xg_in, xg)
    got_kmask = loads.start(kmask_in, kmask)
    pick = pick6(96, 128)
    gain_a, gain_f, r_a, r_f = (vrows[n : n + 1, :] for n in range(4))
    got_hw.wait()
    for b in range(8):
        w[96 * b : 96 * b + 96, :] = dot(pick, hw[b, 0:128, :]).astype(BF)
        wd[32 * b : 32 * b + 32, :] = hw[b, 128:160, 0:768]
    low, head = meta[18], meta[19]
    on = (lax.broadcasted_iota(jnp.int32, (256, 128), 1) >> 6) == head
    got_xg.wait()

    @pl.loop(0, 4)
    def _(b):
        rows = pl.ds(pl.multiple_of(256 * b, 256), 256)
        u, _ = unit(xg[rows, 0:768].astype(F32))
        arb, frb = (u * gain_a).astype(BF), (u * gain_f).astype(BF)
        ar[rows, :], fr[rows, :] = arb, frb
        sab = jax.nn.sigmoid(jnp.sum(arb.astype(F32) * r_a, axis=-1, keepdims=True))
        sfb = jax.nn.sigmoid(jnp.sum(frb.astype(F32) * r_f, axis=-1, keepdims=True))
        sa[rows, :], sf[rows, :] = sab, sfb
        qkv = dot(arb, w[:, 512:896])
        q[rows, :] = jnp.where(on, qkv[:, 0:128], 0.0).astype(BF)
        k[rows, :] = qkv[:, 128:256].astype(BF)
        v[rows, :] = jnp.where(on, qkv[:, 256:384], 0.0).astype(BF)
        dab = (sab * xg[rows, 768:1536].astype(F32)).astype(BF)
        da[rows, :] = dab
        do[rows, :] = dot_nt(dab, wo[...]).astype(BF)

    got_kmask.wait()
    n0 = meta[17]
    dk[...] = jnp.zeros_like(dk)
    dv[...] = jnp.zeros_like(dv)

    @pl.loop(0, 4, unroll=2)
    def _(b):
        rows = pl.ds(pl.multiple_of(256 * b, 256), 256)
        first = entry_of(lax.broadcasted_iota(jnp.int32, (1, 128), 1) + 256 * b) < n0
        second = entry_of(lax.broadcasted_iota(jnp.int32, (1, 128), 1) + 256 * b + 128) < n0
        bias = jnp.concatenate(
            [jnp.where(first, kmask[:, 0:128], kmask[:, 128:256]),
             jnp.where(second, kmask[:, 0:128], kmask[:, 128:256])],
            axis=1,
        )
        qb, dob = q[rows, :], do[rows, :]
        s = dot_nt(k[...], qb) * HEAVY_SCALE + bias
        e = jnp.exp(s - jnp.max(s, axis=0, keepdims=True))
        p = e * (1.0 / jnp.sum(e, axis=0, keepdims=True))
        pb = p.astype(BF)
        ob = dot_tn(pb, v[...]).astype(BF)
        o[rows, :] = ob
        la[rows, :] = (1.0 - sa[rows, :]) * jnp.sum(
            ob.astype(F32) * dob.astype(F32), axis=-1, keepdims=True
        )
        dp = dot_nt(v[...], dob)
        ds = (p * (dp - jnp.sum(p * dp, axis=0, keepdims=True))).astype(BF)
        dqkv[rows, 0:128] = jnp.where(on, dot_tn(ds, k[...]) * HEAVY_SCALE, 0.0).astype(BF)
        dk[...] += dot(ds, qb) * HEAVY_SCALE
        dv[...] += dot(pb, dob)

    dqkv[:, 128:256] = dk[...].astype(BF)
    dqkv[:, 256:384] = dv[...].astype(BF)
    gbuf[:, 512:896] = dot_tn(ar[...], dqkv[...]).astype(BF)
    gbuf[:, R_HO - R_HEAVY : R_VEC - R_HEAVY] = jnp.zeros((768, 768), BF)
    gbuf[pl.ds(pl.multiple_of(low, 128), 128), R_HO - R_HEAVY : R_VEC - R_HEAVY] = dot_tn(o[...], da[...]).astype(BF)
    at = R_HEAVY
    stores.send(gbuf.at[:, 512 : R_VEC - at], rest.at[:, at + 512 : R_VEC])
    gvec[...] = gin[...]

    def send_parts(b):
        rows = pl.ds(pl.multiple_of(256 * b, 256), 256)
        return pltpu.make_async_copy(pbuf.at[rows, :], parts.at[rows, :], out_sems.at[3 + b])

    @pl.loop(0, 4, unroll=2)
    def _(b):
        rows = pl.ds(pl.multiple_of(256 * b, 256), 256)
        frb = fr[rows, :]
        sfb = sf[rows, :]
        dfb = (sfb * xg[rows, 768:1536].astype(F32)).astype(BF)
        both = dot(frb, w[:, 0:512])
        act, slope = gelu_parts(both[:, 0:256])
        up = both[:, 256:512]
        hidden = (act * up).astype(BF)
        hid[rows, :] = hidden
        dh = dot_nt(dfb, wd[...])
        lfb = (1.0 - sfb) * jnp.sum(hidden.astype(F32) * dh, axis=-1, keepdims=True)
        dgub = jnp.concatenate([(dh * up * slope).astype(BF), (dh * act).astype(BF)], axis=1)
        dgu[rows, :] = dgub
        y = sa[rows, :] * dot(o[rows, :], wo[...]) + sfb * dot(hidden, wd[...])
        lab = la[rows, :]
        d_f = dot_nt(dgub, w[:, 0:512]) + lfb * r_f
        d_a = dot_nt(dqkv[rows, :], w[:, 512:896]) + lab * r_a
        u, _ = unit(xg[rows, 0:768].astype(F32))
        gvec[0:1, :] += jnp.sum(d_a * u, axis=0, keepdims=True)
        gvec[1:2, :] += jnp.sum(d_f * u, axis=0, keepdims=True)
        gvec[2:3, :] += jnp.sum(lab * ar[rows, :].astype(F32), axis=0, keepdims=True)
        gvec[3:4, :] += jnp.sum(lfb * frb.astype(F32), axis=0, keepdims=True)
        da[rows, :] = dfb
        pbuf[rows, 0:768] = y.astype(BF)
        pbuf[rows, 768:1536] = (d_a * gain_a + d_f * gain_f).astype(BF)
        send_parts(b).start()

    gbuf[:, 0:512] = dot_tn(fr[...], dgu[...]).astype(BF)
    stores.send(gbuf.at[:, 0:512], rest.at[:, at : at + 512])
    vecs = jnp.concatenate([gvec[...], jnp.zeros((120, 768), F32)], axis=0)
    gbuf[:, R_VEC - R_HEAVY : R_DOWN - R_HEAVY] = vecs.T.astype(BF)
    gd = dot_tn(hid[...], da[...]).astype(BF)
    for r in range(8):
        for t in range(3):
            gbuf[96 * r + 32 * t : 96 * r + 32 * t + 32, R_DOWN - R_HEAVY : R_ALL - R_HEAVY] = gd[
                32 * r : 32 * r + 32, 256 * t : 256 * t + 256
            ]
    stores.send(gbuf.at[:, R_VEC - at : R_ALL - at], rest.at[:, R_VEC:R_ALL])
    stores.finish()
    for b in range(4):
        send_parts(b).wait()


def tokens_kernel(got, st, lo, dxg, hl, hr, out, grad):
    back = dot(st[...], got[:, :, S_BACK:S_ALL].reshape(128, 1536))
    out[...] = (lo[...] + back[:, 0:768]).astype(BF)
    dx = dxg[...] + back[:, 768:1536]
    grad[0:64, :] = (dx[0:64, :] + hl[...].astype(F32)).astype(BF)
    grad[64:448, :] = dx[64:448, :].astype(BF)
    grad[448:512, :] = (dx[448:512, :] + hr[...].astype(F32)).astype(BF)


def tail_rows(block, low):
    last = jnp.concatenate([block[32 * t : 32 * t + 32, low + 768 : low + 1024] for t in range(3)], axis=1)
    return jnp.concatenate([block[:, low : low + 768], last], axis=0)


def owner_rows(r, cols):
    quarter = cols // 4
    row = lax.broadcasted_iota(jnp.int32, (128, 96), 0)
    col = lax.broadcasted_iota(jnp.int32, (128, 96), 1)
    device, low = 6 * (row >> 3), row & 7
    main = ((low < 6) & (col == device + low)).astype(F32).astype(BF)
    tail = r[:, 3 * quarter : cols]
    pieces = []
    for t in range(3):
        extra = ((low >= 6) & (col == device + 3 * (low - 6) + t)).astype(F32).astype(BF)
        pieces.append((dot(main, r[:, quarter * t : quarter * t + quarter]) + dot(extra, tail)).astype(BF))
    return jnp.concatenate(pieces, axis=1)


def tail_of(block):
    cols = block.shape[1] // 3
    return jnp.concatenate(
        [block[6 + n : 7 + n, cols * t : cols * t + cols] for n in range(2) for t in range(3)], axis=0
    )


def spread_ffn_kernel(r, send, rows, sems):
    rows[:, 0:S_DOWN] = owner_rows(r, F_DOWN)
    rows[:, S_DOWN:S_REST] = tail_rows(r[...], F_DOWN)
    Copies(sems).start(rows, send.at[:, 0:S_REST]).wait()


def spread_rest_kernel(r, send_in, send, hd, rows, sems):
    rows[...] = owner_rows(r, R_ALL)
    copy = Copies(sems).start(rows, send.at[:, S_REST:S_BACK])
    hd[...] = jnp.concatenate([r[32 * t : 32 * t + 32, R_DOWN:R_ALL] for t in range(3)], axis=1)
    copy.wait()


def sum_parts(got, a, b):
    t = got[0, :, a:b].astype(F32)
    for d in range(1, 16):
        t = t + got[d, :, a:b].astype(F32)
    return t


def sum_ffn_kernel(got, gate, up, down):
    both = sum_parts(got, 0, S_DOWN)
    for c in range(3):
        gate[:, 256 * c : 256 * c + 256] = both[0:6, 512 * c : 512 * c + 256]
        up[:, 256 * c : 256 * c + 256] = both[0:6, 512 * c + 256 : 512 * c + 512]
    both = tail_of(both)
    gate[:, 768:1024] = both[:, 0:256]
    up[:, 768:1024] = both[:, 256:512]
    down[...] = sum_parts(got, S_DOWN, S_REST)


def sum_rest_kernel(got, q, k, v, o, hq, hk, hv, ho, hgate, hup, vecs):
    total = sum_parts(got, S_REST, S_BACK)
    for n, ref in enumerate((q, k, v, o)):
        ref[...] = total[0:6, 768 * n : 768 * n + 768]
    rest = tail_of(total)
    ho[...] = rest[:, 128:896]
    rows = jnp.concatenate([rest[:, 896:1024], jnp.zeros((122, 128), F32)], axis=0).T
    for n, ref in enumerate(vecs):
        ref[...] = rows[n : n + 1, 0:6]
    at = S_REST + R_HEAVY
    for j in range(16):
        hgate[:, 256 * j : 256 * j + 256] = got[j, :, at : at + 256].astype(F32)[0:6]
        hup[:, 256 * j : 256 * j + 256] = got[j, :, at + 256 : at + 512].astype(F32)[0:6]
    at = at + 512
    for p in range(6):
        two = [got[2 * p + n, :, S_REST:S_BACK].astype(F32) for n in range(2)]
        pair = two[0][:, R_HEAVY + 512 : R_HEAVY + 768] + two[1][:, R_HEAVY + 512 : R_HEAVY + 768]
        hq[:, 128 * p : 128 * p + 128] = pair[0:6, 0:128]
        hk[:, 128 * p : 128 * p + 128] = pair[0:6, 128:256]
        hv[:, 128 * p : 128 * p + 128] = tail_of(two[0] + two[1])[:, 0:128]


def last_kernel(
    got_in, st, lo_in, dxg_in, hl, hr,
    out, grad, q, k, v, o, gate, up, down, hq, hk, hv, ho, hgate, hup, *rest,
):
    *vecs, got, lo, dxg, sems = rest
    copies = Copies(sems)
    pieces = [
        copies.start(got_in.at[:, :, a:b], got.at[:, :, a:b])
        for a, b in ((0, S_REST), (S_REST, S_BACK), (S_BACK, S_ALL))
    ]
    got_lo, got_dxg = copies.start(lo_in, lo), copies.start(dxg_in, dxg)
    pieces[0].wait()
    sum_ffn_kernel(got, gate, up, down)
    pieces[1].wait()
    sum_rest_kernel(got, q, k, v, o, hq, hk, hv, ho, hgate, hup, vecs)
    pieces[2].wait()
    got_lo.wait()
    got_dxg.wait()
    tokens_kernel(got, st, lo, dxg, hl, hr, out, grad)


def call(kernel, outs, args, scratch=(), in_specs=None, out_specs=None, sems=(), name=None, us=0.05, aliases={}):
    return pl.pallas_call(
        kernel,
        out_shape=[jax.ShapeDtypeStruct(s, t) for s, t in outs],
        in_specs=in_specs or [VMEM] * len(args),
        out_specs=out_specs or [VMEM] * len(outs),
        scratch_shapes=[pltpu.VMEM(s, t) for s, t in scratch]
        + [pltpu.SemaphoreType.DMA((n,)) for n in sems],
        compiler_params=PARAMS,
        cost_estimate=pl.CostEstimate(
            flops=int(us * 1.0e9), bytes_accessed=int(us * 3.0e6), transcendentals=0
        ),
        input_output_aliases=aliases,
        name=name,
    )(*args)


def run_light_ffn(tokens, cotangent, wall):
    return call(
        light_ffn_kernel,
        [((512, 768), F32), ((512, 768), F32), ((768, F_ALL), BF), ((8, 768), F32), ((8, 768), F32)],
        (tokens, cotangent, wall),
        [
            ((512, 768), BF), ((512, 768), BF),
            ((768, 512), BF), ((512, 768), BF), ((768, 512), BF), ((768, 3072), BF),
            ((1024, 2048), BF), ((1024, 256), BF), ((1024, 128), BF), ((256, 768), BF),
        ],
        [HBM, HBM, HBM],
        [VMEM, VMEM, HBM, VMEM, VMEM],
        sems=(11, 8),
        name="light_ffn",
        us=200,
    )


def run_light_attn(meta, xl, tokens, xr, cotangent, wall, ffn, cf, gvec, vrows):
    return call(
        light_attn_kernel,
        [
            ((512, 768), F32), ((512, 768), F32), ((128, 768), BF), ((768, R_ALL), BF), ((8, 768), F32),
            ((128, 768), BF),
        ],
        (meta, xl, tokens, xr, cotangent, wall, ffn, cf, gvec, vrows),
        [
            ((768, 3072), BF), ((640, 768), BF), ((640, 768), BF), ((768, 640), BF), ((640, 2304), BF),
            ((512, 768), BF), ((512, 768), BF), ((640, 2304), BF),
            ((640, 768), F32), ((640, 768), F32), ((4, 256, 256), F32),
            ((1024, 3072), BF), ((512, 768), BF), ((512, 768), F32), ((512, 768), F32),
            ((512, 768), F32), ((640, 768), F32), ((768, 3072), BF),
        ],
        [SMEM, VMEM, HBM, VMEM, HBM] + [HBM] * 3 + [VMEM, VMEM],
        [HBM, VMEM, VMEM, HBM, VMEM, VMEM],
        sems=(8, 5),
        name="light_attn",
        us=2,
    )


def run_heavy(meta, xg, hw, wo, kmask, gvec, vrows, rest):
    col = ((1024, 1), F32)
    rows, narrow = ((1024, 768), BF), ((1024, 128), BF)
    return call(
        heavy_kernel,
        [((1024, 1536), BF), ((768, R_ALL), BF)],
        (meta, xg, hw, wo, kmask, gvec, vrows, rest),
        [
            ((1024, 1536), BF), ((768, 896), BF), ((256, 768), BF), rows, rows,
            narrow, narrow, narrow, narrow, narrow, ((1024, 384), BF),
            ((1024, 128), F32), ((1024, 128), F32), ((1024, 256), F32),
            rows, ((1024, 512), BF), ((1024, 256), BF), col, col, col,
            ((8, 160, 896), BF), ((1024, 1536), BF), ((768, R_ALL - R_HEAVY), BF), ((8, 768), F32),
        ],
        [SMEM, HBM, HBM, VMEM, HBM, VMEM, VMEM, HBM],
        [HBM, HBM],
        sems=(3, 7),
        aliases={7: 1},
        name="heavy",
        us=200,
    )


def body(
    tokens, lengths, routed, cotangent, gain_attn, gain_ffn, router_attn, router_ffn,
    light_q, light_k, light_v, light_o, light_gate, light_up, light_down,
    heavy_q, heavy_k, heavy_v, heavy_o, heavy_gate, heavy_up, heavy_down,
):
    me = lax.axis_index("fsdp")
    vectors = [v.reshape(1, 6) for v in (gain_attn, gain_ffn, router_attn, router_ffn)]
    pack, hsend, hd = call(
        prep_kernel,
        [((8, C_ALL), BF), ((16, 8, 896), BF), ((32, 768), BF)],
        (
            light_q, light_k, light_v, light_o, light_gate, light_up, light_down,
            heavy_q, heavy_k, heavy_v, heavy_o, heavy_gate, heavy_up, heavy_down, *vectors,
        ),
        [((8, C_ALL), F32), ((128, 128), F32), ((8, 4096), F32)],
        name="prep",
    )
    wall = lax.all_gather(pack, ALL, axis=0, tiled=True)

    hcols = lax.all_to_all(hsend, "fsdp", split_axis=0, concat_axis=0, tiled=True)
    hd = lax.ppermute(hd, ALL, [(d, (d % 8) * 16 + d // 8) for d in range(128)])
    hblock = jnp.concatenate([hcols.reshape(128, 896), jnp.pad(hd, ((0, 0), (0, 128)))], axis=0)

    edges = jnp.arange(17, dtype=jnp.int32) * 512
    bounds = jnp.sum((routed[0][None, :] < edges[:, None]).astype(jnp.int32), axis=1)
    dp = lax.axis_index("dp")
    pair = jnp.where(me < 12, me // 2, 5)
    meta = jnp.concatenate(
        [
            bounds,
            jnp.stack(
                [
                    lengths[0, 0] // 8, 128 * pair, jnp.where(me < 12, me % 2, 2),
                    me, dp // 2, dp % 2, lengths[0, 0],
                ]
            ),
        ]
    )

    def swap(rows):
        return lax.all_to_all(rows, "fsdp", split_axis=0, concat_axis=0, tiled=True)

    slots, st = call(
        slots_kernel,
        [((128, 1536), BF), ((512, 128), BF)],
        (meta, routed, tokens, cotangent),
        in_specs=[SMEM, VMEM, VMEM, VMEM],
        name="slots",
    )
    own, many, kmask = call(
        entries_kernel,
        [((64, 1536), BF), ((16, 64, 1536), BF), ((1024, 256), F32)],
        (meta, swap(slots.reshape(16, 8, 1536)).reshape(128, 1536)),
        in_specs=[SMEM, VMEM],
        name="entries",
    )
    right = [(i, i + 1) for i in range(15)]
    left = [(i + 1, i) for i in range(15)]
    xl = lax.ppermute(tokens[448:512], "fsdp", right)
    xr = lax.ppermute(tokens[0:64], "fsdp", left)

    wall, many, xl, xr, hblock = lax.optimization_barrier((wall, many, xl, xr, hblock))
    hw = lax.all_gather(hblock, "dp", axis=0, tiled=False)
    xg = swap(many).reshape(1024, 1536)
    ffn, cf, grad_ffn, gvec, vrows = run_light_ffn(tokens, cotangent, wall)
    rs_ffn = lax.psum_scatter(grad_ffn, "dp", scatter_dimension=0, tiled=True)
    lmeta = jnp.concatenate([jnp.stack([lengths[0, 0], me * 512, jnp.int32(8192)]), meta[18:20]])
    lo, dxg, halo, rest, gvec, heavy_wo = run_light_attn(
        lmeta, xl, tokens, xr, cotangent, wall, ffn, cf, gvec, vrows
    )
    parts, rest = run_heavy(meta, xg, hw, heavy_wo, kmask, gvec, vrows, rest)
    rs_rest = lax.psum_scatter(rest, "dp", scatter_dimension=0, tiled=True)
    hr = lax.ppermute(halo[0:64], "fsdp", left)
    hl = lax.ppermute(halo[64:128], "fsdp", right)
    (send,) = call(
        spread_ffn_kernel,
        [((128, S_ALL), BF)],
        (rs_ffn,),
        [((128, S_REST), BF)],
        out_specs=[HBM],
        sems=(1,),
        name="spread_ffn",
    )
    parts = swap(parts.reshape(16, 64, 1536))
    parts, send, hr, hl = lax.optimization_barrier((parts, send, hr, hl))
    (send,) = call(
        home_kernel,
        [((128, S_ALL), BF)],
        (meta, parts, own, send),
        [((128, 1536), BF), ((64, 1536), BF), ((16, 64, 1536), BF)],
        [SMEM, HBM, HBM, HBM],
        [HBM],
        sems=(6,),
        name="home",
        aliases={3: 0},
    )
    send, g_hd = call(
        spread_rest_kernel,
        [((128, S_ALL), BF), ((32, 768), BF)],
        (rs_rest, send),
        [((128, S_BACK - S_REST), BF)],
        [VMEM, HBM],
        [HBM, VMEM],
        sems=(1,),
        name="spread_rest",
        aliases={1: 0},
    )
    g_hd = lax.ppermute(g_hd, ALL, [((d % 8) * 16 + d // 8, d) for d in range(128)])
    got = swap(send.reshape(16, 8, S_ALL))
    six, four, big = ((6, 768), F32), ((6, 1024), F32), ((6, 4096), F32)
    (
        output, grad_tokens, g_q, g_k, g_v, g_o, g_gate, g_up, g_down,
        g_hq, g_hk, g_hv, g_ho, g_hgate, g_hup, *g_vecs,
    ) = call(
        last_kernel,
        [((512, 768), BF), ((512, 768), BF)] + [six] * 4 + [four, four, ((8, 768), F32)]
        + [six] * 4 + [big, big] + [((1, 6), F32)] * 4,
        (got, st, lo, dxg, hl, hr),
        [((16, 8, S_ALL), BF), ((512, 768), F32), ((512, 768), F32)],
        [HBM, VMEM, HBM, HBM, VMEM, VMEM],
        sems=(5,),
        name="last",
    )
    return (
        output, grad_tokens,
        *[v.reshape(6) for v in g_vecs],
        g_q, g_k, g_v, g_o, g_gate, g_up, g_down,
        g_hq, g_hk, g_hv, g_ho, g_hgate, g_hup, g_hd.astype(F32),
    )


def solution(mesh):
    rows = P(ALL, None)
    flat = P(ALL)
    in_specs = (rows, P("dp", None), P("dp", None), rows) + (flat,) * 4 + (rows,) * 14
    out_specs = (rows, rows) + (flat,) * 4 + (rows,) * 14
    return jax.shard_map(body, mesh=mesh, in_specs=in_specs, out_specs=out_specs, check_vma=False)
```

```python
import jax
import jax.numpy as jnp
from jax import lax
from jax.experimental import pallas as pl
from jax.experimental.pallas import tpu as pltpu
from jax.sharding import PartitionSpec as P

BF = jnp.bfloat16
F32 = jnp.float32
EPS = 1e-6
NEG = -1e30
ALL = ("dp", "fsdp")
CAP = 96
LIGHT_SCALE = 96**-0.5
HEAVY_SCALE = 64**-0.5
PARAMS = pltpu.CompilerParams(vmem_limit_bytes=60 * 1024 * 1024)
SMEM = pl.BlockSpec(memory_space=pltpu.SMEM)
VMEM = pl.BlockSpec(memory_space=pltpu.VMEM)
HBM = pl.BlockSpec(memory_space=pl.ANY)

C_QKVO, C_VEC, C_DOWN, C_ALL = 2048, 5120, 5248, 5504
F_DOWN, F_ALL = 2048, 3072
R_HEAVY, R_HO, R_VEC, R_DOWN, R_ALL = 3072, 3968, 4736, 4864, 5120
S_DOWN, S_FFN = 1536, 2304
S_BACK, S_ALL = 3840, 5376

def dot(a, b):
    return jnp.dot(a, b, preferred_element_type=F32)


def dot_nt(a, b):
    return lax.dot_general(a, b, (((1,), (1,)), ((), ())), preferred_element_type=F32)


def dot_tn(a, b):
    return lax.dot_general(a, b, (((0,), (0,)), ((), ())), preferred_element_type=F32)


def pick6(rows, cols, shift=0):
    r = lax.broadcasted_iota(jnp.int32, (rows, cols), 0) + shift
    c = lax.broadcasted_iota(jnp.int32, (rows, cols), 1)
    low = c & 7
    return ((6 * (c >> 3) + low == r) & (low < 6)).astype(F32).astype(BF)


def unpad_rows(ref, out_ref, pick, at=0, width=None):
    width = width or ref.shape[1]
    for b in range(8):
        block = dot(pick, ref[128 * b : 128 * b + 128, at : at + width])
        out_ref[96 * b : 96 * b + 96, at : at + width] = block.astype(BF)


def vector_rows(vec_ref, pick):
    blocks = [dot(pick, vec_ref[128 * b : 128 * b + 128, :]) for b in range(8)]
    return jnp.concatenate(blocks, axis=0).T


class Copies:
    def __init__(self, sems, used=0):
        self.sems, self.used, self.open = sems, used, []

    def start(self, src, dst):
        copy = pltpu.make_async_copy(src, dst, self.sems.at[self.used])
        self.used += 1
        copy.start()
        return copy

    def send(self, src, dst):
        self.open.append(self.start(src, dst))

    def finish(self):
        for copy in self.open:
            copy.wait()


def unit(rows):
    scale = lax.rsqrt(jnp.mean(rows * rows, axis=-1, keepdims=True) + EPS)
    return rows * scale, scale


def gelu_parts(gate):
    c0, c1 = 0.7978845608, 0.044715
    sq = gate * gate
    t = jnp.tanh(gate * (c0 + (c0 * c1) * sq))
    half = 0.5 * (1.0 + t)
    slope = half + (0.5 * gate) * (1.0 - t * t) * (c0 + (3.0 * c0 * c1) * sq)
    return gate * half, slope


def prep_kernel(
    q, k, v, o, gate, up, down, hq, hk, hv, ho, hgate, hup, hdown, ga, gf, ra, rf, pack, hsend, hd, scr, rows, wide
):
    scr[...] = jnp.zeros_like(scr)
    zero128 = jnp.zeros((8, 128), BF)
    for c in range(4):
        cols = slice(256 * c, 256 * c + 256)
        scr[0:6, 512 * c : 512 * c + 256] = gate[:, cols]
        scr[0:6, 512 * c + 256 : 512 * c + 512] = up[:, cols]
    for n, ref in enumerate((q, k, v, o)):
        scr[0:6, C_QKVO + 768 * n : C_QKVO + 768 * n + 768] = ref[...]
    for a in range(2):
        for b in range(4):
            scr[6 + a : 7 + a, 512 * b : 512 * b + 512] = down[4 * a + b : 4 * a + b + 1, 0:512]
        for b in range(3):
            at = C_QKVO + 768 * b
            scr[6 + a : 7 + a, at : at + 768] = ho[3 * a + b : 3 * a + b + 1, :]
    scr[:, C_DOWN:C_ALL] = down[:, 512:768]
    rows[...] = jnp.zeros_like(rows)
    for n, ref in enumerate((ga, gf, ra, rf)):
        rows[n : n + 1, 0:6] = ref[...]
    scr[:, C_VEC : C_VEC + 128] = rows[...].T[0:8, :]
    pack[...] = scr[...].astype(BF)
    wide[...] = jnp.zeros_like(wide)

    def padded(ref):
        cols = ref.shape[1]
        wide[0:6, 0:cols] = ref[...]
        return wide[:, 0:cols].astype(BF)

    wq, wk, wv = padded(hq), padded(hk), padded(hv)
    wg, wu = padded(hgate), padded(hup)
    for j in range(16):
        hsend[j, :, 0:256] = wg[:, 256 * j : 256 * j + 256]
        hsend[j, :, 256:512] = wu[:, 256 * j : 256 * j + 256]
        for n, w in enumerate((wq, wk, wv)):
            p = j // 2
            part = w[:, 128 * p : 128 * p + 128] if j < 12 else zero128
            hsend[j, :, 512 + 128 * n : 640 + 128 * n] = part
    hd[...] = hdown[...].astype(BF)


def light_ffn_kernel(
    x_in, g_in, wall, ffn, cf, light, gvec, vrows, x, g, gu, fin, fin_t, gbuf, gu_pad, down, vec, wd, in_sems, out_sems
):
    def wide(c, at=0):
        return pl.ds(pl.multiple_of(at + 512 * c, 128), 512)

    def loads(c):
        rows = pl.ds(pl.multiple_of(256 * c, 256), 256)
        yield pltpu.make_async_copy(wall.at[:, wide(c)], gu_pad.at[:, wide(c)], in_sems.at[2 * c])
        yield pltpu.make_async_copy(
            wall.at[rows, C_DOWN:C_ALL], down.at[rows, :], in_sems.at[2 * c + 1]
        )

    def stores(c):
        rows = pl.ds(pl.multiple_of(192 * c, 64), 192)
        yield pltpu.make_async_copy(gbuf.at[:, wide(c)], light.at[:, wide(c)], out_sems.at[2 * c])
        yield pltpu.make_async_copy(
            gbuf.at[rows, 2048:3072], light.at[rows, F_DOWN:F_ALL], out_sems.at[2 * c + 1]
        )

    first = Copies(in_sems, 8)
    got_x = first.start(x_in, x)
    got_vec = first.start(wall.at[:, C_VEC : C_VEC + 128], vec)
    got_g = first.start(g_in, g)
    for c in range(4):
        for copy in loads(c):
            copy.start()
    pick = pick6(96, 128)
    got_x.wait()
    u, _ = unit(x[...].astype(F32))
    got_vec.wait()
    vrows[...] = vector_rows(vec, pick)[0:8, :]
    gain_f = vrows[1:2, :]
    f = (u * gain_f).astype(BF)
    fin[...] = f
    fin_t[...] = f.T
    ffn[...] = jnp.zeros_like(ffn)
    cf[...] = jnp.zeros_like(cf)
    got_g.wait()

    for c in range(4):
        for copy in loads(c):
            copy.wait()
    out_row = lax.broadcasted_iota(jnp.int32, (256, 256), 0)
    in_row = lax.broadcasted_iota(jnp.int32, (256, 256), 1)
    spare = (out_row & ~7) + 6 + ((out_row >> 2) & 1) == in_row
    spread = [(spare & ((out_row & 3) == b)).astype(F32).astype(BF) for b in range(4)]

    @pl.loop(0, 4)
    def _(c):
        for b in range(8):
            block = dot(pick, gu_pad[128 * b : 128 * b + 128, wide(c)])
            gu[96 * b : 96 * b + 96, :] = block.astype(BF)
        w = gu[...]
        rows = pl.ds(pl.multiple_of(256 * c, 256), 256)
        left = dot(spread[0], gu_pad[rows, 0:512])
        for b in range(1, 4):
            left = left + dot(spread[b], gu_pad[rows, 512 * b : 512 * b + 512])
        wd[:, 0:512] = left.astype(BF)
        wd[:, 512:768] = down[rows, :]
        both = dot(fin[...], w)
        act, slope = gelu_parts(both[:, 0:256])
        up = both[:, 256:512]
        hidden = (act * up).astype(BF)
        dh = dot_nt(g[...], wd[...])
        dgu = jnp.concatenate([(dh * up * slope).astype(BF), (dh * act).astype(BF)], axis=1)
        ffn[...] += dot(hidden, wd[...])
        cf[...] += dot_nt(dgu, w)
        gbuf[:, wide(c)] = dot(fin_t[...], dgu).astype(BF)
        gd = dot_tn(hidden, g[...]).astype(BF)
        for n in range(2):
            r0 = 128 * n
            at = pl.multiple_of(192 * c + 96 * n, 32)
            gbuf[pl.ds(at, 96), 2048:2816] = gd[r0 : r0 + 96, :]
            for t in range(3):
                gbuf[pl.ds(pl.multiple_of(at + 32 * t, 32), 32), 2816:3072] = gd[
                    r0 + 96 : r0 + 128, 256 * t : 256 * t + 256
                ]
        for copy in stores(c):
            copy.start()

    u, _ = unit(x[...].astype(F32))
    d_f = cf[...]
    gvec[...] = jnp.zeros_like(gvec)
    gvec[1:2, :] = jnp.sum(d_f * u, axis=0, keepdims=True)
    cf[...] = d_f * gain_f
    for c in range(4):
        for copy in stores(c):
            copy.wait()


def light_attn_kernel(
    meta, xl, x_in, xr, g_in, wall, ffn_in, cf_in, gin, vrows,
    lo, dxg, halo, rest, gvec, heavy_wo,
    w, xs, a, a_t, qkv, o, do, dqkv, dk, dv, mask, w_pad, g, ffn, cf, lo_buf, d_a, gbuf, in_sems, out_sems,
):
    def wide(n, at=0):
        return pl.ds(pl.multiple_of(at + 768 * n, 128), 768)

    def load(n):
        return pltpu.make_async_copy(wall.at[:, wide(n, C_QKVO)], w_pad.at[:, wide(n)], in_sems.at[n])

    def store(n):
        return pltpu.make_async_copy(gbuf.at[:, wide(n)], rest.at[:, wide(n)], out_sems.at[n])

    loads, stores = Copies(in_sems, 4), Copies(out_sems, 4)
    x = xs.at[64:576, :]
    got_x = loads.start(x_in, x)
    for n in range(4):
        load(n).start()
    got_g = loads.start(g_in, g)
    got_ffn = loads.start(ffn_in, ffn)
    got_cf = loads.start(cf_in, cf)
    pick = pick6(96, 128)
    xs[0:64, :] = xl[...]
    xs[576:640, :] = xr[...]
    first, base, pack_len = meta[0], meta[1], meta[2]
    key = lax.broadcasted_iota(jnp.int32, (256, 256), 0)
    qry = lax.broadcasted_iota(jnp.int32, (256, 256), 1) & 127
    gap = key - qry

    @pl.loop(0, 4)
    def _(b):
        qpos = base + 128 * b + qry
        kpos = base + 128 * b - 64 + key
        ok = (gap >= 0) & (gap <= 128) & ((qpos < first) == (kpos < first))
        ok = ok & (kpos >= 0) & (kpos < pack_len)
        mask[b] = jnp.where(ok, 0.0, NEG)

    dk[...] = jnp.zeros_like(dk)
    dv[...] = jnp.zeros_like(dv)
    dqkv[0:64, 0:768] = jnp.zeros((64, 768), BF)
    dqkv[576:640, 0:768] = jnp.zeros((64, 768), BF)
    got_x.wait()
    u, _ = unit(xs[...].astype(F32))
    gain_a = vrows[0:1, :]
    a[...] = (u * gain_a).astype(BF)

    def unpad(n):
        load(n).wait()
        for b in range(8):
            w[96 * b : 96 * b + 96, wide(n)] = dot(pick, w_pad[128 * b : 128 * b + 128, wide(n)]).astype(BF)

    @pl.loop(0, 3)
    def _(n):
        unpad(n)
        qkv[:, wide(n)] = dot(a[...], w[:, wide(n)]).astype(BF)

    unpad(3)
    got_g.wait()
    do[...] = dot_nt(g[...], w[:, 2304:3072]).astype(BF)

    row = lax.broadcasted_iota(jnp.int32, (128, 1024), 0)
    col = lax.broadcasted_iota(jnp.int32, (128, 1024), 1)
    entry = 6 * (col >> 3) + 3 * ((col & 7) - 6)
    keep = ((col & 7) >= 6) & ((row >> 6) == meta[4])
    wo = jnp.zeros((128, 768), F32)
    for b in range(3):
        take = (keep & (entry + b == row + meta[3])).astype(F32).astype(BF)
        wo = wo + dot(take, w_pad[:, 768 * b : 768 * b + 768])
    heavy_wo[...] = wo.astype(BF)

    lane = lax.broadcasted_iota(jnp.int32, (128, 256), 1)

    def pair(b, group, second):
        low = 64 * second
        even = (lane >= low) & (lane < low + 96)
        odd = (lane >= low + 96) & (lane < low + 192)

        def split(t):
            zero = jnp.zeros_like(t)
            return jnp.concatenate([jnp.where(even, t, zero), jnp.where(odd, t, zero)], axis=0)

        def join(t):
            return jnp.where(even, t[0:128], 0.0) + jnp.where(odd, t[128:256], 0.0)

        def win(part):
            return pl.ds(pl.multiple_of(768 * part + 384 * group + 128 * second, 128), 256)

        rq = pl.ds(pl.multiple_of(128 * b, 128), 128)
        rd = pl.ds(pl.multiple_of(128 * b + 64, 64), 128)
        rk = pl.ds(pl.multiple_of(128 * b, 128), 256)
        kw, vw = qkv[rk, win(1)], qkv[rk, win(2)]
        q2, do2 = split(qkv[rd, win(0)]), split(do[rq, win(0)])
        s = dot_nt(kw, q2) * LIGHT_SCALE + mask[b]
        dp = dot_nt(vw, do2)
        e = jnp.exp(s - jnp.max(s, axis=0, keepdims=True))
        p = e * (1.0 / jnp.sum(e, axis=0, keepdims=True))
        pb = p.astype(BF)
        ds = (p * (dp - jnp.sum(p * dp, axis=0, keepdims=True))).astype(BF)
        dk[rk, win(0)] += dot(ds, q2) * LIGHT_SCALE
        dv[rk, win(0)] += dot(pb, do2)
        return join(dot_tn(pb, vw)), join(dot_tn(ds, kw)) * LIGHT_SCALE

    @pl.loop(0, 8)
    def _(i):
        b, group = i >> 1, i & 1
        rq = pl.ds(pl.multiple_of(128 * b, 128), 128)
        rd = pl.ds(pl.multiple_of(128 * b + 64, 64), 128)
        o0, dq0 = pair(b, group, 0)
        o1, dq1 = pair(b, group, 1)

        def tile(n):
            return pl.ds(pl.multiple_of(384 * group + 128 * n, 128), 128)

        for ref, rows, t0, t1 in ((o, rq, o0, o1), (dqkv, rd, dq0, dq1)):
            ref[rows, tile(0)] = t0[:, 0:128].astype(BF)
            ref[rows, tile(1)] = (t0[:, 128:256] + t1[:, 0:128]).astype(BF)
            ref[rows, tile(2)] = t1[:, 128:256].astype(BF)

    got_ffn.wait()
    lo_buf[...] = x[...].astype(F32) + ffn[...] + dot(o[...], w[:, 2304:3072])
    stores.send(lo_buf, lo)
    gbuf[:, 2304:3072] = dot_tn(o[...], g[...]).astype(BF)
    store(3).start()
    dqkv[:, 768:1536] = dk[...].astype(BF)
    dqkv[:, 1536:2304] = dv[...].astype(BF)
    a_t[...] = a[...].T
    d_a[...] = jnp.zeros_like(d_a)

    @pl.loop(0, 3)
    def _(n):
        part = dqkv[:, wide(n)]
        gbuf[:, wide(n)] = dot(a_t[...], part).astype(BF)
        store(n).start()
        d_a[...] += dot_nt(part, w[:, wide(n)])

    u, scale = unit(xs[...].astype(F32))
    c = d_a[...]
    gvec[...] = gin[...]
    gvec[0:1, :] = jnp.sum(c * u, axis=0, keepdims=True)
    c = c * gain_a
    got_cf.wait()

    def norm_back(c, rows):
        ur = u[rows]
        return scale[rows] * (c - ur * jnp.mean(ur * c, axis=-1, keepdims=True))

    own = slice(64, 576)
    dxg[...] = norm_back(c[own] + cf[...], own) + g[...].astype(F32)
    halo[0:64, :] = norm_back(c[0:64], slice(0, 64)).astype(BF)
    halo[64:128, :] = norm_back(c[576:640], slice(576, 640)).astype(BF)
    stores.finish()
    for n in range(4):
        store(n).wait()


def slots_kernel(meta, routed, x, g, slots, st):
    me = meta[20]
    start = meta[me]
    token = lax.broadcasted_iota(jnp.int32, (512, 1024), 0) + 512 * me
    r = jnp.broadcast_to(routed[...], (512, 1024))
    rank = jnp.sum((r < token).astype(F32), axis=1, keepdims=True).astype(jnp.int32) - start
    hit = jnp.sum((r == token).astype(F32), axis=1, keepdims=True)
    row = ((start + rank) & 15) * 8 + (rank >> 4)
    row = jnp.where((hit > 0.5) & (rank < CAP), row, -1)
    lane = lax.broadcasted_iota(jnp.int32, (512, 128), 1)
    onehot = (lane == row).astype(F32).astype(BF)
    st[...] = onehot
    slots[:, 0:768] = dot_tn(onehot, x[...]).astype(BF)
    slots[:, 768:1536] = dot_tn(onehot, g[...]).astype(BF)


def entry_slots(meta):
    p = 16 * lax.broadcasted_iota(jnp.int32, (64, 128), 0) + meta[20]
    source, before = jnp.zeros_like(p), jnp.zeros_like(p)
    for d in range(1, 16):
        source = source + (p >= meta[d]).astype(jnp.int32)
        before = jnp.where(p >= meta[d], meta[d], before)
    rank = p - before
    lane = lax.broadcasted_iota(jnp.int32, (64, 128), 1)
    return ((lane == source * 8 + (rank >> 4)) & (rank < CAP)).astype(F32).astype(BF)


def entries_kernel(meta, got, own, many, kmask):
    entry = entry_of(lax.broadcasted_iota(jnp.int32, (1024, 128), 0))
    bias = jnp.zeros((1024, 128), F32)
    for d in range(16):
        bias = jnp.where((entry >= meta[d] + CAP) & (entry < meta[d + 1]), NEG, bias)
    kmask[:, 0:128] = jnp.where(entry < meta[17], bias, NEG)
    kmask[:, 128:256] = jnp.where(entry < meta[17], NEG, bias)
    rows = dot(entry_slots(meta), got[...]).astype(BF)
    own[...] = rows
    for t in range(16):
        many[t] = rows


def first_sum_kernel(meta, y0, y1, y2, y3, c0, c1, c2, c3, *outs):
    for n in range(4):
        for here, parts, out in (
            (meta[20] & 3, (y0, y1, y2, y3), outs[n]), (meta[20] >> 2, (c0, c1, c2, c3), outs[4 + n])
        ):
            rows = pl.ds(pl.multiple_of(64 * ((here + n) & 3), 64), 64)
            total = parts[0][rows, :].astype(F32)
            for part in parts[1:]:
                total = total + part[rows, :].astype(F32)
            out[...] = total.astype(BF)


def home_kernel(meta, y0, y1, y2, y3, c0, c1, c2, c3, own, send, back, sems):
    y, c = (
        a[...].astype(F32) + b[...].astype(F32) + d[...].astype(F32) + e[...].astype(F32)
        for a, b, d, e in ((y0, y1, y2, y3), (c0, c1, c2, c3))
    )
    onehot = entry_slots(meta)
    u, scale = unit(own[:, 0:768].astype(F32))
    dxr = scale * (c - u * jnp.mean(u * c, axis=-1, keepdims=True))
    back[:, 0:768] = dot_tn(onehot, y.astype(BF)).astype(BF)
    back[:, 768:1536] = dot_tn(onehot, dxr.astype(BF)).astype(BF)
    Copies(sems).start(back, send.at[:, S_BACK:S_ALL]).wait()


def entry_of(row):
    return ((row & 63) << 4) + (row >> 6)


def heavy_kernel(
    meta, xg_in, hw_in, wo, kmask_in, gin, vrows, rest_in,
    y0, y1, y2, y3, c0, c1, c2, c3, rest,
    xg, w, wd, ar, fr, q, k, v, o, do, dqkv, dk, dv, kmask, da, dgu, hid, sa, sf, la,
    hw, ybuf, cbuf, gbuf, gvec, in_sems, out_sems,
):
    loads, stores = Copies(in_sems), Copies(out_sems)
    got_hw = loads.start(hw_in, hw)
    got_xg = loads.start(xg_in, xg)
    got_kmask = loads.start(kmask_in, kmask)
    pick = pick6(96, 128)
    gain_a, gain_f, r_a, r_f = (vrows[n : n + 1, :] for n in range(4))
    got_hw.wait()
    for b in range(8):
        w[96 * b : 96 * b + 96, :] = dot(pick, hw[b, 0:128, :]).astype(BF)
        wd[32 * b : 32 * b + 32, :] = hw[b, 128:160, 0:768]
    low, head = meta[18], meta[19]
    on = (lax.broadcasted_iota(jnp.int32, (256, 128), 1) >> 6) == head
    got_xg.wait()

    @pl.loop(0, 4)
    def _(b):
        rows = pl.ds(pl.multiple_of(256 * b, 256), 256)
        u, _ = unit(xg[rows, 0:768].astype(F32))
        arb, frb = (u * gain_a).astype(BF), (u * gain_f).astype(BF)
        ar[rows, :], fr[rows, :] = arb, frb
        sab = jax.nn.sigmoid(jnp.sum(arb.astype(F32) * r_a, axis=-1, keepdims=True))
        sfb = jax.nn.sigmoid(jnp.sum(frb.astype(F32) * r_f, axis=-1, keepdims=True))
        sa[rows, :], sf[rows, :] = sab, sfb
        qkv = dot(arb, w[:, 512:896])
        q[rows, :] = jnp.where(on, qkv[:, 0:128], 0.0).astype(BF)
        k[rows, :] = qkv[:, 128:256].astype(BF)
        v[rows, :] = jnp.where(on, qkv[:, 256:384], 0.0).astype(BF)
        dab = (sab * xg[rows, 768:1536].astype(F32)).astype(BF)
        da[rows, :] = dab
        do[rows, :] = dot_nt(dab, wo[...]).astype(BF)

    got_kmask.wait()
    n0 = meta[17]
    dk[...] = jnp.zeros_like(dk)
    dv[...] = jnp.zeros_like(dv)

    @pl.loop(0, 4, unroll=2)
    def _(b):
        rows = pl.ds(pl.multiple_of(256 * b, 256), 256)
        first = entry_of(lax.broadcasted_iota(jnp.int32, (1, 128), 1) + 256 * b) < n0
        second = entry_of(lax.broadcasted_iota(jnp.int32, (1, 128), 1) + 256 * b + 128) < n0
        bias = jnp.concatenate(
            [jnp.where(first, kmask[:, 0:128], kmask[:, 128:256]),
             jnp.where(second, kmask[:, 0:128], kmask[:, 128:256])],
            axis=1,
        )
        qb, dob = q[rows, :], do[rows, :]
        s = dot_nt(k[...], qb) * HEAVY_SCALE + bias
        e = jnp.exp(s - jnp.max(s, axis=0, keepdims=True))
        p = e * (1.0 / jnp.sum(e, axis=0, keepdims=True))
        pb = p.astype(BF)
        ob = dot_tn(pb, v[...]).astype(BF)
        o[rows, :] = ob
        la[rows, :] = (1.0 - sa[rows, :]) * jnp.sum(
            ob.astype(F32) * dob.astype(F32), axis=-1, keepdims=True
        )
        dp = dot_nt(v[...], dob)
        ds = (p * (dp - jnp.sum(p * dp, axis=0, keepdims=True))).astype(BF)
        dqkv[rows, 0:128] = jnp.where(on, dot_tn(ds, k[...]) * HEAVY_SCALE, 0.0).astype(BF)
        dk[...] += dot(ds, qb) * HEAVY_SCALE
        dv[...] += dot(pb, dob)

    dqkv[:, 128:256] = dk[...].astype(BF)
    dqkv[:, 256:384] = dv[...].astype(BF)
    gbuf[:, 512:896] = dot_tn(ar[...], dqkv[...]).astype(BF)
    gbuf[:, R_HO - R_HEAVY : R_VEC - R_HEAVY] = jnp.zeros((768, 768), BF)
    gbuf[pl.ds(pl.multiple_of(low, 128), 128), R_HO - R_HEAVY : R_VEC - R_HEAVY] = dot_tn(o[...], da[...]).astype(BF)
    at = R_HEAVY
    stores.send(gbuf.at[:, 512 : R_VEC - at], rest.at[:, at + 512 : R_VEC])
    gvec[...] = gin[...]

    @pl.loop(0, 4, unroll=2)
    def _(b):
        rows = pl.ds(pl.multiple_of(256 * b, 256), 256)
        frb = fr[rows, :]
        sfb = sf[rows, :]
        dfb = (sfb * xg[rows, 768:1536].astype(F32)).astype(BF)
        both = dot(frb, w[:, 0:512])
        act, slope = gelu_parts(both[:, 0:256])
        up = both[:, 256:512]
        hidden = (act * up).astype(BF)
        hid[rows, :] = hidden
        dh = dot_nt(dfb, wd[...])
        lfb = (1.0 - sfb) * jnp.sum(hidden.astype(F32) * dh, axis=-1, keepdims=True)
        dgub = jnp.concatenate([(dh * up * slope).astype(BF), (dh * act).astype(BF)], axis=1)
        dgu[rows, :] = dgub
        y = sa[rows, :] * dot(o[rows, :], wo[...]) + sfb * dot(hidden, wd[...])
        lab = la[rows, :]
        d_f = dot_nt(dgub, w[:, 0:512]) + lfb * r_f
        d_a = dot_nt(dqkv[rows, :], w[:, 512:896]) + lab * r_a
        u, _ = unit(xg[rows, 0:768].astype(F32))
        gvec[0:1, :] += jnp.sum(d_a * u, axis=0, keepdims=True)
        gvec[1:2, :] += jnp.sum(d_f * u, axis=0, keepdims=True)
        gvec[2:3, :] += jnp.sum(lab * ar[rows, :].astype(F32), axis=0, keepdims=True)
        gvec[3:4, :] += jnp.sum(lfb * frb.astype(F32), axis=0, keepdims=True)
        da[rows, :] = dfb
        ybuf[rows, :] = y.astype(BF)
        c = (d_a * gain_a + d_f * gain_f).astype(BF)
        for t in range(4):
            cbuf[pl.ds(pl.multiple_of(256 * t + 64 * b, 64), 64), :] = c[64 * t : 64 * t + 64]

    for n, (yk, ck) in enumerate(((y0, c0), (y1, c1), (y2, c2), (y3, c3))):
        to_x = ((meta[20] >> 2) + n) & 3
        to_y = ((meta[20] & 3) + n) & 3
        stores.send(ybuf.at[pl.ds(pl.multiple_of(256 * to_x, 256), 256), :], yk)
        stores.send(cbuf.at[pl.ds(pl.multiple_of(256 * to_y, 256), 256), :], ck)

    gbuf[:, 0:512] = dot_tn(fr[...], dgu[...]).astype(BF)
    stores.send(gbuf.at[:, 0:512], rest.at[:, at : at + 512])
    vecs = jnp.concatenate([gvec[...], jnp.zeros((120, 768), F32)], axis=0)
    gbuf[:, R_VEC - R_HEAVY : R_DOWN - R_HEAVY] = vecs.T.astype(BF)
    gd = dot_tn(hid[...], da[...]).astype(BF)
    for r in range(8):
        for t in range(3):
            gbuf[96 * r + 32 * t : 96 * r + 32 * t + 32, R_DOWN - R_HEAVY : R_ALL - R_HEAVY] = gd[
                32 * r : 32 * r + 32, 256 * t : 256 * t + 256
            ]
    stores.send(gbuf.at[:, R_VEC - at : R_ALL - at], rest.at[:, R_VEC:R_ALL])
    stores.finish()


def tokens_kernel(got, st, lo, dxg, hl, hr, out, grad):
    back = dot(st[...], got[:, :, S_BACK:S_ALL].reshape(128, 1536))
    out[...] = (lo[...] + back[:, 0:768]).astype(BF)
    dx = dxg[...] + back[:, 768:1536]
    grad[0:64, :] = (dx[0:64, :] + hl[...].astype(F32)).astype(BF)
    grad[64:448, :] = dx[64:448, :].astype(BF)
    grad[448:512, :] = (dx[448:512, :] + hr[...].astype(F32)).astype(BF)


def tail_rows(block, low):
    last = jnp.concatenate([block[32 * t : 32 * t + 32, low + 768 : low + 1024] for t in range(3)], axis=1)
    return jnp.concatenate([block[:, low : low + 768], last], axis=0)


def owner_rows(r, cols):
    quarter = cols // 4
    row = lax.broadcasted_iota(jnp.int32, (128, 96), 0)
    col = lax.broadcasted_iota(jnp.int32, (128, 96), 1)
    device, low = 6 * (row >> 3), row & 7
    main = ((low < 6) & (col == device + low)).astype(F32).astype(BF)
    tail = r[:, 3 * quarter : cols]
    pieces = []
    for t in range(3):
        extra = ((low >= 6) & (col == device + 3 * (low - 6) + t)).astype(F32).astype(BF)
        pieces.append((dot(main, r[:, quarter * t : quarter * t + quarter]) + dot(extra, tail)).astype(BF))
    return jnp.concatenate(pieces, axis=1)


def tail_of(block):
    cols = block.shape[1] // 3
    return jnp.concatenate(
        [block[6 + n : 7 + n, cols * t : cols * t + cols] for n in range(2) for t in range(3)], axis=0
    )


def spread_ffn_kernel(r, send):
    send[:, 0:S_DOWN] = owner_rows(r, F_DOWN)
    send[:, S_DOWN:S_FFN] = tail_rows(r[...], F_DOWN)


def spread_rest_kernel(r, send_in, send, hd, rows, sems):
    rows[...] = owner_rows(r, R_ALL)
    copy = Copies(sems).start(rows, send.at[:, 0:S_BACK])
    hd[...] = jnp.concatenate([r[32 * t : 32 * t + 32, R_DOWN:R_ALL] for t in range(3)], axis=1)
    copy.wait()


def sum_parts(got, a, b):
    t = got[0, :, a:b].astype(F32)
    for d in range(1, 16):
        t = t + got[d, :, a:b].astype(F32)
    return t


def sum_ffn_kernel(got, gate, up, down):
    both = sum_parts(got, 0, S_DOWN)
    for c in range(3):
        gate[:, 256 * c : 256 * c + 256] = both[0:6, 512 * c : 512 * c + 256]
        up[:, 256 * c : 256 * c + 256] = both[0:6, 512 * c + 256 : 512 * c + 512]
    both = tail_of(both)
    gate[:, 768:1024] = both[:, 0:256]
    up[:, 768:1024] = both[:, 256:512]
    down[...] = sum_parts(got, S_DOWN, S_FFN)


def sum_rest_kernel(got, q, k, v, o, hq, hk, hv, ho, hgate, hup, vecs):
    total = sum_parts(got, 0, S_BACK)
    for n, ref in enumerate((q, k, v, o)):
        ref[...] = total[0:6, 768 * n : 768 * n + 768]
    rest = tail_of(total)
    ho[...] = rest[:, 128:896]
    rows = jnp.concatenate([rest[:, 896:1024], jnp.zeros((122, 128), F32)], axis=0).T
    for n, ref in enumerate(vecs):
        ref[...] = rows[n : n + 1, 0:6]
    at = R_HEAVY
    for j in range(16):
        hgate[:, 256 * j : 256 * j + 256] = got[j, :, at : at + 256].astype(F32)[0:6]
        hup[:, 256 * j : 256 * j + 256] = got[j, :, at + 256 : at + 512].astype(F32)[0:6]
    at = at + 512
    for p in range(6):
        two = [got[2 * p + n, :, 0:S_BACK].astype(F32) for n in range(2)]
        pair = two[0][:, R_HEAVY + 512 : R_HEAVY + 768] + two[1][:, R_HEAVY + 512 : R_HEAVY + 768]
        hq[:, 128 * p : 128 * p + 128] = pair[0:6, 0:128]
        hk[:, 128 * p : 128 * p + 128] = pair[0:6, 128:256]
        hv[:, 128 * p : 128 * p + 128] = tail_of(two[0] + two[1])[:, 0:128]


def last_kernel(
    got_in, st, lo_in, dxg_in, hl, hr,
    out, grad, q, k, v, o, hq, hk, hv, ho, hgate, hup, *rest,
):
    *vecs, got, lo, dxg, sems = rest
    copies = Copies(sems)
    pieces = [
        copies.start(got_in.at[:, :, a:b], got.at[:, :, a:b]) for a, b in ((0, S_BACK), (S_BACK, S_ALL))
    ]
    got_lo, got_dxg = copies.start(lo_in, lo), copies.start(dxg_in, dxg)
    pieces[0].wait()
    sum_rest_kernel(got, q, k, v, o, hq, hk, hv, ho, hgate, hup, vecs)
    pieces[1].wait()
    got_lo.wait()
    got_dxg.wait()
    tokens_kernel(got, st, lo, dxg, hl, hr, out, grad)


def call(kernel, outs, args, scratch=(), in_specs=None, out_specs=None, sems=(), name=None, us=0.05, aliases={}):
    return pl.pallas_call(
        kernel,
        out_shape=[jax.ShapeDtypeStruct(s, t) for s, t in outs],
        in_specs=in_specs or [VMEM] * len(args),
        out_specs=out_specs or [VMEM] * len(outs),
        scratch_shapes=[pltpu.VMEM(s, t) for s, t in scratch]
        + [pltpu.SemaphoreType.DMA((n,)) for n in sems],
        compiler_params=PARAMS,
        cost_estimate=pl.CostEstimate(
            flops=int(us * 1.0e9), bytes_accessed=int(us * 3.0e6), transcendentals=0
        ),
        input_output_aliases=aliases,
        name=name,
    )(*args)


def run_light_ffn(tokens, cotangent, wall):
    return call(
        light_ffn_kernel,
        [((512, 768), F32), ((512, 768), F32), ((768, F_ALL), BF), ((8, 768), F32), ((8, 768), F32)],
        (tokens, cotangent, wall),
        [
            ((512, 768), BF), ((512, 768), BF),
            ((768, 512), BF), ((512, 768), BF), ((768, 512), BF), ((768, 3072), BF),
            ((1024, 2048), BF), ((1024, 256), BF), ((1024, 128), BF), ((256, 768), BF),
        ],
        [HBM, HBM, HBM],
        [VMEM, VMEM, HBM, VMEM, VMEM],
        sems=(11, 8),
        name="light_ffn",
        us=200,
    )


def run_light_attn(meta, xl, tokens, xr, cotangent, wall, ffn, cf, gvec, vrows):
    return call(
        light_attn_kernel,
        [
            ((512, 768), F32), ((512, 768), F32), ((128, 768), BF), ((768, R_ALL), BF), ((8, 768), F32),
            ((128, 768), BF),
        ],
        (meta, xl, tokens, xr, cotangent, wall, ffn, cf, gvec, vrows),
        [
            ((768, 3072), BF), ((640, 768), BF), ((640, 768), BF), ((768, 640), BF), ((640, 2304), BF),
            ((512, 768), BF), ((512, 768), BF), ((640, 2304), BF),
            ((640, 768), F32), ((640, 768), F32), ((4, 256, 256), F32),
            ((1024, 3072), BF), ((512, 768), BF), ((512, 768), F32), ((512, 768), F32),
            ((512, 768), F32), ((640, 768), F32), ((768, 3072), BF),
        ],
        [SMEM, VMEM, HBM, VMEM, HBM] + [HBM] * 3 + [VMEM, VMEM],
        [HBM, VMEM, VMEM, HBM, VMEM, VMEM],
        sems=(8, 5),
        name="light_attn",
        us=2,
    )


def run_heavy(meta, xg, hw, wo, kmask, gvec, vrows, rest):
    col = ((1024, 1), F32)
    rows, narrow = ((1024, 768), BF), ((1024, 128), BF)
    return call(
        heavy_kernel,
        [((256, 768), BF)] * 8 + [((768, R_ALL), BF)],
        (meta, xg, hw, wo, kmask, gvec, vrows, rest),
        [
            ((1024, 1536), BF), ((768, 896), BF), ((256, 768), BF), rows, rows,
            narrow, narrow, narrow, narrow, narrow, ((1024, 384), BF),
            ((1024, 128), F32), ((1024, 128), F32), ((1024, 256), F32),
            rows, ((1024, 512), BF), ((1024, 256), BF), col, col, col,
            ((8, 160, 896), BF), rows, rows, ((768, R_ALL - R_HEAVY), BF), ((8, 768), F32),
        ],
        [SMEM, HBM, HBM, VMEM, HBM, VMEM, VMEM, HBM],
        [HBM] * 9,
        sems=(3, 11),
        aliases={7: 8},
        name="heavy",
        us=200,
    )


def body(
    tokens, lengths, routed, cotangent, gain_attn, gain_ffn, router_attn, router_ffn,
    light_q, light_k, light_v, light_o, light_gate, light_up, light_down,
    heavy_q, heavy_k, heavy_v, heavy_o, heavy_gate, heavy_up, heavy_down,
):
    me = lax.axis_index("fsdp")
    vectors = [v.reshape(1, 6) for v in (gain_attn, gain_ffn, router_attn, router_ffn)]
    pack, hsend, hd = call(
        prep_kernel,
        [((8, C_ALL), BF), ((16, 8, 896), BF), ((32, 768), BF)],
        (
            light_q, light_k, light_v, light_o, light_gate, light_up, light_down,
            heavy_q, heavy_k, heavy_v, heavy_o, heavy_gate, heavy_up, heavy_down, *vectors,
        ),
        [((8, C_ALL), F32), ((128, 128), F32), ((8, 4096), F32)],
        name="prep",
    )
    wall = lax.all_gather(pack, ALL, axis=0, tiled=True)

    hcols = lax.all_to_all(hsend, "fsdp", split_axis=0, concat_axis=0, tiled=True)
    hd = lax.ppermute(hd, ALL, [(d, (d % 8) * 16 + d // 8) for d in range(128)])
    hblock = jnp.concatenate([hcols.reshape(128, 896), jnp.pad(hd, ((0, 0), (0, 128)))], axis=0)

    edges = jnp.arange(17, dtype=jnp.int32) * 512
    bounds = jnp.sum((routed[0][None, :] < edges[:, None]).astype(jnp.int32), axis=1)
    dp = lax.axis_index("dp")
    pair = jnp.where(me < 12, me // 2, 5)
    meta = jnp.concatenate(
        [
            bounds,
            jnp.stack(
                [
                    lengths[0, 0] // 8, 128 * pair, jnp.where(me < 12, me % 2, 2),
                    me, dp // 2, dp % 2, lengths[0, 0],
                ]
            ),
        ]
    )

    def swap(rows):
        return lax.all_to_all(rows, "fsdp", split_axis=0, concat_axis=0, tiled=True)

    slots, st = call(
        slots_kernel,
        [((128, 1536), BF), ((512, 128), BF)],
        (meta, routed, tokens, cotangent),
        in_specs=[SMEM, VMEM, VMEM, VMEM],
        name="slots",
    )
    own, many, kmask = call(
        entries_kernel,
        [((64, 1536), BF), ((16, 64, 1536), BF), ((1024, 256), F32)],
        (meta, swap(slots.reshape(16, 8, 1536)).reshape(128, 1536)),
        in_specs=[SMEM, VMEM],
        name="entries",
    )
    right = [(i, i + 1) for i in range(15)]
    left = [(i + 1, i) for i in range(15)]
    xl = lax.ppermute(tokens[448:512], "fsdp", right)
    xr = lax.ppermute(tokens[0:64], "fsdp", left)

    wall, many, xl, xr, hblock = lax.optimization_barrier((wall, many, xl, xr, hblock))
    hw = lax.all_gather(hblock, "dp", axis=0, tiled=False)
    xg = swap(many).reshape(1024, 1536)
    ffn, cf, grad_ffn, gvec, vrows = run_light_ffn(tokens, cotangent, wall)
    rs_ffn = lax.psum_scatter(grad_ffn, "dp", scatter_dimension=0, tiled=True)
    lmeta = jnp.concatenate([jnp.stack([lengths[0, 0], me * 512, jnp.int32(8192)]), meta[18:20]])
    lo, dxg, halo, rest, gvec, heavy_wo = run_light_attn(
        lmeta, xl, tokens, xr, cotangent, wall, ffn, cf, gvec, vrows
    )
    *partial, rest = run_heavy(meta, xg, hw, heavy_wo, kmask, gvec, vrows, rest)
    rs_rest = lax.psum_scatter(rest, "dp", scatter_dimension=0, tiled=True)

    def along(blocks, x, y):
        moved = [
            lax.ppermute(
                block, "fsdp", [(i, (i // 4 + n * x) % 4 * 4 + (i % 4 + n * y) % 4) for i in range(16)]
            )
            for n, block in enumerate(blocks[1:], 1)
        ]
        return [blocks[0]] + moved

    blocks = call(
        first_sum_kernel,
        [((64, 768), BF)] * 8,
        (meta, *along(partial[0:4], 1, 0), *along(partial[4:8], 0, 1)),
        in_specs=[SMEM] + [VMEM] * 8,
        name="first_sum",
    )
    blocks = along(blocks[0:4], 0, 1) + along(blocks[4:8], 1, 0)
    hr = lax.ppermute(halo[0:64], "fsdp", left)
    hl = lax.ppermute(halo[64:128], "fsdp", right)
    (send_ffn,) = call(spread_ffn_kernel, [((128, S_FFN), BF)], (rs_ffn,), name="spread_ffn")
    got_ffn = swap(send_ffn.reshape(16, 8, S_FFN))
    *blocks, got_ffn, hr, hl = lax.optimization_barrier((*blocks, got_ffn, hr, hl))
    (send,) = call(
        home_kernel,
        [((128, S_ALL), BF)],
        (meta, *blocks, own),
        [((128, 1536), BF)],
        [SMEM] + [VMEM] * 9,
        [HBM],
        sems=(1,),
        name="home",
    )
    send, g_hd = call(
        spread_rest_kernel,
        [((128, S_ALL), BF), ((32, 768), BF)],
        (rs_rest, send),
        [((128, S_BACK), BF)],
        [VMEM, HBM],
        [HBM, VMEM],
        sems=(1,),
        name="spread_rest",
        aliases={1: 0},
    )
    g_hd = lax.ppermute(g_hd, ALL, [((d % 8) * 16 + d // 8, d) for d in range(128)])
    got = swap(send.reshape(16, 8, S_ALL))
    six, four, big = ((6, 768), F32), ((6, 1024), F32), ((6, 4096), F32)
    g_gate, g_up, g_down = call(
        sum_ffn_kernel, [four, four, ((8, 768), F32)], (got_ffn,), name="sum_ffn"
    )
    output, grad_tokens, g_q, g_k, g_v, g_o, g_hq, g_hk, g_hv, g_ho, g_hgate, g_hup, *g_vecs = call(
        last_kernel,
        [((512, 768), BF), ((512, 768), BF)] + [six] * 8 + [big, big] + [((1, 6), F32)] * 4,
        (got, st, lo, dxg, hl, hr),
        [((16, 8, S_ALL), BF), ((512, 768), F32), ((512, 768), F32)],
        [HBM, VMEM, HBM, HBM, VMEM, VMEM],
        sems=(4,),
        name="last",
    )
    return (
        output, grad_tokens,
        *[v.reshape(6) for v in g_vecs],
        g_q, g_k, g_v, g_o, g_gate, g_up, g_down,
        g_hq, g_hk, g_hv, g_ho, g_hgate, g_hup, g_hd.astype(F32),
    )


def solution(mesh):
    rows = P(ALL, None)
    flat = P(ALL)
    in_specs = (rows, P("dp", None), P("dp", None), rows) + (flat,) * 4 + (rows,) * 14
    out_specs = (rows, rows) + (flat,) * 4 + (rows,) * 14
    return jax.shard_map(body, mesh=mesh, in_specs=in_specs, out_specs=out_specs, check_vma=False)
```

```python
import jax
import jax.numpy as jnp
from jax import lax
from jax.experimental import pallas as pl
from jax.experimental.pallas import tpu as pltpu
from jax.sharding import PartitionSpec as P

BF = jnp.bfloat16
F32 = jnp.float32
EPS = 1e-6
NEG = -1e30
ALL = ("dp", "fsdp")
CAP = 96
LIGHT_SCALE = 96**-0.5
HEAVY_SCALE = 64**-0.5
PARAMS = pltpu.CompilerParams(vmem_limit_bytes=63 * 1024 * 1024)
SMEM = pl.BlockSpec(memory_space=pltpu.SMEM)
VMEM = pl.BlockSpec(memory_space=pltpu.VMEM)
HBM = pl.BlockSpec(memory_space=pl.ANY)

C_QKVO, C_VEC, C_DOWN, C_ALL = 2048, 5120, 5248, 5504
F_DOWN, F_ALL = 2048, 3072
R_HEAVY, R_HO, R_VEC, R_DOWN, R_ALL = 3072, 3968, 4736, 4864, 5120
S_DOWN, S_FFN = 1536, 2304
S_BACK, S_ALL = 3840, 5376

def dot(a, b):
    return jnp.dot(a, b, preferred_element_type=F32)


def dot_nt(a, b):
    return lax.dot_general(a, b, (((1,), (1,)), ((), ())), preferred_element_type=F32)


def dot_tn(a, b):
    return lax.dot_general(a, b, (((0,), (0,)), ((), ())), preferred_element_type=F32)


def pick6(rows, cols, shift=0):
    r = lax.broadcasted_iota(jnp.int32, (rows, cols), 0) + shift
    c = lax.broadcasted_iota(jnp.int32, (rows, cols), 1)
    low = c & 7
    return ((6 * (c >> 3) + low == r) & (low < 6)).astype(F32).astype(BF)


def unpad_rows(ref, out_ref, pick, at=0, width=None):
    width = width or ref.shape[1]
    for b in range(8):
        block = dot(pick, ref[128 * b : 128 * b + 128, at : at + width])
        out_ref[96 * b : 96 * b + 96, at : at + width] = block.astype(BF)


def vector_rows(vec_ref, pick):
    blocks = [dot(pick, vec_ref[128 * b : 128 * b + 128, :]) for b in range(8)]
    return jnp.concatenate(blocks, axis=0).T


class Copies:
    def __init__(self, sems, used=0):
        self.sems, self.used, self.open = sems, used, []

    def start(self, src, dst):
        copy = pltpu.make_async_copy(src, dst, self.sems.at[self.used])
        self.used += 1
        copy.start()
        return copy

    def send(self, src, dst):
        self.open.append(self.start(src, dst))

    def finish(self):
        for copy in self.open:
            copy.wait()


def unit(rows):
    scale = lax.rsqrt(jnp.mean(rows * rows, axis=-1, keepdims=True) + EPS)
    return rows * scale, scale


def gelu_parts(gate):
    c0, c1 = 0.7978845608, 0.044715
    sq = gate * gate
    t = jnp.tanh(gate * (c0 + (c0 * c1) * sq))
    half = 0.5 * (1.0 + t)
    slope = half + (0.5 * gate) * (1.0 - t * t) * (c0 + (3.0 * c0 * c1) * sq)
    return gate * half, slope


def prep_kernel(
    q, k, v, o, gate, up, down, hq, hk, hv, ho, hgate, hup, hdown, ga, gf, ra, rf, pack, hsend, hd, scr, rows, wide
):
    scr[...] = jnp.zeros_like(scr)
    zero128 = jnp.zeros((8, 128), BF)
    for c in range(4):
        cols = slice(256 * c, 256 * c + 256)
        scr[0:6, 512 * c : 512 * c + 256] = gate[:, cols]
        scr[0:6, 512 * c + 256 : 512 * c + 512] = up[:, cols]
    for n, ref in enumerate((q, k, v, o)):
        scr[0:6, C_QKVO + 768 * n : C_QKVO + 768 * n + 768] = ref[...]
    for a in range(2):
        for b in range(4):
            scr[6 + a : 7 + a, 512 * b : 512 * b + 512] = down[4 * a + b : 4 * a + b + 1, 0:512]
        for b in range(3):
            at = C_QKVO + 768 * b
            scr[6 + a : 7 + a, at : at + 768] = ho[3 * a + b : 3 * a + b + 1, :]
    scr[:, C_DOWN:C_ALL] = down[:, 512:768]
    rows[...] = jnp.zeros_like(rows)
    for n, ref in enumerate((ga, gf, ra, rf)):
        rows[n : n + 1, 0:6] = ref[...]
    scr[:, C_VEC : C_VEC + 128] = rows[...].T[0:8, :]
    pack[...] = scr[...].astype(BF)
    wide[...] = jnp.zeros_like(wide)

    def padded(ref):
        cols = ref.shape[1]
        wide[0:6, 0:cols] = ref[...]
        return wide[:, 0:cols].astype(BF)

    wq, wk, wv = padded(hq), padded(hk), padded(hv)
    wg, wu = padded(hgate), padded(hup)
    for j in range(16):
        hsend[j, :, 0:256] = wg[:, 256 * j : 256 * j + 256]
        hsend[j, :, 256:512] = wu[:, 256 * j : 256 * j + 256]
        for n, w in enumerate((wq, wk, wv)):
            p = j // 2
            part = w[:, 128 * p : 128 * p + 128] if j < 12 else zero128
            hsend[j, :, 512 + 128 * n : 640 + 128 * n] = part
    hd[...] = hdown[...].astype(BF)


def light_ffn_kernel(
    x_in, g_in, wall, ffn, cf, light, gvec, vrows, x, g, gu, fin, fin_t, gbuf, gu_pad, down, vec, wd, in_sems, out_sems
):
    def wide(c, at=0):
        return pl.ds(pl.multiple_of(at + 512 * c, 128), 512)

    def loads(c):
        rows = pl.ds(pl.multiple_of(256 * c, 256), 256)
        yield pltpu.make_async_copy(wall.at[:, wide(c)], gu_pad.at[:, wide(c)], in_sems.at[2 * c])
        yield pltpu.make_async_copy(
            wall.at[rows, C_DOWN:C_ALL], down.at[rows, :], in_sems.at[2 * c + 1]
        )

    def stores(c):
        rows = pl.ds(pl.multiple_of(192 * c, 64), 192)
        yield pltpu.make_async_copy(gbuf.at[:, wide(c)], light.at[:, wide(c)], out_sems.at[2 * c])
        yield pltpu.make_async_copy(
            gbuf.at[rows, 2048:3072], light.at[rows, F_DOWN:F_ALL], out_sems.at[2 * c + 1]
        )

    first = Copies(in_sems, 8)
    got_x = first.start(x_in, x)
    got_vec = first.start(wall.at[:, C_VEC : C_VEC + 128], vec)
    got_g = first.start(g_in, g)
    for c in range(4):
        for copy in loads(c):
            copy.start()
    pick = pick6(96, 128)
    got_x.wait()
    u, _ = unit(x[...].astype(F32))
    got_vec.wait()
    vrows[...] = vector_rows(vec, pick)[0:8, :]
    gain_f = vrows[1:2, :]
    f = (u * gain_f).astype(BF)
    fin[...] = f
    fin_t[...] = f.T
    ffn[...] = jnp.zeros_like(ffn)
    cf[...] = jnp.zeros_like(cf)
    got_g.wait()

    for c in range(4):
        for copy in loads(c):
            copy.wait()
    out_row = lax.broadcasted_iota(jnp.int32, (256, 256), 0)
    in_row = lax.broadcasted_iota(jnp.int32, (256, 256), 1)
    spare = (out_row & ~7) + 6 + ((out_row >> 2) & 1) == in_row
    spread = [(spare & ((out_row & 3) == b)).astype(F32).astype(BF) for b in range(4)]

    @pl.loop(0, 4)
    def _(c):
        for b in range(8):
            block = dot(pick, gu_pad[128 * b : 128 * b + 128, wide(c)])
            gu[96 * b : 96 * b + 96, :] = block.astype(BF)
        w = gu[...]
        rows = pl.ds(pl.multiple_of(256 * c, 256), 256)
        left = dot(spread[0], gu_pad[rows, 0:512])
        for b in range(1, 4):
            left = left + dot(spread[b], gu_pad[rows, 512 * b : 512 * b + 512])
        wd[:, 0:512] = left.astype(BF)
        wd[:, 512:768] = down[rows, :]
        both = dot(fin[...], w)
        act, slope = gelu_parts(both[:, 0:256])
        up = both[:, 256:512]
        hidden = (act * up).astype(BF)
        dh = dot_nt(g[...], wd[...])
        dgu = jnp.concatenate([(dh * up * slope).astype(BF), (dh * act).astype(BF)], axis=1)
        ffn[...] += dot(hidden, wd[...])
        cf[...] += dot_nt(dgu, w)
        gbuf[:, wide(c)] = dot(fin_t[...], dgu).astype(BF)
        gd = dot_tn(hidden, g[...]).astype(BF)
        for n in range(2):
            r0 = 128 * n
            at = pl.multiple_of(192 * c + 96 * n, 32)
            gbuf[pl.ds(at, 96), 2048:2816] = gd[r0 : r0 + 96, :]
            for t in range(3):
                gbuf[pl.ds(pl.multiple_of(at + 32 * t, 32), 32), 2816:3072] = gd[
                    r0 + 96 : r0 + 128, 256 * t : 256 * t + 256
                ]
        for copy in stores(c):
            copy.start()

    u, _ = unit(x[...].astype(F32))
    d_f = cf[...]
    gvec[...] = jnp.zeros_like(gvec)
    gvec[1:2, :] = jnp.sum(d_f * u, axis=0, keepdims=True)
    cf[...] = d_f * gain_f
    for c in range(4):
        for copy in stores(c):
            copy.wait()


def light_attn_kernel(
    meta, xl, x_in, xr, g_in, wall, ffn_in, cf_in, gin, vrows,
    lo, dxg, to_left, to_right, rest, gvec, heavy_wo,
    w, xs, a, a_t, qkv, o, do, dqkv, dk, dv, mask, w_pad, g, ffn, cf, lo_buf, d_a, gbuf, in_sems, out_sems,
):
    def wide(n, at=0):
        return pl.ds(pl.multiple_of(at + 768 * n, 128), 768)

    def load(n):
        return pltpu.make_async_copy(wall.at[:, wide(n, C_QKVO)], w_pad.at[:, wide(n)], in_sems.at[n])

    def store(n):
        return pltpu.make_async_copy(gbuf.at[:, wide(n)], rest.at[:, wide(n)], out_sems.at[n])

    loads, stores = Copies(in_sems, 4), Copies(out_sems, 4)
    x = xs.at[64:576, :]
    got_x = loads.start(x_in, x)
    for n in range(4):
        load(n).start()
    got_g = loads.start(g_in, g)
    got_ffn = loads.start(ffn_in, ffn)
    got_cf = loads.start(cf_in, cf)
    pick = pick6(96, 128)
    xs[0:64, :] = xl[...]
    xs[576:640, :] = xr[...]
    first, base, pack_len = meta[0], meta[1], meta[2]
    key = lax.broadcasted_iota(jnp.int32, (256, 256), 0)
    qry = lax.broadcasted_iota(jnp.int32, (256, 256), 1) & 127
    gap = key - qry

    @pl.loop(0, 4)
    def _(b):
        qpos = base + 128 * b + qry
        kpos = base + 128 * b - 64 + key
        ok = (gap >= 0) & (gap <= 128) & ((qpos < first) == (kpos < first))
        ok = ok & (kpos >= 0) & (kpos < pack_len)
        mask[b] = jnp.where(ok, 0.0, NEG)

    dk[...] = jnp.zeros_like(dk)
    dv[...] = jnp.zeros_like(dv)
    dqkv[0:64, 0:768] = jnp.zeros((64, 768), BF)
    dqkv[576:640, 0:768] = jnp.zeros((64, 768), BF)
    got_x.wait()
    u, _ = unit(xs[...].astype(F32))
    gain_a = vrows[0:1, :]
    a[...] = (u * gain_a).astype(BF)

    def unpad(n):
        load(n).wait()
        for b in range(8):
            w[96 * b : 96 * b + 96, wide(n)] = dot(pick, w_pad[128 * b : 128 * b + 128, wide(n)]).astype(BF)

    @pl.loop(0, 3)
    def _(n):
        unpad(n)
        qkv[:, wide(n)] = dot(a[...], w[:, wide(n)]).astype(BF)

    unpad(3)
    got_g.wait()
    do[...] = dot_nt(g[...], w[:, 2304:3072]).astype(BF)

    row = lax.broadcasted_iota(jnp.int32, (128, 1024), 0)
    col = lax.broadcasted_iota(jnp.int32, (128, 1024), 1)
    entry = 6 * (col >> 3) + 3 * ((col & 7) - 6)
    keep = ((col & 7) >= 6) & ((row >> 6) == meta[4])
    wo = jnp.zeros((128, 768), F32)
    for b in range(3):
        take = (keep & (entry + b == row + meta[3])).astype(F32).astype(BF)
        wo = wo + dot(take, w_pad[:, 768 * b : 768 * b + 768])
    heavy_wo[...] = wo.astype(BF)

    lane = lax.broadcasted_iota(jnp.int32, (128, 256), 1)

    def pair(b, group, second):
        low = 64 * second
        even = (lane >= low) & (lane < low + 96)
        odd = (lane >= low + 96) & (lane < low + 192)

        def split(t):
            zero = jnp.zeros_like(t)
            return jnp.concatenate([jnp.where(even, t, zero), jnp.where(odd, t, zero)], axis=0)

        def join(t):
            return jnp.where(even, t[0:128], 0.0) + jnp.where(odd, t[128:256], 0.0)

        def win(part):
            return pl.ds(pl.multiple_of(768 * part + 384 * group + 128 * second, 128), 256)

        rq = pl.ds(pl.multiple_of(128 * b, 128), 128)
        rd = pl.ds(pl.multiple_of(128 * b + 64, 64), 128)
        rk = pl.ds(pl.multiple_of(128 * b, 128), 256)
        kw, vw = qkv[rk, win(1)], qkv[rk, win(2)]
        q2, do2 = split(qkv[rd, win(0)]), split(do[rq, win(0)])
        s = dot_nt(kw, q2) * LIGHT_SCALE + mask[b]
        dp = dot_nt(vw, do2)
        e = jnp.exp(s - jnp.max(s, axis=0, keepdims=True))
        p = e * (1.0 / jnp.sum(e, axis=0, keepdims=True))
        pb = p.astype(BF)
        ds = (p * (dp - jnp.sum(p * dp, axis=0, keepdims=True))).astype(BF)
        dk[rk, win(0)] += dot(ds, q2) * LIGHT_SCALE
        dv[rk, win(0)] += dot(pb, do2)
        return join(dot_tn(pb, vw)), join(dot_tn(ds, kw)) * LIGHT_SCALE

    @pl.loop(0, 8)
    def _(i):
        b, group = i >> 1, i & 1
        rq = pl.ds(pl.multiple_of(128 * b, 128), 128)
        rd = pl.ds(pl.multiple_of(128 * b + 64, 64), 128)
        o0, dq0 = pair(b, group, 0)
        o1, dq1 = pair(b, group, 1)

        def tile(n):
            return pl.ds(pl.multiple_of(384 * group + 128 * n, 128), 128)

        for ref, rows, t0, t1 in ((o, rq, o0, o1), (dqkv, rd, dq0, dq1)):
            ref[rows, tile(0)] = t0[:, 0:128].astype(BF)
            ref[rows, tile(1)] = (t0[:, 128:256] + t1[:, 0:128]).astype(BF)
            ref[rows, tile(2)] = t1[:, 128:256].astype(BF)

    got_ffn.wait()
    lo_buf[...] = x[...].astype(F32) + ffn[...] + dot(o[...], w[:, 2304:3072])
    stores.send(lo_buf, lo)
    gbuf[:, 2304:3072] = dot_tn(o[...], g[...]).astype(BF)
    store(3).start()
    dqkv[:, 768:1536] = dk[...].astype(BF)
    dqkv[:, 1536:2304] = dv[...].astype(BF)
    a_t[...] = a[...].T
    d_a[...] = jnp.zeros_like(d_a)

    @pl.loop(0, 3)
    def _(n):
        part = dqkv[:, wide(n)]
        gbuf[:, wide(n)] = dot(a_t[...], part).astype(BF)
        store(n).start()
        d_a[...] += dot_nt(part, w[:, wide(n)])

    u, scale = unit(xs[...].astype(F32))
    c = d_a[...]
    gvec[...] = gin[...]
    gvec[0:1, :] = jnp.sum(c * u, axis=0, keepdims=True)
    c = c * gain_a
    got_cf.wait()

    def norm_back(c, rows):
        ur = u[rows]
        return scale[rows] * (c - ur * jnp.mean(ur * c, axis=-1, keepdims=True))

    own = slice(64, 576)
    dxg[...] = norm_back(c[own] + cf[...], own) + g[...].astype(F32)
    to_left[...] = norm_back(c[0:64], slice(0, 64)).astype(BF)
    to_right[...] = norm_back(c[576:640], slice(576, 640)).astype(BF)
    stores.finish()
    for n in range(4):
        store(n).wait()


def slots_kernel(meta, routed, x, g, slots, st):
    me = meta[20]
    start = meta[me]
    token = lax.broadcasted_iota(jnp.int32, (512, 1024), 0) + 512 * me
    r = jnp.broadcast_to(routed[...], (512, 1024))
    rank = jnp.sum((r < token).astype(F32), axis=1, keepdims=True).astype(jnp.int32) - start
    hit = jnp.sum((r == token).astype(F32), axis=1, keepdims=True)
    row = ((start + rank) & 15) * 8 + (rank >> 4)
    row = jnp.where((hit > 0.5) & (rank < CAP), row, -1)
    lane = lax.broadcasted_iota(jnp.int32, (512, 128), 1)
    onehot = (lane == row).astype(F32).astype(BF)
    st[...] = onehot
    slots[:, 0:768] = dot_tn(onehot, x[...]).astype(BF)
    slots[:, 768:1536] = dot_tn(onehot, g[...]).astype(BF)


def entry_slots(meta):
    p = 16 * lax.broadcasted_iota(jnp.int32, (64, 128), 0) + meta[20]
    source, before = jnp.zeros_like(p), jnp.zeros_like(p)
    for d in range(1, 16):
        source = source + (p >= meta[d]).astype(jnp.int32)
        before = jnp.where(p >= meta[d], meta[d], before)
    rank = p - before
    lane = lax.broadcasted_iota(jnp.int32, (64, 128), 1)
    return ((lane == source * 8 + (rank >> 4)) & (rank < CAP)).astype(F32).astype(BF)


def entries_kernel(meta, got, own, many, kmask):
    entry = entry_of(lax.broadcasted_iota(jnp.int32, (1024, 128), 0))
    bias = jnp.zeros((1024, 128), F32)
    for d in range(16):
        bias = jnp.where((entry >= meta[d] + CAP) & (entry < meta[d + 1]), NEG, bias)
    kmask[:, 0:128] = jnp.where(entry < meta[17], bias, NEG)
    kmask[:, 128:256] = jnp.where(entry < meta[17], NEG, bias)
    rows = dot(entry_slots(meta), got[...]).astype(BF)
    own[...] = rows
    for t in range(16):
        many[t] = rows


def first_sum_kernel(meta, y0, y1, y2, y3, c0, c1, c2, c3, *outs):
    for n in range(4):
        for here, parts, out in (
            (meta[20] & 3, (y0, y1, y2, y3), outs[n]), (meta[20] >> 2, (c0, c1, c2, c3), outs[4 + n])
        ):
            rows = pl.ds(pl.multiple_of(64 * ((here + n) & 3), 64), 64)
            total = parts[0][rows, :].astype(F32)
            for part in parts[1:]:
                total = total + part[rows, :].astype(F32)
            out[...] = total.astype(BF)


def home_kernel(meta, y0, y1, y2, y3, c0, c1, c2, c3, own, send, back, sems):
    y, c = (
        a[...].astype(F32) + b[...].astype(F32) + d[...].astype(F32) + e[...].astype(F32)
        for a, b, d, e in ((y0, y1, y2, y3), (c0, c1, c2, c3))
    )
    onehot = entry_slots(meta)
    u, scale = unit(own[:, 0:768].astype(F32))
    dxr = scale * (c - u * jnp.mean(u * c, axis=-1, keepdims=True))
    back[:, 0:768] = dot_tn(onehot, y.astype(BF)).astype(BF)
    back[:, 768:1536] = dot_tn(onehot, dxr.astype(BF)).astype(BF)
    Copies(sems).start(back, send.at[:, S_BACK:S_ALL]).wait()


def entry_of(row):
    return ((row & 63) << 4) + (row >> 6)


def heavy_kernel(
    meta, xg_in, hw_in, wo, kmask_in, gin, vrows, rest_in,
    y0, y1, y2, y3, c0, c1, c2, c3, rest,
    xg, w, wd, ar, fr, q, k, v, o, do, dqkv, dk, dv, kmask, da, dgu, hid, sa, sf, la,
    hw, ybuf, cbuf, gbuf, gvec, in_sems, out_sems,
):
    loads, stores = Copies(in_sems), Copies(out_sems)
    got_hw = loads.start(hw_in, hw)
    got_xg = loads.start(xg_in, xg)
    got_kmask = loads.start(kmask_in, kmask)
    pick = pick6(96, 128)
    gain_a, gain_f, r_a, r_f = (vrows[n : n + 1, :] for n in range(4))
    got_hw.wait()
    for b in range(8):
        w[96 * b : 96 * b + 96, :] = dot(pick, hw[b, 0:128, :]).astype(BF)
        wd[32 * b : 32 * b + 32, :] = hw[b, 128:160, 0:768]
    low, head = meta[18], meta[19]
    on = (lax.broadcasted_iota(jnp.int32, (256, 128), 1) >> 6) == head
    got_xg.wait()

    @pl.loop(0, 4)
    def _(b):
        rows = pl.ds(pl.multiple_of(256 * b, 256), 256)
        u, _ = unit(xg[rows, 0:768].astype(F32))
        arb, frb = (u * gain_a).astype(BF), (u * gain_f).astype(BF)
        ar[rows, :], fr[rows, :] = arb, frb
        sab = jax.nn.sigmoid(jnp.sum(arb.astype(F32) * r_a, axis=-1, keepdims=True))
        sfb = jax.nn.sigmoid(jnp.sum(frb.astype(F32) * r_f, axis=-1, keepdims=True))
        sa[rows, :], sf[rows, :] = sab, sfb
        qkv = dot(arb, w[:, 512:896])
        q[rows, :] = jnp.where(on, qkv[:, 0:128] * HEAVY_SCALE, 0.0).astype(BF)
        k[rows, :] = qkv[:, 128:256].astype(BF)
        v[rows, :] = jnp.where(on, qkv[:, 256:384], 0.0).astype(BF)
        dab = (sab * xg[rows, 768:1536].astype(F32)).astype(BF)
        da[rows, :] = dab
        do[rows, :] = dot_nt(dab, wo[...]).astype(BF)

    got_kmask.wait()
    n0 = meta[17]
    dk[...] = jnp.zeros_like(dk)
    dv[...] = jnp.zeros_like(dv)

    @pl.loop(0, 4, unroll=2)
    def _(b):
        rows = pl.ds(pl.multiple_of(256 * b, 256), 256)
        first = entry_of(lax.broadcasted_iota(jnp.int32, (1, 128), 1) + 256 * b) < n0
        second = entry_of(lax.broadcasted_iota(jnp.int32, (1, 128), 1) + 256 * b + 128) < n0
        bias = jnp.concatenate(
            [jnp.where(first, kmask[:, 0:128], kmask[:, 128:256]),
             jnp.where(second, kmask[:, 0:128], kmask[:, 128:256])],
            axis=1,
        )
        qb, dob = q[rows, :], do[rows, :]
        s = dot_nt(k[...], qb) + bias
        e = jnp.exp(s - jnp.max(s, axis=0, keepdims=True))
        p = e * (1.0 / jnp.sum(e, axis=0, keepdims=True))
        pb = p.astype(BF)
        ob = dot_tn(pb, v[...]).astype(BF)
        o[rows, :] = ob
        la[rows, :] = (1.0 - sa[rows, :]) * jnp.sum(
            ob.astype(F32) * dob.astype(F32), axis=-1, keepdims=True
        )
        dp = dot_nt(v[...], dob)
        ds = (p * (dp - jnp.sum(p * dp, axis=0, keepdims=True))).astype(BF)
        dqkv[rows, 0:128] = jnp.where(on, dot_tn(ds, k[...]) * HEAVY_SCALE, 0.0).astype(BF)
        dk[...] += dot(ds, qb)
        dv[...] += dot(pb, dob)

    dqkv[:, 128:256] = dk[...].astype(BF)
    dqkv[:, 256:384] = dv[...].astype(BF)
    gbuf[:, 512:896] = dot_tn(ar[...], dqkv[...]).astype(BF)
    gbuf[:, R_HO - R_HEAVY : R_VEC - R_HEAVY] = jnp.zeros((768, 768), BF)
    gbuf[pl.ds(pl.multiple_of(low, 128), 128), R_HO - R_HEAVY : R_VEC - R_HEAVY] = dot_tn(o[...], da[...]).astype(BF)
    at = R_HEAVY
    stores.send(gbuf.at[:, 512 : R_VEC - at], rest.at[:, at + 512 : R_VEC])
    gvec[...] = gin[...]

    @pl.loop(0, 4, unroll=2)
    def _(b):
        rows = pl.ds(pl.multiple_of(256 * b, 256), 256)
        frb = fr[rows, :]
        sfb = sf[rows, :]
        dfb = (sfb * xg[rows, 768:1536].astype(F32)).astype(BF)
        both = dot(frb, w[:, 0:512])
        act, slope = gelu_parts(both[:, 0:256])
        up = both[:, 256:512]
        hidden = (act * up).astype(BF)
        hid[rows, :] = hidden
        dh = dot_nt(dfb, wd[...])
        lfb = (1.0 - sfb) * jnp.sum(hidden.astype(F32) * dh, axis=-1, keepdims=True)
        dgub = jnp.concatenate([(dh * up * slope).astype(BF), (dh * act).astype(BF)], axis=1)
        dgu[rows, :] = dgub
        y = sa[rows, :] * dot(o[rows, :], wo[...]) + sfb * dot(hidden, wd[...])
        lab = la[rows, :]
        d_f = dot_nt(dgub, w[:, 0:512]) + lfb * r_f
        d_a = dot_nt(dqkv[rows, :], w[:, 512:896]) + lab * r_a
        u, _ = unit(xg[rows, 0:768].astype(F32))
        gvec[0:1, :] += jnp.sum(d_a * u, axis=0, keepdims=True)
        gvec[1:2, :] += jnp.sum(d_f * u, axis=0, keepdims=True)
        gvec[2:3, :] += jnp.sum(lab * ar[rows, :].astype(F32), axis=0, keepdims=True)
        gvec[3:4, :] += jnp.sum(lfb * frb.astype(F32), axis=0, keepdims=True)
        da[rows, :] = dfb
        ybuf[rows, :] = y.astype(BF)
        c = (d_a * gain_a + d_f * gain_f).astype(BF)
        for t in range(4):
            cbuf[pl.ds(pl.multiple_of(256 * t + 64 * b, 64), 64), :] = c[64 * t : 64 * t + 64]

    for n, (yk, ck) in enumerate(((y0, c0), (y1, c1), (y2, c2), (y3, c3))):
        to_x = ((meta[20] >> 2) + n) & 3
        to_y = ((meta[20] & 3) + n) & 3
        stores.send(ybuf.at[pl.ds(pl.multiple_of(256 * to_x, 256), 256), :], yk)
        stores.send(cbuf.at[pl.ds(pl.multiple_of(256 * to_y, 256), 256), :], ck)

    gbuf[:, 0:512] = dot_tn(fr[...], dgu[...]).astype(BF)
    stores.send(gbuf.at[:, 0:512], rest.at[:, at : at + 512])
    vecs = jnp.concatenate([gvec[...], jnp.zeros((120, 768), F32)], axis=0)
    gbuf[:, R_VEC - R_HEAVY : R_DOWN - R_HEAVY] = vecs.T.astype(BF)
    gd = dot_tn(hid[...], da[...]).astype(BF)
    for r in range(8):
        for t in range(3):
            gbuf[96 * r + 32 * t : 96 * r + 32 * t + 32, R_DOWN - R_HEAVY : R_ALL - R_HEAVY] = gd[
                32 * r : 32 * r + 32, 256 * t : 256 * t + 256
            ]
    stores.send(gbuf.at[:, R_VEC - at : R_ALL - at], rest.at[:, R_VEC:R_ALL])
    stores.finish()


def tokens_kernel(got, st, lo, dxg, hl, hr, out, grad):
    back = dot(st[...], got[:, :, S_BACK:S_ALL].reshape(128, 1536))
    out[...] = (lo[...] + back[:, 0:768]).astype(BF)
    dx = dxg[...] + back[:, 768:1536]
    grad[0:64, :] = (dx[0:64, :] + hl[...].astype(F32)).astype(BF)
    grad[64:448, :] = dx[64:448, :].astype(BF)
    grad[448:512, :] = (dx[448:512, :] + hr[...].astype(F32)).astype(BF)


def tail_rows(block, low):
    last = jnp.concatenate([block[32 * t : 32 * t + 32, low + 768 : low + 1024] for t in range(3)], axis=1)
    return jnp.concatenate([block[:, low : low + 768], last], axis=0)


def owner_piece(r, cols, t):
    quarter = cols // 4
    row = lax.broadcasted_iota(jnp.int32, (128, 96), 0)
    col = lax.broadcasted_iota(jnp.int32, (128, 96), 1)
    device, low = 6 * (row >> 3), row & 7
    main = ((low < 6) & (col == device + low)).astype(F32).astype(BF)
    extra = ((low >= 6) & (col == device + 3 * (low - 6) + t)).astype(F32).astype(BF)
    part = dot(main, r[:, quarter * t : quarter * t + quarter]) + dot(extra, r[:, 3 * quarter : cols])
    return part.astype(BF)


def owner_rows(r, cols):
    return jnp.concatenate([owner_piece(r, cols, t) for t in range(3)], axis=1)


def tail_of(block):
    cols = block.shape[1] // 3
    return jnp.concatenate(
        [block[6 + n : 7 + n, cols * t : cols * t + cols] for n in range(2) for t in range(3)], axis=0
    )


def spread_ffn_kernel(r, send):
    send[:, 0:S_DOWN] = owner_rows(r, F_DOWN)
    send[:, S_DOWN:S_FFN] = tail_rows(r[...], F_DOWN)


def spread_rest_kernel(r_in, send_in, send, hd, r, rows, in_sems, out_sems):
    loads, stores = Copies(in_sems), Copies(out_sems)
    quarter = R_ALL // 4
    got = [
        loads.start(r_in.at[:, quarter * t : quarter * t + quarter], r.at[:, quarter * t : quarter * t + quarter])
        for t in (3, 0, 1, 2)
    ]
    got[0].wait()
    hd[...] = jnp.concatenate([r[32 * t : 32 * t + 32, R_DOWN:R_ALL] for t in range(3)], axis=1)
    for t in range(3):
        piece = slice(quarter * t, quarter * t + quarter)
        got[t + 1].wait()
        rows[:, piece] = owner_piece(r, R_ALL, t)
        stores.send(rows.at[:, piece], send.at[:, piece])
    stores.finish()


def sum_parts(got, a, b):
    t = got[0, :, a:b].astype(F32)
    for d in range(1, 16):
        t = t + got[d, :, a:b].astype(F32)
    return t


def sum_ffn_kernel(got, gate, up, down):
    both = sum_parts(got, 0, S_DOWN)
    for c in range(3):
        gate[:, 256 * c : 256 * c + 256] = both[0:6, 512 * c : 512 * c + 256]
        up[:, 256 * c : 256 * c + 256] = both[0:6, 512 * c + 256 : 512 * c + 512]
    both = tail_of(both)
    gate[:, 768:1024] = both[:, 0:256]
    up[:, 768:1024] = both[:, 256:512]
    down[...] = sum_parts(got, S_DOWN, S_FFN)


def sum_rest_kernel(got, q, k, v, o, hq, hk, hv, ho, hgate, hup, vecs):
    total = sum_parts(got, 0, S_BACK)
    for n, ref in enumerate((q, k, v, o)):
        ref[...] = total[0:6, 768 * n : 768 * n + 768]
    rest = tail_of(total)
    ho[...] = rest[:, 128:896]
    rows = jnp.concatenate([rest[:, 896:1024], jnp.zeros((122, 128), F32)], axis=0).T
    for n, ref in enumerate(vecs):
        ref[...] = rows[n : n + 1, 0:6]
    at = R_HEAVY
    for j in range(16):
        hgate[:, 256 * j : 256 * j + 256] = got[j, :, at : at + 256].astype(F32)[0:6]
        hup[:, 256 * j : 256 * j + 256] = got[j, :, at + 256 : at + 512].astype(F32)[0:6]
    at = at + 512
    for p in range(6):
        two = [got[2 * p + n, :, 0:S_BACK].astype(F32) for n in range(2)]
        pair = two[0][:, R_HEAVY + 512 : R_HEAVY + 768] + two[1][:, R_HEAVY + 512 : R_HEAVY + 768]
        hq[:, 128 * p : 128 * p + 128] = pair[0:6, 0:128]
        hk[:, 128 * p : 128 * p + 128] = pair[0:6, 128:256]
        hv[:, 128 * p : 128 * p + 128] = tail_of(two[0] + two[1])[:, 0:128]


def last_kernel(
    got_in, st, lo_in, dxg_in, hl, hr,
    out, grad, q, k, v, o, hq, hk, hv, ho, hgate, hup, *rest,
):
    *vecs, got, lo, dxg, sems = rest
    copies = Copies(sems)
    pieces = [
        copies.start(got_in.at[:, :, a:b], got.at[:, :, a:b]) for a, b in ((0, S_BACK), (S_BACK, S_ALL))
    ]
    got_lo, got_dxg = copies.start(lo_in, lo), copies.start(dxg_in, dxg)
    pieces[0].wait()
    sum_rest_kernel(got, q, k, v, o, hq, hk, hv, ho, hgate, hup, vecs)
    pieces[1].wait()
    got_lo.wait()
    got_dxg.wait()
    tokens_kernel(got, st, lo, dxg, hl, hr, out, grad)


def call(kernel, outs, args, scratch=(), in_specs=None, out_specs=None, sems=(), name=None, us=0.05, aliases={}):
    return pl.pallas_call(
        kernel,
        out_shape=[jax.ShapeDtypeStruct(s, t) for s, t in outs],
        in_specs=in_specs or [VMEM] * len(args),
        out_specs=out_specs or [VMEM] * len(outs),
        scratch_shapes=[pltpu.VMEM(s, t) for s, t in scratch]
        + [pltpu.SemaphoreType.DMA((n,)) for n in sems],
        compiler_params=PARAMS,
        cost_estimate=pl.CostEstimate(
            flops=int(us * 1.0e9), bytes_accessed=int(us * 3.0e6), transcendentals=0
        ),
        input_output_aliases=aliases,
        name=name,
    )(*args)


def run_light_ffn(tokens, cotangent, wall):
    return call(
        light_ffn_kernel,
        [((512, 768), F32), ((512, 768), F32), ((768, F_ALL), BF), ((8, 768), F32), ((8, 768), F32)],
        (tokens, cotangent, wall),
        [
            ((512, 768), BF), ((512, 768), BF),
            ((768, 512), BF), ((512, 768), BF), ((768, 512), BF), ((768, 3072), BF),
            ((1024, 2048), BF), ((1024, 256), BF), ((1024, 128), BF), ((256, 768), BF),
        ],
        [HBM, HBM, HBM],
        [VMEM, VMEM, HBM, VMEM, VMEM],
        sems=(11, 8),
        name="light_ffn",
        us=200,
    )


def run_light_attn(meta, xl, tokens, xr, cotangent, wall, ffn, cf, gvec, vrows):
    return call(
        light_attn_kernel,
        [
            ((512, 768), F32), ((512, 768), F32), ((64, 768), BF), ((64, 768), BF), ((768, R_ALL), BF), ((8, 768), F32),
            ((128, 768), BF),
        ],
        (meta, xl, tokens, xr, cotangent, wall, ffn, cf, gvec, vrows),
        [
            ((768, 3072), BF), ((640, 768), BF), ((640, 768), BF), ((768, 640), BF), ((640, 2304), BF),
            ((512, 768), BF), ((512, 768), BF), ((640, 2304), BF),
            ((640, 768), F32), ((640, 768), F32), ((4, 256, 256), F32),
            ((1024, 3072), BF), ((512, 768), BF), ((512, 768), F32), ((512, 768), F32),
            ((512, 768), F32), ((640, 768), F32), ((768, 3072), BF),
        ],
        [SMEM, VMEM, HBM, VMEM, HBM] + [HBM] * 3 + [VMEM, VMEM],
        [HBM, VMEM, VMEM, VMEM, HBM, VMEM, VMEM],
        sems=(8, 5),
        name="light_attn",
        us=2,
    )


def run_heavy(meta, xg, hw, wo, kmask, gvec, vrows, rest):
    col = ((1024, 1), F32)
    rows, narrow = ((1024, 768), BF), ((1024, 128), BF)
    return call(
        heavy_kernel,
        [((256, 768), BF)] * 8 + [((768, R_ALL), BF)],
        (meta, xg, hw, wo, kmask, gvec, vrows, rest),
        [
            ((1024, 1536), BF), ((768, 896), BF), ((256, 768), BF), rows, rows,
            narrow, narrow, narrow, narrow, narrow, ((1024, 384), BF),
            ((1024, 128), F32), ((1024, 128), F32), ((1024, 256), F32),
            rows, ((1024, 512), BF), ((1024, 256), BF), col, col, col,
            ((8, 160, 896), BF), rows, rows, ((768, R_ALL - R_HEAVY), BF), ((8, 768), F32),
        ],
        [SMEM, HBM, HBM, VMEM, HBM, VMEM, VMEM, HBM],
        [HBM] * 9,
        sems=(3, 11),
        aliases={7: 8},
        name="heavy",
        us=200,
    )


def body(
    tokens, lengths, routed, cotangent, gain_attn, gain_ffn, router_attn, router_ffn,
    light_q, light_k, light_v, light_o, light_gate, light_up, light_down,
    heavy_q, heavy_k, heavy_v, heavy_o, heavy_gate, heavy_up, heavy_down,
):
    me = lax.axis_index("fsdp")
    vectors = [v.reshape(1, 6) for v in (gain_attn, gain_ffn, router_attn, router_ffn)]
    pack, hsend, hd = call(
        prep_kernel,
        [((8, C_ALL), BF), ((16, 8, 896), BF), ((32, 768), BF)],
        (
            light_q, light_k, light_v, light_o, light_gate, light_up, light_down,
            heavy_q, heavy_k, heavy_v, heavy_o, heavy_gate, heavy_up, heavy_down, *vectors,
        ),
        [((8, C_ALL), F32), ((128, 128), F32), ((8, 4096), F32)],
        name="prep",
    )
    wall = lax.all_gather(pack, ALL, axis=0, tiled=True)

    hcols = lax.all_to_all(hsend, "fsdp", split_axis=0, concat_axis=0, tiled=True)
    hd = lax.ppermute(hd, ALL, [(d, (d % 8) * 16 + d // 8) for d in range(128)])
    hblock = jnp.concatenate([hcols.reshape(128, 896), jnp.pad(hd, ((0, 0), (0, 128)))], axis=0)

    edges = jnp.arange(17, dtype=jnp.int32) * 512
    bounds = jnp.sum((routed[0][None, :] < edges[:, None]).astype(jnp.int32), axis=1)
    dp = lax.axis_index("dp")
    pair = jnp.where(me < 12, me // 2, 5)
    meta = jnp.concatenate(
        [
            bounds,
            jnp.stack(
                [
                    lengths[0, 0] // 8, 128 * pair, jnp.where(me < 12, me % 2, 2),
                    me, dp // 2, dp % 2, lengths[0, 0],
                ]
            ),
        ]
    )

    def swap(rows):
        return lax.all_to_all(rows, "fsdp", split_axis=0, concat_axis=0, tiled=True)

    slots, st = call(
        slots_kernel,
        [((128, 1536), BF), ((512, 128), BF)],
        (meta, routed, tokens, cotangent),
        in_specs=[SMEM, VMEM, VMEM, VMEM],
        name="slots",
    )
    own, many, kmask = call(
        entries_kernel,
        [((64, 1536), BF), ((16, 64, 1536), BF), ((1024, 256), F32)],
        (meta, swap(slots.reshape(16, 8, 1536)).reshape(128, 1536)),
        in_specs=[SMEM, VMEM],
        name="entries",
    )
    right = [(i, i + 1) for i in range(15)]
    left = [(i + 1, i) for i in range(15)]
    xl = lax.ppermute(tokens[448:512], "fsdp", right)
    xr = lax.ppermute(tokens[0:64], "fsdp", left)

    wall, many, xl, xr, hblock = lax.optimization_barrier((wall, many, xl, xr, hblock))
    hw = lax.all_gather(hblock, "dp", axis=0, tiled=False)
    xg = swap(many).reshape(1024, 1536)
    ffn, cf, grad_ffn, gvec, vrows = run_light_ffn(tokens, cotangent, wall)
    rs_ffn = lax.psum_scatter(grad_ffn, "dp", scatter_dimension=0, tiled=True)
    lmeta = jnp.concatenate([jnp.stack([lengths[0, 0], me * 512, jnp.int32(8192)]), meta[18:20]])
    lo, dxg, to_left, to_right, rest, gvec, heavy_wo = run_light_attn(
        lmeta, xl, tokens, xr, cotangent, wall, ffn, cf, gvec, vrows
    )
    *partial, rest = run_heavy(meta, xg, hw, heavy_wo, kmask, gvec, vrows, rest)
    rs_rest = lax.psum_scatter(rest, "dp", scatter_dimension=0, tiled=True)

    def along(blocks, x, y):
        moved = [
            lax.ppermute(
                block, "fsdp", [(i, (i // 4 + n * x) % 4 * 4 + (i % 4 + n * y) % 4) for i in range(16)]
            )
            for n, block in enumerate(blocks[1:], 1)
        ]
        return [blocks[0]] + moved

    blocks = call(
        first_sum_kernel,
        [((64, 768), BF)] * 8,
        (meta, *along(partial[0:4], 1, 0), *along(partial[4:8], 0, 1)),
        in_specs=[SMEM] + [VMEM] * 8,
        name="first_sum",
    )
    *blocks, to_left, to_right = lax.optimization_barrier((*blocks, to_left, to_right))
    blocks = along(blocks[0:4], 0, 1) + along(blocks[4:8], 1, 0)
    hr = lax.ppermute(to_left, "fsdp", left)
    hl = lax.ppermute(to_right, "fsdp", right)
    (send_ffn,) = call(spread_ffn_kernel, [((128, S_FFN), BF)], (rs_ffn,), name="spread_ffn")
    got_ffn = swap(send_ffn.reshape(16, 8, S_FFN))
    *blocks, got_ffn, hr, hl = lax.optimization_barrier((*blocks, got_ffn, hr, hl))
    (send,) = call(
        home_kernel,
        [((128, S_ALL), BF)],
        (meta, *blocks, own),
        [((128, 1536), BF)],
        [SMEM] + [VMEM] * 9,
        [HBM],
        sems=(1,),
        name="home",
    )
    send, g_hd = call(
        spread_rest_kernel,
        [((128, S_ALL), BF), ((32, 768), BF)],
        (rs_rest, send),
        [((96, R_ALL), BF), ((128, S_BACK), BF)],
        [HBM, HBM],
        [HBM, VMEM],
        sems=(4, 3),
        name="spread_rest",
        aliases={1: 0},
    )
    g_hd = lax.ppermute(g_hd, ALL, [((d % 8) * 16 + d // 8, d) for d in range(128)])
    got = swap(send.reshape(16, 8, S_ALL))
    six, four, big = ((6, 768), F32), ((6, 1024), F32), ((6, 4096), F32)
    g_gate, g_up, g_down = call(
        sum_ffn_kernel, [four, four, ((8, 768), F32)], (got_ffn,), name="sum_ffn"
    )
    output, grad_tokens, g_q, g_k, g_v, g_o, g_hq, g_hk, g_hv, g_ho, g_hgate, g_hup, *g_vecs = call(
        last_kernel,
        [((512, 768), BF), ((512, 768), BF)] + [six] * 8 + [big, big] + [((1, 6), F32)] * 4,
        (got, st, lo, dxg, hl, hr),
        [((16, 8, S_ALL), BF), ((512, 768), F32), ((512, 768), F32)],
        [HBM, VMEM, HBM, HBM, VMEM, VMEM],
        sems=(4,),
        name="last",
    )
    return (
        output, grad_tokens,
        *[v.reshape(6) for v in g_vecs],
        g_q, g_k, g_v, g_o, g_gate, g_up, g_down,
        g_hq, g_hk, g_hv, g_ho, g_hgate, g_hup, g_hd.astype(F32),
    )


def solution(mesh):
    rows = P(ALL, None)
    flat = P(ALL)
    in_specs = (rows, P("dp", None), P("dp", None), rows) + (flat,) * 4 + (rows,) * 14
    out_specs = (rows, rows) + (flat,) * 4 + (rows,) * 14
    return jax.shard_map(body, mesh=mesh, in_specs=in_specs, out_specs=out_specs, check_vma=False)
```

```python
import jax
import jax.numpy as jnp
from jax import lax
from jax.experimental import pallas as pl
from jax.experimental.pallas import tpu as pltpu
from jax.sharding import PartitionSpec as P

BF = jnp.bfloat16
F32 = jnp.float32
EPS = 1e-6
NEG = -1e30
ALL = ("dp", "fsdp")
CAP = 96
LIGHT_SCALE = 96**-0.5
HEAVY_SCALE = 64**-0.5
PARAMS = pltpu.CompilerParams(vmem_limit_bytes=63 * 1024 * 1024)
SMEM = pl.BlockSpec(memory_space=pltpu.SMEM)
VMEM = pl.BlockSpec(memory_space=pltpu.VMEM)
HBM = pl.BlockSpec(memory_space=pl.ANY)

C_QKVO, C_VEC, C_DOWN, C_ALL = 2048, 5120, 5248, 5504
F_DOWN, F_ALL = 2048, 3072
R_HEAVY, R_HO, R_VEC, R_DOWN, R_ALL = 3072, 3968, 4736, 4864, 5120
S_DOWN, S_FFN = 1536, 2304
S_BACK, S_ALL = 3840, 5376

def dot(a, b):
    return jnp.dot(a, b, preferred_element_type=F32)


def dot_nt(a, b):
    return lax.dot_general(a, b, (((1,), (1,)), ((), ())), preferred_element_type=F32)


def dot_tn(a, b):
    return lax.dot_general(a, b, (((0,), (0,)), ((), ())), preferred_element_type=F32)


def pick6(rows, cols, shift=0):
    r = lax.broadcasted_iota(jnp.int32, (rows, cols), 0) + shift
    c = lax.broadcasted_iota(jnp.int32, (rows, cols), 1)
    low = c & 7
    return ((6 * (c >> 3) + low == r) & (low < 6)).astype(F32).astype(BF)


def unpad_rows(ref, out_ref, pick, at=0, width=None):
    width = width or ref.shape[1]
    for b in range(8):
        block = dot(pick, ref[128 * b : 128 * b + 128, at : at + width])
        out_ref[96 * b : 96 * b + 96, at : at + width] = block.astype(BF)


def vector_rows(vec_ref, pick):
    blocks = [dot(pick, vec_ref[128 * b : 128 * b + 128, :]) for b in range(8)]
    return jnp.concatenate(blocks, axis=0).T


class Copies:
    def __init__(self, sems, used=0):
        self.sems, self.used, self.open = sems, used, []

    def start(self, src, dst):
        copy = pltpu.make_async_copy(src, dst, self.sems.at[self.used])
        self.used += 1
        copy.start()
        return copy

    def send(self, src, dst):
        self.open.append(self.start(src, dst))

    def finish(self):
        for copy in self.open:
            copy.wait()


def unit(rows):
    scale = lax.rsqrt(jnp.mean(rows * rows, axis=-1, keepdims=True) + EPS)
    return rows * scale, scale


def gelu_parts(gate):
    c0, c1 = 0.7978845608, 0.044715
    sq = gate * gate
    t = jnp.tanh(gate * (c0 + (c0 * c1) * sq))
    half = 0.5 * (1.0 + t)
    slope = half + (0.5 * gate) * (1.0 - t * t) * (c0 + (3.0 * c0 * c1) * sq)
    return gate * half, slope


def prep_kernel(
    q, k, v, o, gate, up, down, hq, hk, hv, ho, hgate, hup, hdown, ga, gf, ra, rf, pack, hsend, hd, scr, rows, wide
):
    scr[...] = jnp.zeros_like(scr)
    zero128 = jnp.zeros((8, 128), BF)
    for c in range(4):
        cols = slice(256 * c, 256 * c + 256)
        scr[0:6, 512 * c : 512 * c + 256] = gate[:, cols]
        scr[0:6, 512 * c + 256 : 512 * c + 512] = up[:, cols]
    for n, ref in enumerate((q, k, v, o)):
        scr[0:6, C_QKVO + 768 * n : C_QKVO + 768 * n + 768] = ref[...]
    for a in range(2):
        for b in range(4):
            scr[6 + a : 7 + a, 512 * b : 512 * b + 512] = down[4 * a + b : 4 * a + b + 1, 0:512]
        for b in range(3):
            at = C_QKVO + 768 * b
            scr[6 + a : 7 + a, at : at + 768] = ho[3 * a + b : 3 * a + b + 1, :]
    scr[:, C_DOWN:C_ALL] = down[:, 512:768]
    rows[...] = jnp.zeros_like(rows)
    for n, ref in enumerate((ga, gf, ra, rf)):
        rows[n : n + 1, 0:6] = ref[...]
    scr[:, C_VEC : C_VEC + 128] = rows[...].T[0:8, :]
    pack[...] = scr[...].astype(BF)
    wide[...] = jnp.zeros_like(wide)

    def padded(ref):
        cols = ref.shape[1]
        wide[0:6, 0:cols] = ref[...]
        return wide[:, 0:cols].astype(BF)

    wq, wk, wv = padded(hq), padded(hk), padded(hv)
    wg, wu = padded(hgate), padded(hup)
    for j in range(16):
        hsend[j, :, 0:256] = wg[:, 256 * j : 256 * j + 256]
        hsend[j, :, 256:512] = wu[:, 256 * j : 256 * j + 256]
        for n, w in enumerate((wq, wk, wv)):
            p = j // 2
            part = w[:, 128 * p : 128 * p + 128] if j < 12 else zero128
            hsend[j, :, 512 + 128 * n : 640 + 128 * n] = part
    hd[...] = hdown[...].astype(BF)


def light_ffn_kernel(
    x_in, g_in, wall, ffn, cf, light, gvec, vrows, x, g, gu, fin, fin_t, gbuf, gu_pad, down, vec, wd, in_sems, out_sems
):
    def wide(c, at=0):
        return pl.ds(pl.multiple_of(at + 512 * c, 128), 512)

    def loads(c):
        rows = pl.ds(pl.multiple_of(256 * c, 256), 256)
        yield pltpu.make_async_copy(wall.at[:, wide(c)], gu_pad.at[:, wide(c)], in_sems.at[2 * c])
        yield pltpu.make_async_copy(
            wall.at[rows, C_DOWN:C_ALL], down.at[rows, :], in_sems.at[2 * c + 1]
        )

    def stores(c):
        rows = pl.ds(pl.multiple_of(192 * c, 64), 192)
        yield pltpu.make_async_copy(gbuf.at[:, wide(c)], light.at[:, wide(c)], out_sems.at[2 * c])
        yield pltpu.make_async_copy(
            gbuf.at[rows, 2048:3072], light.at[rows, F_DOWN:F_ALL], out_sems.at[2 * c + 1]
        )

    first = Copies(in_sems, 8)
    got_x = first.start(x_in, x)
    got_vec = first.start(wall.at[:, C_VEC : C_VEC + 128], vec)
    got_g = first.start(g_in, g)
    for c in range(4):
        for copy in loads(c):
            copy.start()
    pick = pick6(96, 128)
    got_x.wait()
    u, _ = unit(x[...].astype(F32))
    got_vec.wait()
    vrows[...] = vector_rows(vec, pick)[0:8, :]
    gain_f = vrows[1:2, :]
    f = (u * gain_f).astype(BF)
    fin[...] = f
    fin_t[...] = f.T
    ffn[...] = jnp.zeros_like(ffn)
    cf[...] = jnp.zeros_like(cf)
    got_g.wait()

    for c in range(4):
        for copy in loads(c):
            copy.wait()
    out_row = lax.broadcasted_iota(jnp.int32, (256, 256), 0)
    in_row = lax.broadcasted_iota(jnp.int32, (256, 256), 1)
    spare = (out_row & ~7) + 6 + ((out_row >> 2) & 1) == in_row
    spread = [(spare & ((out_row & 3) == b)).astype(F32).astype(BF) for b in range(4)]

    @pl.loop(0, 4)
    def _(c):
        for b in range(8):
            block = dot(pick, gu_pad[128 * b : 128 * b + 128, wide(c)])
            gu[96 * b : 96 * b + 96, :] = block.astype(BF)
        w = gu[...]
        rows = pl.ds(pl.multiple_of(256 * c, 256), 256)
        left = dot(spread[0], gu_pad[rows, 0:512])
        for b in range(1, 4):
            left = left + dot(spread[b], gu_pad[rows, 512 * b : 512 * b + 512])
        wd[:, 0:512] = left.astype(BF)
        wd[:, 512:768] = down[rows, :]
        both = dot(fin[...], w)
        act, slope = gelu_parts(both[:, 0:256])
        up = both[:, 256:512]
        hidden = (act * up).astype(BF)
        dh = dot_nt(g[...], wd[...])
        dgu = jnp.concatenate([(dh * up * slope).astype(BF), (dh * act).astype(BF)], axis=1)
        ffn[...] += dot(hidden, wd[...])
        cf[...] += dot_nt(dgu, w)
        gbuf[:, wide(c)] = dot(fin_t[...], dgu).astype(BF)
        gd = dot_tn(hidden, g[...]).astype(BF)
        for n in range(2):
            r0 = 128 * n
            at = pl.multiple_of(192 * c + 96 * n, 32)
            gbuf[pl.ds(at, 96), 2048:2816] = gd[r0 : r0 + 96, :]
            for t in range(3):
                gbuf[pl.ds(pl.multiple_of(at + 32 * t, 32), 32), 2816:3072] = gd[
                    r0 + 96 : r0 + 128, 256 * t : 256 * t + 256
                ]
        for copy in stores(c):
            copy.start()

    u, _ = unit(x[...].astype(F32))
    d_f = cf[...]
    gvec[...] = jnp.zeros_like(gvec)
    gvec[1:2, :] = jnp.sum(d_f * u, axis=0, keepdims=True)
    cf[...] = d_f * gain_f
    for c in range(4):
        for copy in stores(c):
            copy.wait()


def light_attn_kernel(
    meta, xl, x_in, xr, g_in, wall, ffn_in, cf_in, gin, vrows,
    lo, dxg, to_left, to_right, rest, gvec, heavy_wo,
    w, xs, a, a_t, qkv, o, do, dqkv, dk, dv, mask, w_pad, g, ffn, cf, lo_buf, d_a, gbuf, in_sems, out_sems,
):
    def wide(n, at=0):
        return pl.ds(pl.multiple_of(at + 768 * n, 128), 768)

    def load(n):
        return pltpu.make_async_copy(wall.at[:, wide(n, C_QKVO)], w_pad.at[:, wide(n)], in_sems.at[n])

    def store(n):
        return pltpu.make_async_copy(gbuf.at[:, wide(n)], rest.at[:, wide(n)], out_sems.at[n])

    loads, stores = Copies(in_sems, 4), Copies(out_sems, 4)
    x = xs.at[64:576, :]
    got_x = loads.start(x_in, x)
    for n in range(4):
        load(n).start()
    got_g = loads.start(g_in, g)
    got_ffn = loads.start(ffn_in, ffn)
    got_cf = loads.start(cf_in, cf)
    pick = pick6(96, 128)
    xs[0:64, :] = xl[...]
    xs[576:640, :] = xr[...]
    first, base, pack_len = meta[0], meta[1], meta[2]
    key = lax.broadcasted_iota(jnp.int32, (256, 256), 0)
    qry = lax.broadcasted_iota(jnp.int32, (256, 256), 1) & 127
    gap = key - qry

    @pl.loop(0, 4)
    def _(b):
        qpos = base + 128 * b + qry
        kpos = base + 128 * b - 64 + key
        ok = (gap >= 0) & (gap <= 128) & ((qpos < first) == (kpos < first))
        ok = ok & (kpos >= 0) & (kpos < pack_len)
        mask[b] = jnp.where(ok, 0.0, NEG)

    dk[...] = jnp.zeros_like(dk)
    dv[...] = jnp.zeros_like(dv)
    dqkv[0:64, 0:768] = jnp.zeros((64, 768), BF)
    dqkv[576:640, 0:768] = jnp.zeros((64, 768), BF)
    got_x.wait()
    u, _ = unit(xs[...].astype(F32))
    gain_a = vrows[0:1, :]
    a[...] = (u * gain_a).astype(BF)

    def unpad(n):
        load(n).wait()
        for b in range(8):
            w[96 * b : 96 * b + 96, wide(n)] = dot(pick, w_pad[128 * b : 128 * b + 128, wide(n)]).astype(BF)

    @pl.loop(0, 3)
    def _(n):
        unpad(n)
        qkv[:, wide(n)] = dot(a[...], w[:, wide(n)]).astype(BF)

    unpad(3)
    got_g.wait()
    do[...] = dot_nt(g[...], w[:, 2304:3072]).astype(BF)

    row = lax.broadcasted_iota(jnp.int32, (128, 1024), 0)
    col = lax.broadcasted_iota(jnp.int32, (128, 1024), 1)
    entry = 6 * (col >> 3) + 3 * ((col & 7) - 6)
    keep = ((col & 7) >= 6) & ((row >> 6) == meta[4])
    wo = jnp.zeros((128, 768), F32)
    for b in range(3):
        take = (keep & (entry + b == row + meta[3])).astype(F32).astype(BF)
        wo = wo + dot(take, w_pad[:, 768 * b : 768 * b + 768])
    heavy_wo[...] = wo.astype(BF)

    lane = lax.broadcasted_iota(jnp.int32, (128, 256), 1)

    def pair(b, group, second):
        low = 64 * second
        even = (lane >= low) & (lane < low + 96)
        odd = (lane >= low + 96) & (lane < low + 192)

        def split(t):
            zero = jnp.zeros_like(t)
            return jnp.concatenate([jnp.where(even, t, zero), jnp.where(odd, t, zero)], axis=0)

        def join(t):
            return jnp.where(even, t[0:128], 0.0) + jnp.where(odd, t[128:256], 0.0)

        def win(part):
            return pl.ds(pl.multiple_of(768 * part + 384 * group + 128 * second, 128), 256)

        rq = pl.ds(pl.multiple_of(128 * b, 128), 128)
        rd = pl.ds(pl.multiple_of(128 * b + 64, 64), 128)
        rk = pl.ds(pl.multiple_of(128 * b, 128), 256)
        kw, vw = qkv[rk, win(1)], qkv[rk, win(2)]
        q2, do2 = split(qkv[rd, win(0)]), split(do[rq, win(0)])
        s = dot_nt(kw, q2) * LIGHT_SCALE + mask[b]
        dp = dot_nt(vw, do2)
        e = jnp.exp(s - jnp.max(s, axis=0, keepdims=True))
        p = e * (1.0 / jnp.sum(e, axis=0, keepdims=True))
        pb = p.astype(BF)
        ds = (p * (dp - jnp.sum(p * dp, axis=0, keepdims=True))).astype(BF)
        dk[rk, win(0)] += dot(ds, q2) * LIGHT_SCALE
        dv[rk, win(0)] += dot(pb, do2)
        return join(dot_tn(pb, vw)), join(dot_tn(ds, kw)) * LIGHT_SCALE

    @pl.loop(0, 8)
    def _(i):
        b, group = i >> 1, i & 1
        rq = pl.ds(pl.multiple_of(128 * b, 128), 128)
        rd = pl.ds(pl.multiple_of(128 * b + 64, 64), 128)
        o0, dq0 = pair(b, group, 0)
        o1, dq1 = pair(b, group, 1)

        def tile(n):
            return pl.ds(pl.multiple_of(384 * group + 128 * n, 128), 128)

        for ref, rows, t0, t1 in ((o, rq, o0, o1), (dqkv, rd, dq0, dq1)):
            ref[rows, tile(0)] = t0[:, 0:128].astype(BF)
            ref[rows, tile(1)] = (t0[:, 128:256] + t1[:, 0:128]).astype(BF)
            ref[rows, tile(2)] = t1[:, 128:256].astype(BF)

    got_ffn.wait()
    lo_buf[...] = x[...].astype(F32) + ffn[...] + dot(o[...], w[:, 2304:3072])
    stores.send(lo_buf, lo)
    gbuf[:, 2304:3072] = dot_tn(o[...], g[...]).astype(BF)
    store(3).start()
    dqkv[:, 768:1536] = dk[...].astype(BF)
    dqkv[:, 1536:2304] = dv[...].astype(BF)
    a_t[...] = a[...].T
    d_a[...] = jnp.zeros_like(d_a)

    @pl.loop(0, 3)
    def _(n):
        part = dqkv[:, wide(n)]
        gbuf[:, wide(n)] = dot(a_t[...], part).astype(BF)
        store(n).start()
        d_a[...] += dot_nt(part, w[:, wide(n)])

    u, scale = unit(xs[...].astype(F32))
    c = d_a[...]
    gvec[...] = gin[...]
    gvec[0:1, :] = jnp.sum(c * u, axis=0, keepdims=True)
    c = c * gain_a
    got_cf.wait()

    def norm_back(c, rows):
        ur = u[rows]
        return scale[rows] * (c - ur * jnp.mean(ur * c, axis=-1, keepdims=True))

    own = slice(64, 576)
    dxg[...] = norm_back(c[own] + cf[...], own) + g[...].astype(F32)
    to_left[...] = norm_back(c[0:64], slice(0, 64)).astype(BF)
    to_right[...] = norm_back(c[576:640], slice(576, 640)).astype(BF)
    stores.finish()
    for n in range(4):
        store(n).wait()


def slots_kernel(meta, routed, x, g, slots, st):
    me = meta[20]
    start = meta[me]
    token = lax.broadcasted_iota(jnp.int32, (512, 1024), 0) + 512 * me
    r = jnp.broadcast_to(routed[...], (512, 1024))
    rank = jnp.sum((r < token).astype(F32), axis=1, keepdims=True).astype(jnp.int32) - start
    hit = jnp.sum((r == token).astype(F32), axis=1, keepdims=True)
    row = ((start + rank) & 15) * 8 + (rank >> 4)
    row = jnp.where((hit > 0.5) & (rank < CAP), row, -1)
    lane = lax.broadcasted_iota(jnp.int32, (512, 128), 1)
    onehot = (lane == row).astype(F32).astype(BF)
    st[...] = onehot
    slots[:, 0:768] = dot_tn(onehot, x[...]).astype(BF)
    slots[:, 768:1536] = dot_tn(onehot, g[...]).astype(BF)


def entry_slots(meta):
    p = 16 * lax.broadcasted_iota(jnp.int32, (64, 128), 0) + meta[20]
    source, before = jnp.zeros_like(p), jnp.zeros_like(p)
    for d in range(1, 16):
        source = source + (p >= meta[d]).astype(jnp.int32)
        before = jnp.where(p >= meta[d], meta[d], before)
    rank = p - before
    lane = lax.broadcasted_iota(jnp.int32, (64, 128), 1)
    return ((lane == source * 8 + (rank >> 4)) & (rank < CAP)).astype(F32).astype(BF)


def entries_kernel(meta, got, own, many, kmask):
    entry = entry_of(lax.broadcasted_iota(jnp.int32, (1024, 128), 0))
    bias = jnp.zeros((1024, 128), F32)
    for d in range(16):
        bias = jnp.where((entry >= meta[d] + CAP) & (entry < meta[d + 1]), NEG, bias)
    kmask[:, 0:128] = jnp.where(entry < meta[17], bias, NEG)
    kmask[:, 128:256] = jnp.where(entry < meta[17], NEG, bias)
    rows = dot(entry_slots(meta), got[...]).astype(BF)
    own[...] = rows
    for t in range(16):
        many[t] = rows


def first_sum_kernel(meta, y0, y1, y2, y3, c0, c1, c2, c3, *outs):
    for n in range(4):
        for here, parts, out in (
            (meta[20] & 3, (y0, y1, y2, y3), outs[n]), (meta[20] >> 2, (c0, c1, c2, c3), outs[4 + n])
        ):
            rows = pl.ds(pl.multiple_of(64 * ((here + n) & 3), 64), 64)
            total = parts[0][rows, :].astype(F32)
            for part in parts[1:]:
                total = total + part[rows, :].astype(F32)
            out[...] = total.astype(BF)


def home_kernel(meta, y0, y1, y2, y3, c0, c1, c2, c3, own, send, back, sems):
    y, c = (
        a[...].astype(F32) + b[...].astype(F32) + d[...].astype(F32) + e[...].astype(F32)
        for a, b, d, e in ((y0, y1, y2, y3), (c0, c1, c2, c3))
    )
    onehot = entry_slots(meta)
    u, scale = unit(own[:, 0:768].astype(F32))
    dxr = scale * (c - u * jnp.mean(u * c, axis=-1, keepdims=True))
    back[:, 0:768] = dot_tn(onehot, y.astype(BF)).astype(BF)
    back[:, 768:1536] = dot_tn(onehot, dxr.astype(BF)).astype(BF)
    Copies(sems).start(back, send.at[:, S_BACK:S_ALL]).wait()


def entry_of(row):
    return ((row & 63) << 4) + (row >> 6)


def heavy_kernel(
    meta, xg_in, hw_in, wo, kmask_in, gin, vrows, rest_in,
    y0, y1, y2, y3, c0, c1, c2, c3, rest,
    xg, w, wd, ar, fr, q, k, v, o, do, dqkv, dk, dv, kmask, da, dgu, hid, sa, sf, la,
    hw, ybuf, cbuf, gbuf, gvec, in_sems, out_sems,
):
    loads, stores = Copies(in_sems), Copies(out_sems)
    got_hw = loads.start(hw_in, hw)
    got_xg = loads.start(xg_in, xg)
    got_kmask = loads.start(kmask_in, kmask)
    pick = pick6(96, 128)
    gain_a, gain_f, r_a, r_f = (vrows[n : n + 1, :] for n in range(4))
    got_hw.wait()
    for b in range(8):
        w[96 * b : 96 * b + 96, :] = dot(pick, hw[b, 0:128, :]).astype(BF)
        wd[32 * b : 32 * b + 32, :] = hw[b, 128:160, 0:768]
    low, head = meta[18], meta[19]
    on = (lax.broadcasted_iota(jnp.int32, (256, 128), 1) >> 6) == head
    got_xg.wait()

    @pl.loop(0, 4, unroll=2)
    def _(b):
        rows = pl.ds(pl.multiple_of(256 * b, 256), 256)
        u, _ = unit(xg[rows, 0:768].astype(F32))
        arb, frb = (u * gain_a).astype(BF), (u * gain_f).astype(BF)
        ar[rows, :], fr[rows, :] = arb, frb
        sab = jax.nn.sigmoid(jnp.sum(arb.astype(F32) * r_a, axis=-1, keepdims=True))
        sfb = jax.nn.sigmoid(jnp.sum(frb.astype(F32) * r_f, axis=-1, keepdims=True))
        sa[rows, :], sf[rows, :] = sab, sfb
        qkv = dot(arb, w[:, 512:896])
        q[rows, :] = jnp.where(on, qkv[:, 0:128] * HEAVY_SCALE, 0.0).astype(BF)
        k[rows, :] = qkv[:, 128:256].astype(BF)
        v[rows, :] = jnp.where(on, qkv[:, 256:384], 0.0).astype(BF)
        dab = (sab * xg[rows, 768:1536].astype(F32)).astype(BF)
        da[rows, :] = dab
        do[rows, :] = dot_nt(dab, wo[...]).astype(BF)

    got_kmask.wait()
    n0 = meta[17]
    dk[...] = jnp.zeros_like(dk)
    dv[...] = jnp.zeros_like(dv)

    @pl.loop(0, 4, unroll=2)
    def _(b):
        rows = pl.ds(pl.multiple_of(256 * b, 256), 256)
        first = entry_of(lax.broadcasted_iota(jnp.int32, (1, 128), 1) + 256 * b) < n0
        second = entry_of(lax.broadcasted_iota(jnp.int32, (1, 128), 1) + 256 * b + 128) < n0
        bias = jnp.concatenate(
            [jnp.where(first, kmask[:, 0:128], kmask[:, 128:256]),
             jnp.where(second, kmask[:, 0:128], kmask[:, 128:256])],
            axis=1,
        )
        qb, dob = q[rows, :], do[rows, :]
        s = dot_nt(k[...], qb) + bias
        e = jnp.exp(s - jnp.max(s, axis=0, keepdims=True))
        p = e * (1.0 / jnp.sum(e, axis=0, keepdims=True))
        pb = p.astype(BF)
        ob = dot_tn(pb, v[...]).astype(BF)
        o[rows, :] = ob
        la[rows, :] = (1.0 - sa[rows, :]) * jnp.sum(
            ob.astype(F32) * dob.astype(F32), axis=-1, keepdims=True
        )
        dp = dot_nt(v[...], dob)
        ds = (p * (dp - jnp.sum(p * dp, axis=0, keepdims=True))).astype(BF)
        dqkv[rows, 0:128] = jnp.where(on, dot_tn(ds, k[...]) * HEAVY_SCALE, 0.0).astype(BF)
        dk[...] += dot(ds, qb)
        dv[...] += dot(pb, dob)

    dqkv[:, 128:256] = dk[...].astype(BF)
    dqkv[:, 256:384] = dv[...].astype(BF)
    gbuf[:, 512:896] = dot_tn(ar[...], dqkv[...]).astype(BF)
    gbuf[:, R_HO - R_HEAVY : R_VEC - R_HEAVY] = jnp.zeros((768, 768), BF)
    gbuf[pl.ds(pl.multiple_of(low, 128), 128), R_HO - R_HEAVY : R_VEC - R_HEAVY] = dot_tn(o[...], da[...]).astype(BF)
    at = R_HEAVY
    stores.send(gbuf.at[:, 512 : R_VEC - at], rest.at[:, at + 512 : R_VEC])
    gvec[...] = gin[...]

    @pl.loop(0, 4, unroll=2)
    def _(b):
        rows = pl.ds(pl.multiple_of(256 * b, 256), 256)
        frb = fr[rows, :]
        sfb = sf[rows, :]
        dfb = (sfb * xg[rows, 768:1536].astype(F32)).astype(BF)
        both = dot(frb, w[:, 0:512])
        act, slope = gelu_parts(both[:, 0:256])
        up = both[:, 256:512]
        hidden = (act * up).astype(BF)
        hid[rows, :] = hidden
        dh = dot_nt(dfb, wd[...])
        lfb = (1.0 - sfb) * jnp.sum(hidden.astype(F32) * dh, axis=-1, keepdims=True)
        dgub = jnp.concatenate([(dh * up * slope).astype(BF), (dh * act).astype(BF)], axis=1)
        dgu[rows, :] = dgub
        y = sa[rows, :] * dot(o[rows, :], wo[...]) + sfb * dot(hidden, wd[...])
        lab = la[rows, :]
        d_f = dot_nt(dgub, w[:, 0:512]) + lfb * r_f
        d_a = dot_nt(dqkv[rows, :], w[:, 512:896]) + lab * r_a
        u, _ = unit(xg[rows, 0:768].astype(F32))
        gvec[0:1, :] += jnp.sum(d_a * u, axis=0, keepdims=True)
        gvec[1:2, :] += jnp.sum(d_f * u, axis=0, keepdims=True)
        gvec[2:3, :] += jnp.sum(lab * ar[rows, :].astype(F32), axis=0, keepdims=True)
        gvec[3:4, :] += jnp.sum(lfb * frb.astype(F32), axis=0, keepdims=True)
        da[rows, :] = dfb
        ybuf[rows, :] = y.astype(BF)
        c = (d_a * gain_a + d_f * gain_f).astype(BF)
        for t in range(4):
            cbuf[pl.ds(pl.multiple_of(256 * t + 64 * b, 64), 64), :] = c[64 * t : 64 * t + 64]

    for n, (yk, ck) in enumerate(((y0, c0), (y1, c1), (y2, c2), (y3, c3))):
        to_x = ((meta[20] >> 2) + n) & 3
        to_y = ((meta[20] & 3) + n) & 3
        stores.send(ybuf.at[pl.ds(pl.multiple_of(256 * to_x, 256), 256), :], yk)
        stores.send(cbuf.at[pl.ds(pl.multiple_of(256 * to_y, 256), 256), :], ck)

    gbuf[:, 0:512] = dot_tn(fr[...], dgu[...]).astype(BF)
    stores.send(gbuf.at[:, 0:512], rest.at[:, at : at + 512])
    vecs = jnp.concatenate([gvec[...], jnp.zeros((120, 768), F32)], axis=0)
    gbuf[:, R_VEC - R_HEAVY : R_DOWN - R_HEAVY] = vecs.T.astype(BF)
    gd = dot_tn(hid[...], da[...]).astype(BF)
    for r in range(8):
        for t in range(3):
            gbuf[96 * r + 32 * t : 96 * r + 32 * t + 32, R_DOWN - R_HEAVY : R_ALL - R_HEAVY] = gd[
                32 * r : 32 * r + 32, 256 * t : 256 * t + 256
            ]
    stores.send(gbuf.at[:, R_VEC - at : R_ALL - at], rest.at[:, R_VEC:R_ALL])
    stores.finish()


def tokens_kernel(got, st, lo, dxg, hl, hr, out, grad):
    back = dot(st[...], got[:, :, S_BACK:S_ALL].reshape(128, 1536))
    out[...] = (lo[...] + back[:, 0:768]).astype(BF)
    dx = dxg[...] + back[:, 768:1536]
    grad[0:64, :] = (dx[0:64, :] + hl[...].astype(F32)).astype(BF)
    grad[64:448, :] = dx[64:448, :].astype(BF)
    grad[448:512, :] = (dx[448:512, :] + hr[...].astype(F32)).astype(BF)


def tail_rows(block, low):
    last = jnp.concatenate([block[32 * t : 32 * t + 32, low + 768 : low + 1024] for t in range(3)], axis=1)
    return jnp.concatenate([block[:, low : low + 768], last], axis=0)


def owner_piece(r, cols, t):
    quarter = cols // 4
    row = lax.broadcasted_iota(jnp.int32, (128, 96), 0)
    col = lax.broadcasted_iota(jnp.int32, (128, 96), 1)
    device, low = 6 * (row >> 3), row & 7
    main = ((low < 6) & (col == device + low)).astype(F32).astype(BF)
    extra = ((low >= 6) & (col == device + 3 * (low - 6) + t)).astype(F32).astype(BF)
    part = dot(main, r[:, quarter * t : quarter * t + quarter]) + dot(extra, r[:, 3 * quarter : cols])
    return part.astype(BF)


def owner_rows(r, cols):
    return jnp.concatenate([owner_piece(r, cols, t) for t in range(3)], axis=1)


def tail_of(block):
    cols = block.shape[1] // 3
    return jnp.concatenate(
        [block[6 + n : 7 + n, cols * t : cols * t + cols] for n in range(2) for t in range(3)], axis=0
    )


def spread_ffn_kernel(r, send):
    send[:, 0:S_DOWN] = owner_rows(r, F_DOWN)
    send[:, S_DOWN:S_FFN] = tail_rows(r[...], F_DOWN)


def spread_rest_kernel(r_in, send_in, send, hd, r, rows, in_sems, out_sems):
    loads, stores = Copies(in_sems), Copies(out_sems)
    quarter = R_ALL // 4
    got = [
        loads.start(r_in.at[:, quarter * t : quarter * t + quarter], r.at[:, quarter * t : quarter * t + quarter])
        for t in (3, 0, 1, 2)
    ]
    got[0].wait()
    hd[...] = jnp.concatenate([r[32 * t : 32 * t + 32, R_DOWN:R_ALL] for t in range(3)], axis=1)
    for t in range(3):
        piece = slice(quarter * t, quarter * t + quarter)
        got[t + 1].wait()
        rows[:, piece] = owner_piece(r, R_ALL, t)
        stores.send(rows.at[:, piece], send.at[:, piece])
    stores.finish()


def sum_parts(got, a, b):
    t = got[0, :, a:b].astype(F32)
    for d in range(1, 16):
        t = t + got[d, :, a:b].astype(F32)
    return t


def sum_ffn_kernel(got, gate, up, down):
    both = sum_parts(got, 0, S_DOWN)
    for c in range(3):
        gate[:, 256 * c : 256 * c + 256] = both[0:6, 512 * c : 512 * c + 256]
        up[:, 256 * c : 256 * c + 256] = both[0:6, 512 * c + 256 : 512 * c + 512]
    both = tail_of(both)
    gate[:, 768:1024] = both[:, 0:256]
    up[:, 768:1024] = both[:, 256:512]
    down[...] = sum_parts(got, S_DOWN, S_FFN)


def sum_rest_kernel(got, q, k, v, o, hq, hk, hv, ho, hgate, hup, vecs):
    total = sum_parts(got, 0, S_BACK)
    for n, ref in enumerate((q, k, v, o)):
        ref[...] = total[0:6, 768 * n : 768 * n + 768]
    rest = tail_of(total)
    ho[...] = rest[:, 128:896]
    rows = jnp.concatenate([rest[:, 896:1024], jnp.zeros((122, 128), F32)], axis=0).T
    for n, ref in enumerate(vecs):
        ref[...] = rows[n : n + 1, 0:6]
    at = R_HEAVY
    for j in range(16):
        hgate[:, 256 * j : 256 * j + 256] = got[j, :, at : at + 256].astype(F32)[0:6]
        hup[:, 256 * j : 256 * j + 256] = got[j, :, at + 256 : at + 512].astype(F32)[0:6]
    at = at + 512
    for p in range(6):
        two = [got[2 * p + n, :, 0:S_BACK].astype(F32) for n in range(2)]
        pair = two[0][:, R_HEAVY + 512 : R_HEAVY + 768] + two[1][:, R_HEAVY + 512 : R_HEAVY + 768]
        hq[:, 128 * p : 128 * p + 128] = pair[0:6, 0:128]
        hk[:, 128 * p : 128 * p + 128] = pair[0:6, 128:256]
        hv[:, 128 * p : 128 * p + 128] = tail_of(two[0] + two[1])[:, 0:128]


def last_kernel(
    got_in, st, lo_in, dxg_in, hl, hr,
    out, grad, q, k, v, o, hq, hk, hv, ho, hgate, hup, *rest,
):
    *vecs, got, lo, dxg, sems = rest
    copies = Copies(sems)
    pieces = [
        copies.start(got_in.at[:, :, a:b], got.at[:, :, a:b]) for a, b in ((0, S_BACK), (S_BACK, S_ALL))
    ]
    got_lo, got_dxg = copies.start(lo_in, lo), copies.start(dxg_in, dxg)
    pieces[0].wait()
    sum_rest_kernel(got, q, k, v, o, hq, hk, hv, ho, hgate, hup, vecs)
    pieces[1].wait()
    got_lo.wait()
    got_dxg.wait()
    tokens_kernel(got, st, lo, dxg, hl, hr, out, grad)


def call(kernel, outs, args, scratch=(), in_specs=None, out_specs=None, sems=(), name=None, us=0.05, aliases={}):
    return pl.pallas_call(
        kernel,
        out_shape=[jax.ShapeDtypeStruct(s, t) for s, t in outs],
        in_specs=in_specs or [VMEM] * len(args),
        out_specs=out_specs or [VMEM] * len(outs),
        scratch_shapes=[pltpu.VMEM(s, t) for s, t in scratch]
        + [pltpu.SemaphoreType.DMA((n,)) for n in sems],
        compiler_params=PARAMS,
        cost_estimate=pl.CostEstimate(
            flops=int(us * 1.0e9), bytes_accessed=int(us * 3.0e6), transcendentals=0
        ),
        input_output_aliases=aliases,
        name=name,
    )(*args)


def run_light_ffn(tokens, cotangent, wall):
    return call(
        light_ffn_kernel,
        [((512, 768), F32), ((512, 768), F32), ((768, F_ALL), BF), ((8, 768), F32), ((8, 768), F32)],
        (tokens, cotangent, wall),
        [
            ((512, 768), BF), ((512, 768), BF),
            ((768, 512), BF), ((512, 768), BF), ((768, 512), BF), ((768, 3072), BF),
            ((1024, 2048), BF), ((1024, 256), BF), ((1024, 128), BF), ((256, 768), BF),
        ],
        [HBM, HBM, HBM],
        [VMEM, VMEM, HBM, VMEM, VMEM],
        sems=(11, 8),
        name="light_ffn",
        us=200,
    )


def run_light_attn(meta, xl, tokens, xr, cotangent, wall, ffn, cf, gvec, vrows):
    return call(
        light_attn_kernel,
        [
            ((512, 768), F32), ((512, 768), F32), ((64, 768), BF), ((64, 768), BF), ((768, R_ALL), BF), ((8, 768), F32),
            ((128, 768), BF),
        ],
        (meta, xl, tokens, xr, cotangent, wall, ffn, cf, gvec, vrows),
        [
            ((768, 3072), BF), ((640, 768), BF), ((640, 768), BF), ((768, 640), BF), ((640, 2304), BF),
            ((512, 768), BF), ((512, 768), BF), ((640, 2304), BF),
            ((640, 768), F32), ((640, 768), F32), ((4, 256, 256), F32),
            ((1024, 3072), BF), ((512, 768), BF), ((512, 768), F32), ((512, 768), F32),
            ((512, 768), F32), ((640, 768), F32), ((768, 3072), BF),
        ],
        [SMEM, VMEM, HBM, VMEM, HBM] + [HBM] * 3 + [VMEM, VMEM],
        [HBM, VMEM, VMEM, VMEM, HBM, VMEM, VMEM],
        sems=(8, 5),
        name="light_attn",
        us=2,
    )


def run_heavy(meta, xg, hw, wo, kmask, gvec, vrows, rest):
    col = ((1024, 1), F32)
    rows, narrow = ((1024, 768), BF), ((1024, 128), BF)
    return call(
        heavy_kernel,
        [((256, 768), BF)] * 8 + [((768, R_ALL), BF)],
        (meta, xg, hw, wo, kmask, gvec, vrows, rest),
        [
            ((1024, 1536), BF), ((768, 896), BF), ((256, 768), BF), rows, rows,
            narrow, narrow, narrow, narrow, narrow, ((1024, 384), BF),
            ((1024, 128), F32), ((1024, 128), F32), ((1024, 256), F32),
            rows, ((1024, 512), BF), ((1024, 256), BF), col, col, col,
            ((8, 160, 896), BF), rows, rows, ((768, R_ALL - R_HEAVY), BF), ((8, 768), F32),
        ],
        [SMEM, HBM, HBM, VMEM, HBM, VMEM, VMEM, HBM],
        [HBM] * 9,
        sems=(3, 11),
        aliases={7: 8},
        name="heavy",
        us=200,
    )


def body(
    tokens, lengths, routed, cotangent, gain_attn, gain_ffn, router_attn, router_ffn,
    light_q, light_k, light_v, light_o, light_gate, light_up, light_down,
    heavy_q, heavy_k, heavy_v, heavy_o, heavy_gate, heavy_up, heavy_down,
):
    me = lax.axis_index("fsdp")
    vectors = [v.reshape(1, 6) for v in (gain_attn, gain_ffn, router_attn, router_ffn)]
    pack, hsend, hd = call(
        prep_kernel,
        [((8, C_ALL), BF), ((16, 8, 896), BF), ((32, 768), BF)],
        (
            light_q, light_k, light_v, light_o, light_gate, light_up, light_down,
            heavy_q, heavy_k, heavy_v, heavy_o, heavy_gate, heavy_up, heavy_down, *vectors,
        ),
        [((8, C_ALL), F32), ((128, 128), F32), ((8, 4096), F32)],
        name="prep",
    )
    wall = lax.all_gather(pack, ALL, axis=0, tiled=True)

    hcols = lax.all_to_all(hsend, "fsdp", split_axis=0, concat_axis=0, tiled=True)
    hd = lax.ppermute(hd, ALL, [(d, (d % 8) * 16 + d // 8) for d in range(128)])
    hblock = jnp.concatenate([hcols.reshape(128, 896), jnp.pad(hd, ((0, 0), (0, 128)))], axis=0)

    edges = jnp.arange(17, dtype=jnp.int32) * 512
    bounds = jnp.sum((routed[0][None, :] < edges[:, None]).astype(jnp.int32), axis=1)
    dp = lax.axis_index("dp")
    pair = jnp.where(me < 12, me // 2, 5)
    meta = jnp.concatenate(
        [
            bounds,
            jnp.stack(
                [
                    lengths[0, 0] // 8, 128 * pair, jnp.where(me < 12, me % 2, 2),
                    me, dp // 2, dp % 2, lengths[0, 0],
                ]
            ),
        ]
    )

    def swap(rows):
        return lax.all_to_all(rows, "fsdp", split_axis=0, concat_axis=0, tiled=True)

    slots, st = call(
        slots_kernel,
        [((128, 1536), BF), ((512, 128), BF)],
        (meta, routed, tokens, cotangent),
        in_specs=[SMEM, VMEM, VMEM, VMEM],
        name="slots",
    )
    own, many, kmask = call(
        entries_kernel,
        [((64, 1536), BF), ((16, 64, 1536), BF), ((1024, 256), F32)],
        (meta, swap(slots.reshape(16, 8, 1536)).reshape(128, 1536)),
        in_specs=[SMEM, VMEM],
        name="entries",
    )
    right = [(i, i + 1) for i in range(15)]
    left = [(i + 1, i) for i in range(15)]
    xl = lax.ppermute(tokens[448:512], "fsdp", right)
    xr = lax.ppermute(tokens[0:64], "fsdp", left)

    wall, many, xl, xr, hblock = lax.optimization_barrier((wall, many, xl, xr, hblock))
    hw = lax.all_gather(hblock, "dp", axis=0, tiled=False)
    xg = swap(many).reshape(1024, 1536)
    ffn, cf, grad_ffn, gvec, vrows = run_light_ffn(tokens, cotangent, wall)
    rs_ffn = lax.psum_scatter(grad_ffn, "dp", scatter_dimension=0, tiled=True)
    lmeta = jnp.concatenate([jnp.stack([lengths[0, 0], me * 512, jnp.int32(8192)]), meta[18:20]])
    lo, dxg, to_left, to_right, rest, gvec, heavy_wo = run_light_attn(
        lmeta, xl, tokens, xr, cotangent, wall, ffn, cf, gvec, vrows
    )
    *partial, rest = run_heavy(meta, xg, hw, heavy_wo, kmask, gvec, vrows, rest)
    rs_rest = lax.psum_scatter(rest, "dp", scatter_dimension=0, tiled=True)

    def along(blocks, x, y):
        moved = [
            lax.ppermute(
                block, "fsdp", [(i, (i // 4 + n * x) % 4 * 4 + (i % 4 + n * y) % 4) for i in range(16)]
            )
            for n, block in enumerate(blocks[1:], 1)
        ]
        return [blocks[0]] + moved

    blocks = call(
        first_sum_kernel,
        [((64, 768), BF)] * 8,
        (meta, *along(partial[0:4], 1, 0), *along(partial[4:8], 0, 1)),
        in_specs=[SMEM] + [VMEM] * 8,
        name="first_sum",
    )
    *blocks, to_left, to_right = lax.optimization_barrier((*blocks, to_left, to_right))
    blocks = along(blocks[0:4], 0, 1) + along(blocks[4:8], 1, 0)
    hr = lax.ppermute(to_left, "fsdp", left)
    hl = lax.ppermute(to_right, "fsdp", right)
    (send_ffn,) = call(spread_ffn_kernel, [((128, S_FFN), BF)], (rs_ffn,), name="spread_ffn")
    got_ffn = swap(send_ffn.reshape(16, 8, S_FFN))
    *blocks, got_ffn, hr, hl = lax.optimization_barrier((*blocks, got_ffn, hr, hl))
    (send,) = call(
        home_kernel,
        [((128, S_ALL), BF)],
        (meta, *blocks, own),
        [((128, 1536), BF)],
        [SMEM] + [VMEM] * 9,
        [HBM],
        sems=(1,),
        name="home",
    )
    send, g_hd = call(
        spread_rest_kernel,
        [((128, S_ALL), BF), ((32, 768), BF)],
        (rs_rest, send),
        [((96, R_ALL), BF), ((128, S_BACK), BF)],
        [HBM, HBM],
        [HBM, VMEM],
        sems=(4, 3),
        name="spread_rest",
        aliases={1: 0},
    )
    g_hd = lax.ppermute(g_hd, ALL, [((d % 8) * 16 + d // 8, d) for d in range(128)])
    got = swap(send.reshape(16, 8, S_ALL))
    six, four, big = ((6, 768), F32), ((6, 1024), F32), ((6, 4096), F32)
    g_gate, g_up, g_down = call(
        sum_ffn_kernel, [four, four, ((8, 768), F32)], (got_ffn,), name="sum_ffn"
    )
    output, grad_tokens, g_q, g_k, g_v, g_o, g_hq, g_hk, g_hv, g_ho, g_hgate, g_hup, *g_vecs = call(
        last_kernel,
        [((512, 768), BF), ((512, 768), BF)] + [six] * 8 + [big, big] + [((1, 6), F32)] * 4,
        (got, st, lo, dxg, hl, hr),
        [((16, 8, S_ALL), BF), ((512, 768), F32), ((512, 768), F32)],
        [HBM, VMEM, HBM, HBM, VMEM, VMEM],
        sems=(4,),
        name="last",
    )
    return (
        output, grad_tokens,
        *[v.reshape(6) for v in g_vecs],
        g_q, g_k, g_v, g_o, g_gate, g_up, g_down,
        g_hq, g_hk, g_hv, g_ho, g_hgate, g_hup, g_hd.astype(F32),
    )


def solution(mesh):
    rows = P(ALL, None)
    flat = P(ALL)
    in_specs = (rows, P("dp", None), P("dp", None), rows) + (flat,) * 4 + (rows,) * 14
    out_specs = (rows, rows) + (flat,) * 4 + (rows,) * 14
    return jax.shard_map(body, mesh=mesh, in_specs=in_specs, out_specs=out_specs, check_vma=False)
```
